128 devices in a mesh: ctx: 16 (over x_hi, y, core), fsdp: 8 (over x_lo, z).
Axes of the slice: x: 4 (x_hi: 2, x_lo: 2; x = x_hi * 2 + x_lo), y: 4, z: 4, core: 2. Of those that a mesh axis runs over, the one named last changes fastest.
Arguments:
- query_rows: bfloat16 [8, 2048, 1024], P('fsdp', 'ctx'), may hold values from -12 to 12
- key_rows: bfloat16 [8, 2048, 1024], P('fsdp', 'ctx'), may hold values from -12 to 12
- value_rows: bfloat16 [8, 2048, 1024], P('fsdp', 'ctx'), may hold values from -6 to 6
- session: int32 [8, 2048], P('fsdp'), may hold values from 0 to 127, never falling along the last dimension, each value on 1 to 64 neighbouring positions
- lengths: int32 [8], P('fsdp'), may hold values from 256 to 2048, as said below
- out_weight: bfloat16 [1024, 2048], P('fsdp'), may hold values from -0.1875 to 0.1875
- upstream: bfloat16 [8, 2048, 2048], P('fsdp', 'ctx'), may hold values from -6 to 6
Outputs:
- attended: bfloat16 [8, 2048, 2048], P('fsdp', 'ctx')
- query_grad: bfloat16 [8, 2048, 1024], P('fsdp', 'ctx')
- key_grad: bfloat16 [8, 2048, 1024], P('fsdp', 'ctx')
- value_grad: bfloat16 [8, 2048, 1024], P('fsdp', 'ctx')
- weight_grad: float32 [1024, 2048], P('fsdp')
The draws below stay inside these ranges and needn't reach their ends.
Inputs may be any that keep to these rules, and one draw needn't show every extreme that they name: `lengths`: some history has all 2048 events valid and some history only one eighth of 2048. session numbers never fall along a history; a session spans 1 to 64 events.
All inputs are finite; a program needn't handle non-finite values.
Results may differ from the reference program's by a relative error of at most 0.022.
Values may be sent and summed in bfloat16 or wider, within the bound.
No kernel may reach another device: no remote copies, remote signals or barrier semaphores. Data moves between devices by JAX's collectives and lax.ppermute only.
A program may use at most 128 MiB of HBM per device.

```python
import math
import jax
import jax.numpy as jnp
import numpy as np
from jax import lax

D = 2048
HEADS = 8
HS = 128
HD = 1024
LEN = 2048
HIST = 8


def rough_rows(key, salt):
    seeded = jax.random.fold_in(key, salt)
    values = jnp.clip(jax.random.normal(jax.random.fold_in(seeded, 1), (HIST, LEN, HEADS * HS), jnp.float32), -4.0, 4.0)
    return values


def draw_query_rows(key, part):
    values = rough_rows(key, 11)
    return values.astype(jnp.bfloat16)


def draw_key_rows(key, part):
    values = rough_rows(key, 23)
    return values.astype(jnp.bfloat16)


def draw_lengths(key, part):
    lowest = LEN // 8
    picks = jax.random.randint(jax.random.fold_in(key, 31), (HIST,), lowest, LEN + 1)
    order = jax.random.permutation(jax.random.fold_in(key, 37), HIST)
    picks = picks.at[order[0]].set(LEN).at[order[1]].set(lowest)
    return picks.astype(jnp.int32)


def block_levels(key, shape, pieces, least, top_value):
    gain, own = 1.0, jax.random.fold_in(key, 6)
    for position, blocks in pieces:
        heights = jnp.exp(jax.random.uniform(jax.random.fold_in(own, position), (blocks,), jnp.float32, least / len(pieces), top_value / len(pieces)))
        gain = gain * jnp.repeat(heights, shape[position] // blocks).reshape([-1 if axis == position else 1 for axis in range(len(shape))])
    return gain


def split_up(amount, total, limit, skew):
    weights = [(1 << 20) // math.isqrt(rank ** skew) + 1 for rank in range(2, amount + 1)]
    surplus, holding = total - limit - (amount - 1), [1] * (amount - 1)
    while surplus > 0:
        candidates = [i for i in range(amount - 1) if holding[i] < limit]
        mass, remaining = sum([weights[i] for i in candidates]), surplus
        for i in candidates:
            addition = min(limit - holding[i], max(1, remaining * weights[i] // mass), surplus)
            holding[i] = holding[i] + addition
            surplus = surplus - addition
    return np.array([limit] + holding)


def ragged_sizes(stream_key, count, total, limit, lean):
    if count == 2:
        one = jax.random.randint(stream_key, (), max(1, total - limit), min(limit, total - 1) + 1)
        return jnp.stack([one, total - one])
    sizes = jnp.asarray(split_up(count, total, limit, lean), jnp.int32)
    twos = (count - 1) // 2
    source_of, taker = sizes[1:1 + 2 * twos:2], sizes[2:2 + 2 * twos:2]
    slack = jnp.minimum(source_of - 1, limit - taker)
    shifted = jax.random.randint(jax.random.fold_in(stream_key, 1), (twos,), 0, 1 << 20) % (slack + 1)
    sizes = sizes.at[1:1 + 2 * twos:2].set(source_of - shifted).at[2:2 + 2 * twos:2].set(taker + shifted)
    return sizes[jax.random.permutation(jax.random.fold_in(stream_key, 2), count)]


def bell_draw(key, extent, deviation, most, split=(), kind=jnp.bfloat16):
    values = jax.random.normal(key, extent, jnp.float32) * deviation
    if len(split) > 0:
        values = block_levels(key, extent, split, -0.22, 0.18) * values
    return jnp.clip(values, min=-most, max=most).astype(kind)


def setup_inputs(seed: int = 0) -> dict:
    streams_of = jax.random.split(jax.random.key(seed), 8)
    return {
        "query_rows": draw_query_rows(jax.random.fold_in(streams_of[7], 71), 0),
        "key_rows": draw_key_rows(jax.random.fold_in(streams_of[7], 71), 0),
        "value_rows": bell_draw(streams_of[2], (HIST, LEN, HD), 1.0, 6.0, ((0, 8), (1, 16))),
        "session": jax.vmap(lambda own: jnp.searchsorted(jnp.cumsum(ragged_sizes(own, LEN // 16, LEN, 64, 2)), jnp.arange(LEN), side="right"))(jax.random.split(streams_of[3], HIST)).reshape((HIST, LEN)).astype(jnp.int32),
        "lengths": draw_lengths(jax.random.fold_in(streams_of[7], 71), 0),
        "out_weight": bell_draw(streams_of[5], (HD, D), HD ** -0.5, 0.1875, ((0, 8),)),
        "upstream": bell_draw(streams_of[6], (HIST, LEN, D), 1.0, 6.0, ((0, 8), (1, 16))),
    }


NEG = -1e+30

def one_history(inputs, out_weight):
    query_rows, key_rows, value_rows, session, length, upstream = inputs
    positions = jnp.arange(LEN, dtype=jnp.int32)
    allowed = (session[None, :] <= session[:, None]) & (positions[None, :] < length)
    allowed = allowed[None]
    valid = (positions < length).astype(jnp.float32)[:, None]
    query_heads = query_rows.astype(jnp.float32).reshape(LEN, HEADS, HS)
    key_heads = key_rows.astype(jnp.float32).reshape(LEN, HEADS, HS)
    value_heads = value_rows.astype(jnp.float32).reshape(LEN, HEADS, HS)
    score_scale = 1.0 / math.sqrt(HS)
    scores = jnp.einsum('qhd,khd->hqk', query_heads, key_heads) * score_scale
    masked = jnp.where(allowed, scores, NEG)
    largest = lax.optimization_barrier(jnp.max(masked, axis=2, keepdims=True))
    total = lax.optimization_barrier(jnp.sum(jnp.where(allowed, jnp.exp(masked - largest), 0.0), axis=2, keepdims=True))
    log_total = largest + jnp.log(total)
    probability = jnp.where(allowed, jnp.exp(masked - log_total), 0.0)
    probability_low = probability.astype(jnp.bfloat16)
    probability_back = lax.optimization_barrier(probability_low).astype(jnp.float32)
    context = jnp.einsum('hqk,khd->qhd', probability_back, value_heads).reshape(LEN, HEADS * HS) * valid
    context_low = context.astype(jnp.bfloat16)
    attended = jnp.dot(context_low, out_weight, preferred_element_type=jnp.float32).astype(jnp.bfloat16)
    back_proj = lax.dot_general(upstream, out_weight, (((1,), (1,)), ((), ())), preferred_element_type=jnp.float32)
    context_grad = (back_proj * valid).astype(jnp.bfloat16)
    grad_heads = lax.optimization_barrier(context_grad).astype(jnp.float32).reshape(LEN, HEADS, HS)
    context_heads = lax.optimization_barrier(context_low).astype(jnp.float32).reshape(LEN, HEADS, HS)
    delta = lax.optimization_barrier(jnp.sum(grad_heads * context_heads, axis=2))
    dprob = jnp.einsum('qhd,khd->hqk', grad_heads, value_heads)
    dscore = (probability * (dprob - delta.T[:, :, None]) * score_scale).astype(jnp.bfloat16)
    dscore_back = lax.optimization_barrier(dscore).astype(jnp.float32)
    query_grad = jnp.einsum('hqk,khd->qhd', dscore_back, key_heads).reshape(LEN, HEADS * HS).astype(jnp.bfloat16)
    key_grad = jnp.einsum('hqk,qhd->khd', dscore_back, query_heads).reshape(LEN, HEADS * HS).astype(jnp.bfloat16)
    value_grad = jnp.einsum('hqk,qhd->khd', probability_back, grad_heads).reshape(LEN, HEADS * HS).astype(jnp.bfloat16)
    weight_term = lax.dot_general(context_low, upstream, (((0,), (0,)), ((), ())), preferred_element_type=jnp.float32)
    return (attended, query_grad, key_grad, value_grad, weight_term)

def reference(query_rows, key_rows, value_rows, session, lengths, out_weight, upstream):

    def each_history(inputs):
        return one_history(inputs, out_weight)
    attended, query_grad, key_grad, value_grad, weight_terms = lax.map(each_history, (query_rows, key_rows, value_rows, session, lengths, upstream))
    return (attended, query_grad, key_grad, value_grad, lax.optimization_barrier(jnp.sum(weight_terms, axis=0)))
```

```python
import functools
import math

import jax
import jax.numpy as jnp
from jax import lax
from jax.experimental import pallas as pl
from jax.experimental.pallas import tpu as pltpu
from jax.sharding import PartitionSpec as P

HEADS = 8
HS = 128
BLOCK = 128
TILE = 256
SPAN = 512
REACH = 128
CHIPS = 8
LEN = 2048
NEG = -1e30
SCALE = 1.0 / math.sqrt(HS)
SCALE2 = SCALE * math.log2(math.e)
F32 = jnp.float32
BF16 = jnp.bfloat16

CORE_SWAP = [(i, i ^ 1) for i in range(16)]
PAIR_SWAP = [(i, i ^ 8) for i in range(16)]
SAME_CORE = [[2 * j + c for j in range(CHIPS)] for c in range(2)]
REDUCE = [
    [(8 * h + 2 * y + c) * 8 + f for f in range(8) for y in range(4)]
    for h in range(2)
    for c in range(2)
]


def dot_nt(a, b):
    return lax.dot_general(a, b, (((1,), (1,)), ((), ())), preferred_element_type=F32)


def dot_tn(a, b):
    return lax.dot_general(a, b, (((0,), (0,)), ((), ())), preferred_element_type=F32)


def dot_nn(a, b):
    return lax.dot_general(a, b, (((1,), (0,)), ((), ())), preferred_element_type=F32)


def params():
    return pltpu.CompilerParams(vmem_limit_bytes=56 * 1024 * 1024)


def call(kernel, out_shape, smem=0, scratch=(), flops=0, inputs=()):
    specs = [
        pl.BlockSpec(memory_space=pltpu.SMEM if i < smem else pltpu.VMEM)
        for i in range(len(inputs))
    ]
    outs = jax.tree.map(lambda _: pl.BlockSpec(memory_space=pltpu.VMEM), out_shape)
    return pl.pallas_call(
        kernel,
        out_shape=out_shape,
        in_specs=specs,
        out_specs=outs,
        scratch_shapes=list(scratch),
        compiler_params=params(),
        cost_estimate=pl.CostEstimate(flops=flops, bytes_accessed=2_000_000, transcendentals=0),
    )(*inputs)


def pack_kernel(q_ref, k_ref, v_ref, out_ref):
    for a in range(HEADS):
        cols = slice(a * HS, (a + 1) * HS)
        out_ref[a, 0] = q_ref[0, :, cols]
        out_ref[a, 1] = k_ref[0, :, cols]
        out_ref[a, 2] = v_ref[0, :, cols]


def in_order(core, own_ref, other_ref, slot, dst_ref):
    for j in range(CHIPS):
        own = pl.multiple_of(2 * BLOCK * j + BLOCK * core, BLOCK)
        other = pl.multiple_of(2 * BLOCK * j + BLOCK * (1 - core), BLOCK)
        dst_ref[pl.ds(own, BLOCK)] = own_ref[j, slot]
        dst_ref[pl.ds(other, BLOCK)] = other_ref[j, slot]


def chunks_of(m):
    stop = min(SPAN * (m + 1) + REACH, LEN)
    return [(start, min(start + SPAN, stop)) for start in range(0, stop, SPAN)]


def masked_scores(k_s, q, end, m, start, stop):
    scores = dot_nt(k_s[start:stop], q)
    if stop > SPAN * m:
        at = lax.broadcasted_iota(jnp.int32, scores.shape, 0) + start
        scores = jnp.where(at < end, scores, NEG)
    return scores


def forward_kernel(core_ref, own_ref, other_ref, end_ref, valid_ref, ctx_ref, lse_ref, k_s, v_s, s_s):
    core = core_ref[0]
    in_order(core, own_ref, other_ref, 1, k_s)
    in_order(core, own_ref, other_ref, 2, v_s)
    for m in range(4):
        q = own_ref[2 * m : 2 * m + 2, 0].reshape(TILE, HS)
        end = end_ref[m]
        top = jnp.full((1, TILE), NEG, F32)
        for start, stop in chunks_of(m):
            scores = masked_scores(k_s, q, end, m, start, stop)
            s_s[start:stop] = scores
            top = jnp.maximum(top, jnp.max(scores, axis=0, keepdims=True))
        top2 = top * SCALE2
        total = jnp.zeros((1, TILE), F32)
        acc = jnp.zeros((HS, TILE), F32)
        for start, stop in chunks_of(m):
            p = jnp.exp2(s_s[start:stop] * SCALE2 - top2)
            total = total + jnp.sum(p, axis=0, keepdims=True)
            acc = acc + dot_tn(v_s[start:stop], p.astype(BF16))
        lse_ref[m] = top2 + jnp.log2(total)
        ctx = (acc * (valid_ref[m] / total)).T.astype(BF16)
        for t in range(2):
            j = 2 * m + t
            block = ctx[t * BLOCK : (t + 1) * BLOCK]
            ctx_ref[j, 0] = block
            ctx_ref[j ^ 4, 1] = block


def backward_kernel(
    core_ref, own_ref, other_ref, end_ref, lse_ref, ctx_ref, grad_ref,
    dq_ref, keep_ref, send_ref, k_s, v_s, dk_s, dv_s,
):
    core = core_ref[0]
    in_order(core, own_ref, other_ref, 1, k_s)
    in_order(core, own_ref, other_ref, 2, v_s)
    dk_s[...] = jnp.zeros(dk_s.shape, F32)
    dv_s[...] = jnp.zeros(dv_s.shape, F32)
    for m in range(4):
        rows = slice(2 * m, 2 * m + 2)
        q = own_ref[rows, 0].reshape(TILE, HS)
        do = grad_ref[rows].reshape(TILE, HS)
        ctx = ctx_ref[rows, 0].reshape(TILE, HS)
        delta = jnp.sum((do.astype(F32) * ctx.astype(F32)).T, axis=0, keepdims=True)
        end = end_ref[m]
        lse = lse_ref[m]
        dq = jnp.zeros((HS, TILE), F32)
        for start, stop in chunks_of(m):
            scores = masked_scores(k_s, q, end, m, start, stop)
            p = jnp.exp2(scores * SCALE2 - lse)
            dp = dot_nt(v_s[start:stop], do)
            ds = (p * (dp - delta) * SCALE).astype(BF16)
            dv_s[start:stop] += dot_nn(p.astype(BF16), do)
            dk_s[start:stop] += dot_nn(ds, q)
            dq = dq + dot_tn(k_s[start:stop], ds)
        dq_rows = dq.T.astype(BF16)
        dq_ref[2 * m] = dq_rows[:BLOCK]
        dq_ref[2 * m + 1] = dq_rows[BLOCK:]
    for j in range(CHIPS):
        own = pl.multiple_of(2 * BLOCK * j + BLOCK * core, BLOCK)
        other = pl.multiple_of(2 * BLOCK * j + BLOCK * (1 - core), BLOCK)
        keep_ref[j, 0] = dk_s[pl.ds(own, BLOCK)]
        keep_ref[j, 1] = dv_s[pl.ds(own, BLOCK)]
        send_ref[j, 0] = dk_s[pl.ds(other, BLOCK)].astype(BF16)
        send_ref[j, 1] = dv_s[pl.ds(other, BLOCK)].astype(BF16)


def project_kernel(core_ref, up_ref, mine_ref, other_ref, valid_ref, out_ref):
    half = mine_ref.shape[1]
    core = core_ref[0]
    up_mine = up_ref[0, :, pl.ds(pl.multiple_of(core * half, half), half)]
    up_other = up_ref[0, :, pl.ds(pl.multiple_of((1 - core) * half, half), half)]
    for a in range(HEADS):
        rows = slice(a * HS, (a + 1) * HS)
        total = dot_nt(up_mine, mine_ref[rows]) + dot_nt(up_other, other_ref[rows])
        out_ref[a] = (total * valid_ref[...]).astype(BF16)


def attend_kernel(core_ref, ctx_ref, mine_ref, other_ref, out_ref):
    half = mine_ref.shape[1]
    core = core_ref[0]
    ctx = jnp.concatenate([ctx_ref[a, 0] for a in range(HEADS)], axis=1)
    for n in range(4):
        cols = slice(n * half // 4, (n + 1) * half // 4)
        at = pl.multiple_of(core * half + n * half // 4, half // 4)
        out_ref[0, :, pl.ds(at, half // 4)] = dot_nn(ctx, mine_ref[:, cols]).astype(BF16)
        at = pl.multiple_of((1 - core) * half + n * half // 4, half // 4)
        out_ref[0, :, pl.ds(at, half // 4)] = dot_nn(ctx, other_ref[:, cols]).astype(BF16)


def weight_kernel(ctx_ref, ctx_other_ref, up_ref, up_other_ref, out_ref):
    quarter = up_ref.shape[2]
    up = up_ref[...].reshape(TILE, quarter)
    up_other = up_other_ref[...].reshape(TILE, quarter)
    for a in range(HEADS):
        total = dot_tn(ctx_ref[a].reshape(TILE, HS), up)
        total = total + dot_tn(ctx_other_ref[a].reshape(TILE, HS), up_other)
        out_ref[4 * a : 4 * a + 4] = total.reshape(4, HS // 4, quarter).astype(BF16)


def join_kernel(dq_ref, keep_ref, came_ref, terms_ref, out_ref):
    total = terms_ref[0].astype(F32)
    for s in range(1, terms_ref.shape[0]):
        total = total + terms_ref[s].astype(F32)
    weight = total.astype(BF16)
    rows = weight.shape[0]
    for j in range(CHIPS):
        out_ref[j, 0] = dq_ref[j]
        out_ref[j, 1] = (keep_ref[j, 0] + came_ref[j, 0].astype(F32)).astype(BF16)
        out_ref[j, 2] = (keep_ref[j, 1] + came_ref[j, 1].astype(F32)).astype(BF16)
        for t in range(4):
            out_ref[j, 3, t * rows : (t + 1) * rows] = weight[:, t * HS : (t + 1) * HS]


def unpack_kernel(core_ref, mine_ref, other_ref, dq_ref, dk_ref, dv_ref, dw_ref):
    core = core_ref[0]
    for a in range(HEADS):
        cols = slice(a * HS, (a + 1) * HS)
        dq_ref[0, :, cols] = mine_ref[a, 0]
        dk_ref[0, :, cols] = mine_ref[a, 1]
        dv_ref[0, :, cols] = mine_ref[a, 2]
        x, y = a // 4, a % 4
        for t in range(4):
            rows = slice(32 * y, 32 * y + 32)
            part = slice(32 * t, 32 * t + 32)
            at = pl.multiple_of(1024 * x + 512 * core + HS * t, HS)
            dw_ref[rows, pl.ds(at, HS)] = mine_ref[a, 3, part].astype(F32)
            at = pl.multiple_of(1024 * x + 512 * (1 - core) + HS * t, HS)
            dw_ref[rows, pl.ds(at, HS)] = other_ref[a, part].astype(F32)


def shape(dims, dtype):
    return jax.ShapeDtypeStruct(dims, dtype)


def exchange(operand):
    return lax.all_to_all(
        operand, "ctx", split_axis=0, concat_axis=0, tiled=True, axis_index_groups=SAME_CORE
    )


def shards(query_rows, key_rows, value_rows, session, lengths, out_weight, upstream):
    index = lax.axis_index("ctx")
    core = index % 2
    high = index // 8
    core_ref = core.reshape(1).astype(jnp.int32)
    valid_len = lengths[0]
    half = out_weight.shape[1] // 2
    quarter = half // 2

    own_half = lax.dynamic_slice_in_dim(out_weight, core * half, half, 1)
    weight_mine = lax.all_gather(own_half, "fsdp", axis=0, tiled=True)
    weight_other = lax.ppermute(weight_mine, "ctx", CORE_SWAP)

    up = upstream[0]
    up_pair = lax.ppermute(
        lax.dynamic_slice_in_dim(up, (1 - high) * half, half, 1), "ctx", PAIR_SWAP
    )
    up_both = jnp.stack([lax.dynamic_slice_in_dim(up, high * half, half, 1), up_pair])
    up_mine = lax.dynamic_slice_in_dim(up_both, core * quarter, quarter, 2)
    up_other = lax.ppermute(
        lax.dynamic_slice_in_dim(up_both, (1 - core) * quarter, quarter, 2), "ctx", CORE_SWAP
    )

    session_ids = session[0]
    positions = jnp.arange(LEN, dtype=jnp.int32).reshape(CHIPS, 2, BLOCK)
    own_sessions = lax.dynamic_index_in_dim(session_ids.reshape(CHIPS, 2, BLOCK), core, 1, False)
    own_positions = lax.dynamic_index_in_dim(positions, core, 1, False)
    end = jnp.sum(
        (session_ids[:, None] <= own_sessions.reshape(1, -1)).astype(jnp.int32), axis=0
    )
    end = jnp.minimum(end, valid_len).reshape(4, 1, TILE)
    valid = (own_positions < valid_len).astype(F32).reshape(4, 1, TILE)
    rows_here = index * BLOCK + jnp.arange(BLOCK, dtype=jnp.int32)
    valid_here = (rows_here < valid_len).astype(F32)[:, None]

    packed = call(
        pack_kernel,
        shape((HEADS, 3, BLOCK, HS), BF16),
        inputs=(query_rows, key_rows, value_rows),
    )
    own = exchange(packed)
    other = lax.ppermute(own, "ctx", CORE_SWAP)
    pairs = 4 * TILE * SPAN * 5 // 2
    context, lse = call(
        forward_kernel,
        (shape((CHIPS, 2, BLOCK, HS), BF16), shape((4, 1, TILE), F32)),
        smem=1,
        scratch=(
            pltpu.VMEM((LEN, HS), BF16),
            pltpu.VMEM((LEN, HS), BF16),
            pltpu.VMEM((LEN, TILE), F32),
        ),
        flops=4 * pairs * HS,
        inputs=(core_ref, own, other, end, valid),
    )
    context_mine = exchange(context)
    context_other = lax.ppermute(context_mine, "ctx", CORE_SWAP)
    terms = call(
        weight_kernel,
        shape((32, 32, quarter), BF16),
        flops=2 * 512 * 1024 * 512,
        inputs=(context_mine, context_other, up_mine, up_other),
    )
    terms = lax.all_to_all(
        terms, ("ctx", "fsdp"), split_axis=0, concat_axis=0, tiled=True, axis_index_groups=REDUCE
    )

    grads = call(
        project_kernel,
        shape((HEADS, BLOCK, HS), BF16),
        smem=1,
        flops=2 * 128 * 1024 * 2048,
        inputs=(core_ref, upstream, weight_mine, weight_other, valid_here),
    )
    grads = exchange(grads)
    dq, keep, send = call(
        backward_kernel,
        (
            shape((CHIPS, BLOCK, HS), BF16),
            shape((CHIPS, 2, BLOCK, HS), F32),
            shape((CHIPS, 2, BLOCK, HS), BF16),
        ),
        smem=1,
        scratch=(
            pltpu.VMEM((LEN, HS), BF16),
            pltpu.VMEM((LEN, HS), BF16),
            pltpu.VMEM((LEN, HS), F32),
            pltpu.VMEM((LEN, HS), F32),
        ),
        flops=10 * pairs * HS,
        inputs=(core_ref, own, other, end, lse, context, grads),
    )
    came = lax.ppermute(send, "ctx", CORE_SWAP)
    attended = call(
        attend_kernel,
        shape((1, BLOCK, 2 * half), BF16),
        smem=1,
        flops=2 * 128 * 1024 * 2048,
        inputs=(core_ref, context_mine, weight_mine, weight_other),
    )
    joined = call(
        join_kernel,
        shape((CHIPS, 4, BLOCK, HS), BF16),
        inputs=(dq, keep, came, terms),
    )
    result = exchange(joined)
    weight_part = lax.ppermute(result[:, 3], "ctx", CORE_SWAP)
    query_grad, key_grad, value_grad, weight_grad = call(
        unpack_kernel,
        (
            shape((1, BLOCK, HEADS * HS), BF16),
            shape((1, BLOCK, HEADS * HS), BF16),
            shape((1, BLOCK, HEADS * HS), BF16),
            shape((HS, 2 * half), F32),
        ),
        smem=1,
        inputs=(core_ref, result, weight_part),
    )
    return (attended, query_grad, key_grad, value_grad, weight_grad)


def solution(mesh):
    rows = P("fsdp", "ctx", None)
    return jax.shard_map(
        shards,
        mesh=mesh,
        in_specs=(rows, rows, rows, P("fsdp", None), P("fsdp"), P("fsdp", None), rows),
        out_specs=(rows, rows, rows, rows, P("fsdp", None)),
        check_vma=False,
    )
```

```python
import functools
import math

import jax
import jax.numpy as jnp
from jax import lax
from jax.experimental import pallas as pl
from jax.experimental.pallas import tpu as pltpu
from jax.sharding import PartitionSpec as P

HEADS = 8
HS = 128
BLOCK = 128
TILE = 256
SPAN = 512
REACH = 128
CHIPS = 8
LEN = 2048
NEG = -1e30
SCALE = 1.0 / math.sqrt(HS)
SCALE2 = SCALE * math.log2(math.e)
F32 = jnp.float32
BF16 = jnp.bfloat16

CORE_SWAP = [(i, i ^ 1) for i in range(16)]
PAIR_SWAP = [(i, i ^ 8) for i in range(16)]
DIAG_SWAP = [(i, i ^ 9) for i in range(16)]
SAME_CORE = [[2 * j + c for j in range(CHIPS)] for c in range(2)]
REDUCE = [
    [(8 * h + 2 * y + c) * 8 + f for f in range(8) for y in range(4)]
    for h in range(2)
    for c in range(2)
]


def dot_nt(a, b):
    return lax.dot_general(a, b, (((1,), (1,)), ((), ())), preferred_element_type=F32)


def dot_tn(a, b):
    return lax.dot_general(a, b, (((0,), (0,)), ((), ())), preferred_element_type=F32)


def dot_nn(a, b):
    return lax.dot_general(a, b, (((1,), (0,)), ((), ())), preferred_element_type=F32)


def params():
    return pltpu.CompilerParams(vmem_limit_bytes=14 * 1024 * 1024)


def call(kernel, out_shape, smem=0, scratch=(), flops=0, inputs=()):
    specs = [
        pl.BlockSpec(memory_space=pltpu.SMEM if i < smem else pltpu.VMEM)
        for i in range(len(inputs))
    ]
    outs = jax.tree.map(lambda _: pl.BlockSpec(memory_space=pltpu.VMEM), out_shape)
    return pl.pallas_call(
        kernel,
        out_shape=out_shape,
        in_specs=specs,
        out_specs=outs,
        scratch_shapes=list(scratch),
        compiler_params=params(),
        cost_estimate=pl.CostEstimate(flops=flops, bytes_accessed=2_000_000, transcendentals=0),
    )(*inputs)


def pack_kernel(
    core_ref, high_ref, q_ref, k_ref, v_ref, w_ref, up_ref,
    out_ref, half_ref, keep_ref, core_out_ref, pair_ref, diag_ref,
):
    core, high = core_ref[0], high_ref[0]
    for a in range(HEADS):
        cols = slice(a * HS, (a + 1) * HS)
        out_ref[a, 0] = q_ref[0, :, cols]
        out_ref[a, 1] = k_ref[0, :, cols]
        out_ref[a, 2] = v_ref[0, :, cols]
    half = half_ref.shape[1]
    quarter = half // 2
    half_ref[...] = w_ref[:, pl.ds(pl.multiple_of(core * half, half), half)]
    for ref, x, c in (
        (keep_ref, high, core),
        (core_out_ref, high, 1 - core),
        (pair_ref, 1 - high, core),
        (diag_ref, 1 - high, 1 - core),
    ):
        at = pl.multiple_of(x * half + c * quarter, quarter)
        ref[...] = up_ref[0, :, pl.ds(at, quarter)]


def in_order(core, own_ref, other_ref, slot, dst_ref):
    for j in range(CHIPS):
        own = pl.multiple_of(2 * BLOCK * j + BLOCK * core, BLOCK)
        other = pl.multiple_of(2 * BLOCK * j + BLOCK * (1 - core), BLOCK)
        dst_ref[pl.ds(own, BLOCK)] = own_ref[j, slot]
        dst_ref[pl.ds(other, BLOCK)] = other_ref[j, slot]


def chunks_of(m):
    stop = min(SPAN * (m + 1) + REACH, LEN)
    return [(start, min(start + SPAN, stop)) for start in range(0, stop, SPAN)]


def masked_scores(k_s, q, end, m, start, stop):
    scores = dot_nt(k_s[start:stop], q)
    if stop > SPAN * m:
        at = lax.broadcasted_iota(jnp.int32, scores.shape, 0) + start
        scores = jnp.where(at < end, scores, NEG)
    return scores


def forward_kernel(core_ref, own_ref, other_ref, end_ref, valid_ref, ctx_ref, lse_ref, k_s, v_s, s_s):
    core = core_ref[0]
    in_order(core, own_ref, other_ref, 1, k_s)
    in_order(core, own_ref, other_ref, 2, v_s)
    for m in range(4):
        q = own_ref[2 * m : 2 * m + 2, 0].reshape(TILE, HS)
        end = end_ref[m]
        top = jnp.full((1, TILE), NEG, F32)
        for start, stop in chunks_of(m):
            scores = masked_scores(k_s, q, end, m, start, stop)
            s_s[start:stop] = scores
            top = jnp.maximum(top, jnp.max(scores, axis=0, keepdims=True))
        top2 = top * SCALE2
        total = jnp.zeros((1, TILE), F32)
        acc = jnp.zeros((HS, TILE), F32)
        for start, stop in chunks_of(m):
            p = jnp.exp2(s_s[start:stop] * SCALE2 - top2)
            total = total + jnp.sum(p, axis=0, keepdims=True)
            acc = acc + dot_tn(v_s[start:stop], p.astype(BF16))
        lse_ref[m] = top2 + jnp.log2(total)
        ctx = (acc * (valid_ref[m] / total)).T.astype(BF16)
        for t in range(2):
            j = 2 * m + t
            block = ctx[t * BLOCK : (t + 1) * BLOCK]
            ctx_ref[j, 0] = block
            ctx_ref[j ^ 4, 1] = block


def backward_kernel(
    core_ref, own_ref, other_ref, end_ref, lse_ref, ctx_ref, grad_ref,
    dq_ref, keep_ref, send_ref, k_s, v_s, dk_s, dv_s,
):
    core = core_ref[0]
    in_order(core, own_ref, other_ref, 1, k_s)
    in_order(core, own_ref, other_ref, 2, v_s)
    dk_s[...] = jnp.zeros(dk_s.shape, F32)
    dv_s[...] = jnp.zeros(dv_s.shape, F32)
    for m in range(4):
        rows = slice(2 * m, 2 * m + 2)
        q = own_ref[rows, 0].reshape(TILE, HS)
        do = grad_ref[rows].reshape(TILE, HS)
        ctx = ctx_ref[rows, 0].reshape(TILE, HS)
        delta = jnp.sum((do.astype(F32) * ctx.astype(F32)).T, axis=0, keepdims=True)
        end = end_ref[m]
        lse = lse_ref[m]
        dq = jnp.zeros((HS, TILE), F32)
        for start, stop in chunks_of(m):
            scores = masked_scores(k_s, q, end, m, start, stop)
            p = jnp.exp2(scores * SCALE2 - lse)
            dp = dot_nt(v_s[start:stop], do)
            ds = (p * (dp - delta) * SCALE).astype(BF16)
            dv_s[start:stop] += dot_nn(p.astype(BF16), do)
            dk_s[start:stop] += dot_nn(ds, q)
            dq = dq + dot_tn(k_s[start:stop], ds)
        dq_rows = dq.T.astype(BF16)
        dq_ref[2 * m] = dq_rows[:BLOCK]
        dq_ref[2 * m + 1] = dq_rows[BLOCK:]
    for j in range(CHIPS):
        own = pl.multiple_of(2 * BLOCK * j + BLOCK * core, BLOCK)
        other = pl.multiple_of(2 * BLOCK * j + BLOCK * (1 - core), BLOCK)
        keep_ref[j, 0] = dk_s[pl.ds(own, BLOCK)]
        keep_ref[j, 1] = dv_s[pl.ds(own, BLOCK)]
        send_ref[j, 0] = dk_s[pl.ds(other, BLOCK)].astype(BF16)
        send_ref[j, 1] = dv_s[pl.ds(other, BLOCK)].astype(BF16)


def project_kernel(core_ref, row_ref, up_ref, own_ref, valid_ref, *refs):
    mine, other, out_ref = refs[:7], refs[7:14], refs[14]
    half = mine[0].shape[1]
    core, row = core_ref[0], row_ref[0]
    valid = valid_ref[...]
    out_ref[row] = (dot_nt(up_ref[0], own_ref[...]) * valid).astype(BF16)
    up_mine = up_ref[0, :, pl.ds(pl.multiple_of(core * half, half), half)]
    up_other = up_ref[0, :, pl.ds(pl.multiple_of((1 - core) * half, half), half)]
    for s in range(1, HEADS):
        total = dot_nt(up_mine, mine[s - 1][...]) + dot_nt(up_other, other[s - 1][...])
        out_ref[jnp.bitwise_xor(row, s)] = (total * valid).astype(BF16)


def attend_kernel(core_ref, row_ref, ctx_ref, own_ref, *refs):
    mine, other, out_ref = refs[:7], refs[7:14], refs[14]
    half = mine[0].shape[1]
    core, row = core_ref[0], row_ref[0]
    ctx = jnp.concatenate([ctx_ref[jnp.bitwise_xor(row, s), 0] for s in range(HEADS)], axis=1)
    step = half // 4
    for side, parts in ((core, mine), (1 - core, other)):
        for n in range(4):
            at = pl.multiple_of(side * half + n * step, step)
            cols = slice(n * step, (n + 1) * step)
            weight = jnp.concatenate(
                [own_ref[:, pl.ds(at, step)]] + [part[:, cols] for part in parts], axis=0
            )
            out_ref[0, :, pl.ds(at, step)] = dot_nn(ctx, weight).astype(BF16)


def weight_kernel(ctx_ref, ctx_other_ref, keep_ref, pair_ref, core_ref, diag_ref, out_ref):
    quarter = keep_ref.shape[1]
    up = jnp.concatenate([keep_ref[...], pair_ref[...]], axis=0)
    up_other = jnp.concatenate([core_ref[...], diag_ref[...]], axis=0)
    for a in range(HEADS):
        total = dot_tn(ctx_ref[a].reshape(TILE, HS), up)
        total = total + dot_tn(ctx_other_ref[a].reshape(TILE, HS), up_other)
        out_ref[4 * a : 4 * a + 4] = total.reshape(4, HS // 4, quarter).astype(BF16)


def join_kernel(dq_ref, keep_ref, came_ref, terms_ref, out_ref):
    total = terms_ref[0].astype(F32)
    for s in range(1, terms_ref.shape[0]):
        total = total + terms_ref[s].astype(F32)
    weight = total.astype(BF16)
    rows = weight.shape[0]
    for j in range(CHIPS):
        out_ref[j, 0] = dq_ref[j]
        out_ref[j, 1] = (keep_ref[j, 0] + came_ref[j, 0].astype(F32)).astype(BF16)
        out_ref[j, 2] = (keep_ref[j, 1] + came_ref[j, 1].astype(F32)).astype(BF16)
        for t in range(4):
            out_ref[j, 3, t * rows : (t + 1) * rows] = weight[:, t * HS : (t + 1) * HS]


def unpack_kernel(core_ref, mine_ref, other_ref, dq_ref, dk_ref, dv_ref, dw_ref):
    core = core_ref[0]
    for a in range(HEADS):
        cols = slice(a * HS, (a + 1) * HS)
        dq_ref[0, :, cols] = mine_ref[a, 0]
        dk_ref[0, :, cols] = mine_ref[a, 1]
        dv_ref[0, :, cols] = mine_ref[a, 2]
        x, y = a // 4, a % 4
        for t in range(4):
            rows = slice(32 * y, 32 * y + 32)
            part = slice(32 * t, 32 * t + 32)
            at = pl.multiple_of(1024 * x + 512 * core + HS * t, HS)
            dw_ref[rows, pl.ds(at, HS)] = mine_ref[a, 3, part].astype(F32)
            at = pl.multiple_of(1024 * x + 512 * (1 - core) + HS * t, HS)
            dw_ref[rows, pl.ds(at, HS)] = other_ref[a, part].astype(F32)


def shape(dims, dtype):
    return jax.ShapeDtypeStruct(dims, dtype)


def exchange(operand):
    return lax.all_to_all(
        operand, "ctx", split_axis=0, concat_axis=0, tiled=True, axis_index_groups=SAME_CORE
    )


def after(value, *others):
    return lax.optimization_barrier((value, *others))[0]


def shards(query_rows, key_rows, value_rows, session, lengths, out_weight, upstream):
    index = lax.axis_index("ctx").astype(jnp.int32)
    core = index & 1
    core_ref = core.reshape(1)
    high_ref = (index >> 3).reshape(1)
    row_ref = lax.axis_index("fsdp").astype(jnp.int32).reshape(1)
    valid_len = lengths[0]
    width = out_weight.shape[1]
    half = width // 2
    quarter = half // 2

    part = shape((BLOCK, quarter), BF16)
    packed, own_half, up_keep, up_core, up_pair, up_diag = call(
        pack_kernel,
        (shape((HEADS, 3, BLOCK, HS), BF16), shape((HS, half), BF16), part, part, part, part),
        smem=2,
        inputs=(core_ref, high_ref, query_rows, key_rows, value_rows, out_weight, upstream),
    )
    own = exchange(packed)

    mine, other_half = [], []
    for s in range(1, HEADS):
        piece = lax.ppermute(own_half, "fsdp", [(i, i ^ s) for i in range(8)])
        mine.append(piece)
        other_half.append(lax.ppermute(piece, "ctx", CORE_SWAP))
    up_core = lax.ppermute(up_core, "ctx", CORE_SWAP)
    up_pair = lax.ppermute(up_pair, "ctx", PAIR_SWAP)
    up_diag = lax.ppermute(up_diag, "ctx", DIAG_SWAP)

    session_ids = session[0]
    positions = jnp.arange(LEN, dtype=jnp.int32).reshape(CHIPS, 2, BLOCK)
    own_sessions = lax.dynamic_index_in_dim(session_ids.reshape(CHIPS, 2, BLOCK), core, 1, False)
    own_positions = lax.dynamic_index_in_dim(positions, core, 1, False)
    end = jnp.sum(
        (session_ids[:, None] <= own_sessions.reshape(1, -1)).astype(jnp.int32), axis=0
    )
    end = jnp.minimum(end, valid_len).reshape(4, 1, TILE)
    valid = (own_positions < valid_len).astype(F32).reshape(4, 1, TILE)
    rows_here = index * BLOCK + jnp.arange(BLOCK, dtype=jnp.int32)
    valid_here = (rows_here < valid_len).astype(F32)[:, None]

    own = after(own, end, valid, valid_here, up_core, up_pair, up_diag, *mine[:3])
    other = lax.ppermute(own, "ctx", CORE_SWAP)
    pairs = 4 * TILE * SPAN * 5 // 2
    context, lse = call(
        forward_kernel,
        (shape((CHIPS, 2, BLOCK, HS), BF16), shape((4, 1, TILE), F32)),
        smem=1,
        scratch=(
            pltpu.VMEM((LEN, HS), BF16),
            pltpu.VMEM((LEN, HS), BF16),
            pltpu.VMEM((LEN, TILE), F32),
        ),
        flops=4 * pairs * HS,
        inputs=(core_ref, own, other, end, valid),
    )
    context_mine = exchange(context)
    grads = call(
        project_kernel,
        shape((HEADS, BLOCK, HS), BF16),
        smem=2,
        flops=2 * 128 * 1024 * 2048,
        inputs=(core_ref, row_ref, upstream, out_weight, valid_here, *mine, *other_half),
    )
    grads = exchange(after(grads, context_mine))
    context_other = lax.ppermute(context_mine, "ctx", CORE_SWAP)
    terms = call(
        weight_kernel,
        shape((32, 32, quarter), BF16),
        flops=2 * 512 * 1024 * 512,
        inputs=(context_mine, context_other, up_keep, up_pair, up_core, up_diag),
    )
    terms = lax.all_to_all(
        after(terms, grads),
        ("ctx", "fsdp"),
        split_axis=0,
        concat_axis=0,
        tiled=True,
        axis_index_groups=REDUCE,
    )
    dq, keep, send = call(
        backward_kernel,
        (
            shape((CHIPS, BLOCK, HS), BF16),
            shape((CHIPS, 2, BLOCK, HS), F32),
            shape((CHIPS, 2, BLOCK, HS), BF16),
        ),
        smem=1,
        scratch=(
            pltpu.VMEM((LEN, HS), BF16),
            pltpu.VMEM((LEN, HS), BF16),
            pltpu.VMEM((LEN, HS), F32),
            pltpu.VMEM((LEN, HS), F32),
        ),
        flops=10 * pairs * HS,
        inputs=(core_ref, own, other, end, lse, context, grads),
    )
    came = lax.ppermute(send, "ctx", CORE_SWAP)
    attended = call(
        attend_kernel,
        shape((1, BLOCK, width), BF16),
        smem=2,
        flops=2 * 128 * 1024 * 2048,
        inputs=(core_ref, row_ref, context_mine, out_weight, *mine, *other_half),
    )
    joined = call(
        join_kernel,
        shape((CHIPS, 4, BLOCK, HS), BF16),
        inputs=(after(dq, attended), keep, came, terms),
    )
    result = exchange(joined)
    weight_part = lax.ppermute(result[:, 3], "ctx", CORE_SWAP)
    query_grad, key_grad, value_grad, weight_grad = call(
        unpack_kernel,
        (
            shape((1, BLOCK, HEADS * HS), BF16),
            shape((1, BLOCK, HEADS * HS), BF16),
            shape((1, BLOCK, HEADS * HS), BF16),
            shape((HS, width), F32),
        ),
        smem=1,
        inputs=(core_ref, result, weight_part),
    )
    return (attended, query_grad, key_grad, value_grad, weight_grad)


def solution(mesh):
    rows = P("fsdp", "ctx", None)
    return jax.shard_map(
        shards,
        mesh=mesh,
        in_specs=(rows, rows, rows, P("fsdp", None), P("fsdp"), P("fsdp", None), rows),
        out_specs=(rows, rows, rows, rows, P("fsdp", None)),
        check_vma=False,
    )
```

```python
import functools
import math

import jax
import jax.numpy as jnp
from jax import lax
from jax.experimental import pallas as pl
from jax.experimental.pallas import tpu as pltpu
from jax.sharding import PartitionSpec as P

HEADS = 8
HS = 128
BLOCK = 128
TILE = 256
SPAN = 512
REACH = 128
CHIPS = 8
LEN = 2048
NEG = -1e30
SEMS = 48
SCALE = 1.0 / math.sqrt(HS)
SCALE2 = SCALE * math.log2(math.e)
F32 = jnp.float32
BF16 = jnp.bfloat16

CORE_SWAP = [(i, i ^ 1) for i in range(16)]
PAIR_SWAP = [(i, i ^ 8) for i in range(16)]
DIAG_SWAP = [(i, i ^ 9) for i in range(16)]
SAME_CORE = [[2 * j + c for j in range(CHIPS)] for c in range(2)]
REDUCE = [
    [(8 * h + 2 * y + c) * 8 + f for f in range(8) for y in range(4)]
    for h in range(2)
    for c in range(2)
]


def dot_nt(a, b):
    return lax.dot_general(a, b, (((1,), (1,)), ((), ())), preferred_element_type=F32)


def dot_tn(a, b):
    return lax.dot_general(a, b, (((0,), (0,)), ((), ())), preferred_element_type=F32)


def dot_nn(a, b):
    return lax.dot_general(a, b, (((1,), (0,)), ((), ())), preferred_element_type=F32)


class Load:
    def __init__(self, copy, ref):
        self.copy, self.ref, self.done = copy, ref, False

    def get(self):
        if not self.done:
            self.copy.wait()
            self.done = True
        return self.ref


class Store:
    def __init__(self, hbm, ref, sems):
        self.hbm, self.ref, self.sems, self.copies = hbm, ref, sems, []

    def push(self, *index):
        src = self.ref.at[index] if index else self.ref
        dst = self.hbm.at[index] if index else self.hbm
        copy = pltpu.make_async_copy(src, dst, next(self.sems))
        copy.start()
        self.copies.append(copy)


SPACES = {"S": pltpu.SMEM, "V": pltpu.VMEM, "H": pltpu.HBM, "A": pl.ANY, "R": pltpu.HBM}


def call(kernel, ins, outs, scratch=(), flops=0, mib=14):
    copied = [
        pltpu.VMEM(jax.eval_shape(lambda x: x[i[2]] if len(i) > 2 else x, i[1]).shape, i[1].dtype)
        for i in ins
        if i[0] in "HA"
    ] + [pltpu.VMEM(o[1], o[2]) for o in outs if o[0] == "H"]

    def body(*refs):
        refs = list(refs)
        in_refs = [refs.pop(0) for _ in ins]
        out_refs = [refs.pop(0) for _ in outs]
        sem_ref = refs.pop(0)
        buffers = [refs.pop(0) for _ in copied]
        sems = (sem_ref.at[n] for n in range(SEMS))
        given, made = [], []
        for one, ref in zip(ins, in_refs):
            if one[0] in "HA":
                buffer = buffers.pop(0)
                copy = pltpu.make_async_copy(
                    ref.at[one[2]] if len(one) > 2 else ref, buffer, next(sems)
                )
                copy.start()
                ref = Load(copy, buffer)
            given.append(ref)
        for one, ref in zip(outs, out_refs):
            made.append(Store(ref, buffers.pop(0), sems) if one[0] == "H" else ref)
        more = kernel(given, made, refs, sems) or []
        for one in given:
            if isinstance(one, Load):
                one.get()
        for one in made:
            if isinstance(one, Store):
                for copy in one.copies:
                    copy.wait()
        for copy in more:
            copy.wait()

    result = pl.pallas_call(
        body,
        out_shape=[
            SPACES[o[0]](o[1], o[2]) if o[0] in "HR" else jax.ShapeDtypeStruct(o[1], o[2])
            for o in outs
        ],
        in_specs=[pl.BlockSpec(memory_space=SPACES[i[0]]) for i in ins],
        out_specs=[pl.BlockSpec(memory_space=SPACES[o[0]]) for o in outs],
        scratch_shapes=[pltpu.SemaphoreType.DMA((SEMS,)), *copied, *scratch],
        compiler_params=pltpu.CompilerParams(vmem_limit_bytes=mib * 1024 * 1024),
        cost_estimate=pl.CostEstimate(flops=flops, bytes_accessed=2_000_000, transcendentals=0),
    )(*[
        pltpu.with_memory_space_constraint(i[1], pltpu.HBM) if i[0] in "HR" else i[1] for i in ins
    ])
    return result[0] if len(outs) == 1 else result


def pack_kernel(ins, outs, scratch, sems):
    core_ref, high_ref, q_ref, k_ref, v_ref, w_ref, up_ref = ins
    out_ref, half_ref, keep_ref, core_out_ref, pair_ref, diag_ref = outs
    core, high = core_ref[0], high_ref[0]
    half = half_ref.shape[1]
    quarter = half // 2
    copies = []

    def copy(src, dst):
        copies.append(pltpu.make_async_copy(src, dst, next(sems)))
        copies[-1].start()

    for a in range(HEADS):
        cols = pl.ds(a * HS, HS)
        copy(q_ref.at[0, :, cols], out_ref.at[a, 0])
        copy(k_ref.at[0, :, cols], out_ref.at[a, 1])
        copy(v_ref.at[0, :, cols], out_ref.at[a, 2])
    copy(w_ref.at[:, pl.ds(pl.multiple_of(core * half, half), half)], half_ref)
    for ref, x, c in (
        (keep_ref, high, core),
        (core_out_ref, high, 1 - core),
        (pair_ref, 1 - high, core),
        (diag_ref, 1 - high, 1 - core),
    ):
        at = pl.multiple_of(x * half + c * quarter, quarter)
        copy(up_ref.at[0, :, pl.ds(at, quarter)], ref)
    return copies


def in_order(core, own_ref, other_ref, slot, dst_ref):
    for j in range(CHIPS):
        own = pl.multiple_of(2 * BLOCK * j + BLOCK * core, BLOCK)
        other = pl.multiple_of(2 * BLOCK * j + BLOCK * (1 - core), BLOCK)
        dst_ref[pl.ds(own, BLOCK)] = own_ref[j, slot]
        dst_ref[pl.ds(other, BLOCK)] = other_ref[j, slot]


def chunks_of(m):
    stop = min(SPAN * (m + 1) + REACH, LEN)
    return [(start, min(start + SPAN, stop)) for start in range(0, stop, SPAN)]


def masked_scores(k_s, q, end, m, start, stop):
    scores = dot_nt(k_s[start:stop], q)
    if stop > SPAN * m:
        at = lax.broadcasted_iota(jnp.int32, scores.shape, 0) + start
        scores = jnp.where(at < end, scores, NEG)
    return scores


def forward_kernel(ins, outs, scratch, sems):
    core_ref, own_ref, other_ref, end_ref, valid_ref = ins
    ctx_out, lse_out, q_out, k_out, v_out = outs
    (s_s,) = scratch
    core = core_ref[0]
    k_s, v_s = k_out.ref, v_out.ref
    in_order(core, own_ref, other_ref, 1, k_s)
    k_out.push()
    in_order(core, own_ref, other_ref, 2, v_s)
    v_out.push()
    q_out.ref[...] = own_ref[:, 0]
    q_out.push()
    for m in range(4):
        q = own_ref[2 * m : 2 * m + 2, 0].reshape(TILE, HS)
        end = end_ref[m]
        top = jnp.full((1, TILE), NEG, F32)
        for start, stop in chunks_of(m):
            scores = masked_scores(k_s, q, end, m, start, stop)
            s_s[start:stop] = scores
            top = jnp.maximum(top, jnp.max(scores, axis=0, keepdims=True))
        top2 = top * SCALE2
        total = jnp.zeros((1, TILE), F32)
        acc = jnp.zeros((HS, TILE), F32)
        for start, stop in chunks_of(m):
            p = jnp.exp2(s_s[start:stop] * SCALE2 - top2)
            total = total + jnp.sum(p, axis=0, keepdims=True)
            acc = acc + dot_tn(v_s[start:stop], p.astype(BF16))
        lse_out.ref[m] = top2 + jnp.log2(total)
        ctx = (acc * (valid_ref[m] / total)).T.astype(BF16)
        for t in range(2):
            j = 2 * m + t
            block = ctx[t * BLOCK : (t + 1) * BLOCK]
            ctx_out.ref[j, 0] = block
            ctx_out.ref[j ^ 4, 1] = block
            ctx_out.push(j, 0)
            ctx_out.push(j ^ 4, 1)
    lse_out.push()


def backward_kernel(ins, outs, scratch, sems):
    core_ref, q_in, k_in, grad_in, v_in, ctx_in, end_in, lse_in = ins
    dq_out, keep_out, send_out = outs
    dk_s, dv_s = scratch
    core = core_ref[0]
    dk_s[...] = jnp.zeros(dk_s.shape, F32)
    dv_s[...] = jnp.zeros(dv_s.shape, F32)
    end_ref, lse_ref = end_in.get(), lse_in.get()
    q_ref, k_s = q_in.get(), k_in.get()
    grad_ref, v_s, ctx_ref = grad_in.get(), v_in.get(), ctx_in.get()
    for m in range(3, -1, -1):
        rows = slice(2 * m, 2 * m + 2)
        q = q_ref[rows].reshape(TILE, HS)
        do = grad_ref[rows].reshape(TILE, HS)
        ctx = ctx_ref[rows].reshape(TILE, HS)
        delta = jnp.sum((do.astype(F32) * ctx.astype(F32)).T, axis=0, keepdims=True)
        end = end_ref[m]
        lse = lse_ref[m]
        dq = jnp.zeros((HS, TILE), F32)
        for start, stop in chunks_of(m):
            scores = masked_scores(k_s, q, end, m, start, stop)
            p = jnp.exp2(scores * SCALE2 - lse)
            dp = dot_nt(v_s[start:stop], do)
            ds = (p * (dp - delta) * SCALE).astype(BF16)
            dv_s[start:stop] += dot_nn(p.astype(BF16), do)
            dk_s[start:stop] += dot_nn(ds, q)
            dq = dq + dot_tn(k_s[start:stop], ds)
        dq_rows = dq.T.astype(BF16)
        dq_out.ref[2 * m] = dq_rows[:BLOCK]
        dq_out.ref[2 * m + 1] = dq_rows[BLOCK:]
        dq_out.push(pl.ds(2 * m, 2))
        first = 2 * m + 1 if m else 0
        last = 2 * m + 3 if m < 3 else CHIPS
        for j in range(first, last):
            own = pl.multiple_of(2 * BLOCK * j + BLOCK * core, BLOCK)
            other = pl.multiple_of(2 * BLOCK * j + BLOCK * (1 - core), BLOCK)
            send_out.ref[j, 0] = dk_s[pl.ds(other, BLOCK)].astype(BF16)
            send_out.ref[j, 1] = dv_s[pl.ds(other, BLOCK)].astype(BF16)
            send_out.push(j)
            keep_out.ref[j, 0] = dk_s[pl.ds(own, BLOCK)]
            keep_out.ref[j, 1] = dv_s[pl.ds(own, BLOCK)]
            keep_out.push(j)


def project_kernel(ins, outs, scratch, sems):
    core_ref, row_ref, valid_ref, up_in, own_in = ins[:5]
    mine, other = ins[5:12], ins[12:19]
    out = outs[0]
    core, row = core_ref[0], row_ref[0]
    half = up_in.ref.shape[1] // 2
    valid = valid_ref[...]
    up_ref = up_in.get()
    out.ref[row] = (dot_nt(up_ref[...], own_in.get()[...]) * valid).astype(BF16)
    out.push(row)
    up_mine = up_ref[:, pl.ds(pl.multiple_of(core * half, half), half)]
    up_other = up_ref[:, pl.ds(pl.multiple_of((1 - core) * half, half), half)]
    for s in range(1, HEADS):
        total = dot_nt(up_mine, mine[s - 1].get()[...]) + dot_nt(up_other, other[s - 1].get()[...])
        at = jnp.bitwise_xor(row, s)
        out.ref[at] = (total * valid).astype(BF16)
        out.push(at)


def attend_kernel(ins, outs, scratch, sems):
    core_ref, row_ref, ctx_in, own_in = ins[:4]
    mine, other = ins[4:11], ins[11:18]
    out = outs[0]
    core, row = core_ref[0], row_ref[0]
    ctx_ref, own_ref = ctx_in.get(), own_in.get()
    half = own_ref.shape[1] // 2
    ctx = jnp.concatenate([ctx_ref[jnp.bitwise_xor(row, s)] for s in range(HEADS)], axis=1)
    step = half // 4
    for side, parts in ((core, mine), (1 - core, other)):
        parts = [part.get() for part in parts]
        for n in range(4):
            at = pl.ds(pl.multiple_of(side * half + n * step, step), step)
            cols = slice(n * step, (n + 1) * step)
            weight = jnp.concatenate(
                [own_ref[:, at]] + [part[:, cols] for part in parts], axis=0
            )
            out.ref[0, :, at] = dot_nn(ctx, weight).astype(BF16)
            out.push(0, slice(None), at)


def weight_kernel(ins, outs, scratch, sems):
    out = outs[0]
    keep, pair, core, diag, ctx_ref, ctx_other_ref = [one.get() for one in ins]
    quarter = keep.shape[1]
    up = jnp.concatenate([keep[...], pair[...]], axis=0)
    up_other = jnp.concatenate([core[...], diag[...]], axis=0)
    for a in range(HEADS):
        total = dot_tn(ctx_ref[a].reshape(TILE, HS), up)
        total = total + dot_tn(ctx_other_ref[a].reshape(TILE, HS), up_other)
        part = pl.ds(4 * a, 4)
        out.ref[part] = total.reshape(4, HS // 4, quarter).astype(BF16)
        out.push(part)


def join_kernel(ins, outs, scratch, sems):
    dq_in, keep_in, came_in, terms_ref = ins
    out_ref = outs[0]
    total = terms_ref[0].astype(F32)
    for s in range(1, terms_ref.shape[0]):
        total = total + terms_ref[s].astype(F32)
    weight = total.astype(BF16)
    rows = weight.shape[0]
    for j in range(CHIPS):
        for t in range(4):
            out_ref[j, 3, t * rows : (t + 1) * rows] = weight[:, t * HS : (t + 1) * HS]
    dq_ref, keep_ref, came_ref = dq_in.get(), keep_in.get(), came_in.get()
    for j in range(CHIPS):
        out_ref[j, 0] = dq_ref[j]
        out_ref[j, 1] = (keep_ref[j, 0] + came_ref[j, 0].astype(F32)).astype(BF16)
        out_ref[j, 2] = (keep_ref[j, 1] + came_ref[j, 1].astype(F32)).astype(BF16)


def unpack_kernel(ins, outs, scratch, sems):
    core_ref, mine_ref, other_ref = ins
    dw_out = outs[3]
    core = core_ref[0]
    copies = []
    for a in range(HEADS):
        for i in range(3):
            dst = outs[i].at[0, :, pl.ds(a * HS, HS)]
            copies.append(pltpu.make_async_copy(mine_ref.at[a, i], dst, next(sems)))
            copies[-1].start()
    for y in range(4):
        rows = pl.ds(32 * y, 32)
        for x in range(2):
            a = 4 * x + y
            for t in range(4):
                part = slice(32 * t, 32 * t + 32)
                at = pl.multiple_of(1024 * x + 512 * core + HS * t, HS)
                dw_out.ref[rows, pl.ds(at, HS)] = mine_ref[a, 3, part].astype(F32)
                at = pl.multiple_of(1024 * x + 512 * (1 - core) + HS * t, HS)
                dw_out.ref[rows, pl.ds(at, HS)] = other_ref[a, part].astype(F32)
        dw_out.push(rows)
    return copies


def exchange(operand):
    return lax.all_to_all(
        operand, "ctx", split_axis=0, concat_axis=0, tiled=True, axis_index_groups=SAME_CORE
    )


def after(value, *others):
    return lax.optimization_barrier((value, *others))[0]


def shards(query_rows, key_rows, value_rows, session, lengths, out_weight, upstream):
    index = lax.axis_index("ctx").astype(jnp.int32)
    core = index & 1
    core_ref = core.reshape(1)
    high_ref = (index >> 3).reshape(1)
    row_ref = lax.axis_index("fsdp").astype(jnp.int32).reshape(1)
    valid_len = lengths[0]
    width = out_weight.shape[1]
    half = width // 2
    quarter = half // 2

    part = ("R", (BLOCK, quarter), BF16)
    packed, own_half, up_keep, up_core, up_pair, up_diag = call(
        pack_kernel,
        [
            ("S", core_ref), ("S", high_ref), ("R", query_rows), ("R", key_rows),
            ("R", value_rows), ("R", out_weight), ("R", upstream),
        ],
        [("R", (HEADS, 3, BLOCK, HS), BF16), ("R", (HS, half), BF16), part, part, part, part],
    )
    own = exchange(packed)

    session_ids = session[0]
    positions = jnp.arange(LEN, dtype=jnp.int32).reshape(CHIPS, 2, BLOCK)
    own_sessions = lax.dynamic_index_in_dim(session_ids.reshape(CHIPS, 2, BLOCK), core, 1, False)
    own_positions = lax.dynamic_index_in_dim(positions, core, 1, False)
    end = jnp.sum(
        (session_ids[:, None] <= own_sessions.reshape(1, -1)).astype(jnp.int32), axis=0
    )
    end = jnp.minimum(end, valid_len).reshape(4, 1, TILE)
    valid = (own_positions < valid_len).astype(F32).reshape(4, 1, TILE)
    rows_here = index * BLOCK + jnp.arange(BLOCK, dtype=jnp.int32)
    valid_here = (rows_here < valid_len).astype(F32)[:, None]

    def gather(halves, s):
        piece = lax.ppermute(halves, "fsdp", [(i, i ^ s) for i in range(8)])
        return piece, lax.ppermute(piece, "ctx", CORE_SWAP)

    pieces = [gather(own_half, s) for s in (1, 2, 3)]
    own = after(own, end, valid, valid_here, *[one for one, _ in pieces])
    own_half = after(own_half, own)
    pieces += [gather(own_half, s) for s in (4, 5, 6, 7)]
    mine = [("A", one) for one, _ in pieces]
    other_half = [("A", one) for _, one in pieces]

    other = lax.ppermute(own, "ctx", CORE_SWAP)
    pairs = 4 * TILE * SPAN * 5 // 2
    rows = ("H", (LEN, HS), BF16)
    context, lse, query, key, value = call(
        forward_kernel,
        [("S", core_ref), ("V", own), ("V", other), ("V", end), ("V", valid)],
        [
            ("H", (CHIPS, 2, BLOCK, HS), BF16),
            ("H", (4, 1, TILE), F32),
            ("H", (CHIPS, BLOCK, HS), BF16),
            rows,
            rows,
        ],
        scratch=(pltpu.VMEM((LEN, TILE), F32),),
        flops=4 * pairs * HS,
    )
    context_mine = exchange(context)
    up_pair = lax.ppermute(after(up_pair, context), "ctx", PAIR_SWAP)
    up_diag = lax.ppermute(after(up_diag, context), "ctx", DIAG_SWAP)
    up_core = lax.ppermute(after(up_core, context), "ctx", CORE_SWAP)
    grads = call(
        project_kernel,
        [
            ("S", core_ref), ("S", row_ref), ("V", valid_here), ("H", upstream, 0),
            ("H", out_weight), *mine, *other_half,
        ],
        [("H", (HEADS, BLOCK, HS), BF16)],
        flops=2 * 128 * 1024 * 2048,
    )
    grads = exchange(after(grads, context_mine))
    context_other = lax.ppermute(context_mine, "ctx", CORE_SWAP)
    terms = call(
        weight_kernel,
        [
            ("H", up_keep), ("A", up_pair), ("A", up_core), ("A", up_diag),
            ("A", context_mine), ("A", context_other),
        ],
        [("H", (32, 32, quarter), BF16)],
        flops=2 * 512 * 1024 * 512,
    )
    terms = lax.all_to_all(
        after(terms, grads),
        ("ctx", "fsdp"),
        split_axis=0,
        concat_axis=0,
        tiled=True,
        axis_index_groups=REDUCE,
    )
    dq, keep, send = call(
        backward_kernel,
        [
            ("S", core_ref), ("H", query), ("H", key), ("H", grads), ("H", value),
            ("H", context, (slice(None), 0)), ("A", end), ("H", lse),
        ],
        [
            ("H", (CHIPS, BLOCK, HS), BF16),
            ("H", (CHIPS, 2, BLOCK, HS), F32),
            ("H", (CHIPS, 2, BLOCK, HS), BF16),
        ],
        scratch=(pltpu.VMEM((LEN, HS), F32), pltpu.VMEM((LEN, HS), F32)),
        flops=10 * pairs * HS,
    )
    came = lax.ppermute(send, "ctx", CORE_SWAP)
    attended = call(
        attend_kernel,
        [
            ("S", core_ref), ("S", row_ref), ("A", context_mine, (slice(None), 0)),
            ("H", out_weight), *mine, *other_half,
        ],
        [("H", (1, BLOCK, width), BF16)],
        flops=2 * 128 * 1024 * 2048,
    )
    joined = call(
        join_kernel,
        [("H", after(dq, attended)), ("H", keep), ("H", came), ("V", terms)],
        [("V", (CHIPS, 4, BLOCK, HS), BF16)],
    )
    result = exchange(joined)
    weight_part = lax.ppermute(result[:, 3], "ctx", CORE_SWAP)
    grad = ("R", (1, BLOCK, HEADS * HS), BF16)
    query_grad, key_grad, value_grad, weight_grad = call(
        unpack_kernel,
        [("S", core_ref), ("V", result), ("V", weight_part)],
        [grad, grad, grad, ("H", (HS, width), F32)],
    )
    return (attended, query_grad, key_grad, value_grad, weight_grad)


def solution(mesh):
    rows = P("fsdp", "ctx", None)
    return jax.shard_map(
        shards,
        mesh=mesh,
        in_specs=(rows, rows, rows, P("fsdp", None), P("fsdp"), P("fsdp", None), rows),
        out_specs=(rows, rows, rows, rows, P("fsdp", None)),
        check_vma=False,
    )
```

```python
import functools
import math

import jax
import jax.numpy as jnp
from jax import lax
from jax.experimental import pallas as pl
from jax.experimental.pallas import tpu as pltpu
from jax.sharding import PartitionSpec as P

HEADS = 8
HS = 128
BLOCK = 128
TILE = 256
SPAN = 512
REACH = 128
CHIPS = 8
LEN = 2048
NEG = -1e30
SEMS = 48
SCALE = 1.0 / math.sqrt(HS)
SCALE2 = SCALE * math.log2(math.e)
F32 = jnp.float32
BF16 = jnp.bfloat16

CORE_SWAP = [(i, i ^ 1) for i in range(16)]
PAIR_SWAP = [(i, i ^ 8) for i in range(16)]
DIAG_SWAP = [(i, i ^ 9) for i in range(16)]
SAME_CORE = [[2 * j + c for j in range(CHIPS)] for c in range(2)]
REDUCE = [
    [(8 * h + 2 * y + c) * 8 + f for f in range(8) for y in range(4)]
    for h in range(2)
    for c in range(2)
]


def dot_nt(a, b):
    return lax.dot_general(a, b, (((1,), (1,)), ((), ())), preferred_element_type=F32)


def dot_tn(a, b):
    return lax.dot_general(a, b, (((0,), (0,)), ((), ())), preferred_element_type=F32)


def dot_nn(a, b):
    return lax.dot_general(a, b, (((1,), (0,)), ((), ())), preferred_element_type=F32)


class Load:
    def __init__(self, copy, ref):
        self.copy, self.ref, self.done = copy, ref, False

    def get(self):
        if not self.done:
            self.copy.wait()
            self.done = True
        return self.ref


class Store:
    def __init__(self, hbm, ref, sems):
        self.hbm, self.ref, self.sems, self.copies = hbm, ref, sems, []

    def push(self, *index):
        src = self.ref.at[index] if index else self.ref
        dst = self.hbm.at[index] if index else self.hbm
        copy = pltpu.make_async_copy(src, dst, next(self.sems))
        copy.start()
        self.copies.append(copy)


SPACES = {"S": pltpu.SMEM, "V": pltpu.VMEM, "H": pltpu.HBM, "A": pl.ANY, "R": pltpu.HBM}


def call(kernel, ins, outs, scratch=(), flops=0, mib=14):
    copied = [
        pltpu.VMEM(jax.eval_shape(lambda x: x[i[2]] if len(i) > 2 else x, i[1]).shape, i[1].dtype)
        for i in ins
        if i[0] in "HA"
    ] + [pltpu.VMEM(o[1], o[2]) for o in outs if o[0] == "H"]

    def body(*refs):
        refs = list(refs)
        in_refs = [refs.pop(0) for _ in ins]
        out_refs = [refs.pop(0) for _ in outs]
        sem_ref = refs.pop(0)
        buffers = [refs.pop(0) for _ in copied]
        sems = (sem_ref.at[n] for n in range(SEMS))
        given, made = [], []
        for one, ref in zip(ins, in_refs):
            if one[0] in "HA":
                buffer = buffers.pop(0)
                copy = pltpu.make_async_copy(
                    ref.at[one[2]] if len(one) > 2 else ref, buffer, next(sems)
                )
                copy.start()
                ref = Load(copy, buffer)
            given.append(ref)
        for one, ref in zip(outs, out_refs):
            made.append(Store(ref, buffers.pop(0), sems) if one[0] == "H" else ref)
        more = kernel(given, made, refs, sems) or []
        for one in given:
            if isinstance(one, Load):
                one.get()
        for one in made:
            if isinstance(one, Store):
                for copy in one.copies:
                    copy.wait()
        for copy in more:
            copy.wait()

    result = pl.pallas_call(
        body,
        out_shape=[
            SPACES[o[0]](o[1], o[2]) if o[0] in "HR" else jax.ShapeDtypeStruct(o[1], o[2])
            for o in outs
        ],
        in_specs=[pl.BlockSpec(memory_space=SPACES[i[0]]) for i in ins],
        out_specs=[pl.BlockSpec(memory_space=SPACES[o[0]]) for o in outs],
        scratch_shapes=[pltpu.SemaphoreType.DMA((SEMS,)), *copied, *scratch],
        compiler_params=pltpu.CompilerParams(vmem_limit_bytes=mib * 1024 * 1024),
        cost_estimate=pl.CostEstimate(flops=flops, bytes_accessed=2_000_000, transcendentals=0),
    )(*[
        pltpu.with_memory_space_constraint(i[1], pltpu.HBM) if i[0] in "HR" else i[1] for i in ins
    ])
    return result[0] if len(outs) == 1 else result


def pack_kernel(ins, outs, scratch, sems):
    core_ref, high_ref, *data = ins
    out_ref, half_ref, keep_ref, core_out_ref, pair_ref, diag_ref = outs
    core, high = core_ref[0], high_ref[0]
    half = half_ref.shape[1]
    quarter = half // 2
    copies = []

    def copy(src, dst):
        copies.append(pltpu.make_async_copy(src, dst, next(sems)))
        copies[-1].start()

    for i in range(3):
        ref = data[i].get()
        for a in range(HEADS):
            copy(ref.at[:, pl.ds(a * HS, HS)], out_ref.at[a, i])
    w_ref = data[3].get()
    copy(w_ref.at[:, pl.ds(pl.multiple_of(core * half, half), half)], half_ref)
    up_ref = data[4].get()
    for ref, x, c in (
        (keep_ref, high, core),
        (core_out_ref, high, 1 - core),
        (pair_ref, 1 - high, core),
        (diag_ref, 1 - high, 1 - core),
    ):
        at = pl.multiple_of(x * half + c * quarter, quarter)
        copy(up_ref.at[:, pl.ds(at, quarter)], ref)
    return copies


def in_order(core, own_ref, other_ref, slot, dst_ref):
    for j in range(CHIPS):
        own = pl.multiple_of(2 * BLOCK * j + BLOCK * core, BLOCK)
        other = pl.multiple_of(2 * BLOCK * j + BLOCK * (1 - core), BLOCK)
        dst_ref[pl.ds(own, BLOCK)] = own_ref[j, slot]
        dst_ref[pl.ds(other, BLOCK)] = other_ref[j, slot]


def chunks_of(m):
    stop = min(SPAN * (m + 1) + REACH, LEN)
    return [(start, min(start + SPAN, stop)) for start in range(0, stop, SPAN)]


def masked_scores(k_s, q, end, m, start, stop):
    scores = dot_nt(k_s[start:stop], q)
    if stop > SPAN * m:
        at = lax.broadcasted_iota(jnp.int32, scores.shape, 0) + start
        scores = jnp.where(at < end, scores, NEG)
    return scores


def forward_kernel(ins, outs, scratch, sems):
    core_ref, own_ref, other_ref, end_ref, valid_ref = ins
    ctx_out, lse_out, q_out, k_out, v_out = outs
    (s_s,) = scratch
    core = core_ref[0]
    k_s, v_s = k_out.ref, v_out.ref
    in_order(core, own_ref, other_ref, 1, k_s)
    k_out.push()
    in_order(core, own_ref, other_ref, 2, v_s)
    v_out.push()
    q_out.ref[...] = own_ref[:, 0]
    q_out.push()
    for m in range(4):
        q = own_ref[2 * m : 2 * m + 2, 0].reshape(TILE, HS)
        end = end_ref[m]
        top = jnp.full((1, TILE), NEG, F32)
        for start, stop in chunks_of(m):
            scores = masked_scores(k_s, q, end, m, start, stop)
            s_s[start:stop] = scores
            top = jnp.maximum(top, jnp.max(scores, axis=0, keepdims=True))
        top2 = top * SCALE2
        total = jnp.zeros((1, TILE), F32)
        acc = jnp.zeros((HS, TILE), F32)
        for start, stop in chunks_of(m):
            p = jnp.exp2(s_s[start:stop] * SCALE2 - top2)
            total = total + jnp.sum(p, axis=0, keepdims=True)
            acc = acc + dot_tn(v_s[start:stop], p.astype(BF16))
        lse_out.ref[m] = top2 + jnp.log2(total)
        ctx = (acc * (valid_ref[m] / total)).T.astype(BF16)
        for t in range(2):
            j = 2 * m + t
            block = ctx[t * BLOCK : (t + 1) * BLOCK]
            ctx_out.ref[j, 0] = block
            ctx_out.ref[j ^ 4, 1] = block
            ctx_out.push(j, 0)
            ctx_out.push(j ^ 4, 1)
    lse_out.push()


def backward_kernel(ins, outs, scratch, sems):
    core_ref, q_in, k_in, grad_in, v_in, ctx_in, end_in, lse_in = ins
    dq_out, keep_out, send_out = outs
    dk_s, dv_s = scratch
    core = core_ref[0]
    dk_s[...] = jnp.zeros(dk_s.shape, F32)
    dv_s[...] = jnp.zeros(dv_s.shape, F32)
    end_ref, lse_ref = end_in.get(), lse_in.get()
    q_ref, k_s = q_in.get(), k_in.get()
    grad_ref, v_s, ctx_ref = grad_in.get(), v_in.get(), ctx_in.get()
    for m in range(3, -1, -1):
        rows = slice(2 * m, 2 * m + 2)
        q = q_ref[rows].reshape(TILE, HS)
        do = grad_ref[rows].reshape(TILE, HS)
        ctx = ctx_ref[rows].reshape(TILE, HS)
        delta = jnp.sum((do.astype(F32) * ctx.astype(F32)).T, axis=0, keepdims=True)
        end = end_ref[m]
        lse = lse_ref[m]
        dq = jnp.zeros((HS, TILE), F32)
        for start, stop in chunks_of(m):
            scores = masked_scores(k_s, q, end, m, start, stop)
            p = jnp.exp2(scores * SCALE2 - lse)
            dp = dot_nt(v_s[start:stop], do)
            ds = (p * (dp - delta) * SCALE).astype(BF16)
            dv_s[start:stop] += dot_nn(p.astype(BF16), do)
            dk_s[start:stop] += dot_nn(ds, q)
            dq = dq + dot_tn(k_s[start:stop], ds)
        dq_rows = dq.T.astype(BF16)
        dq_out.ref[2 * m] = dq_rows[:BLOCK]
        dq_out.ref[2 * m + 1] = dq_rows[BLOCK:]
        dq_out.push(pl.ds(2 * m, 2))
        first = 2 * m + 1 if m else 0
        last = 2 * m + 3 if m < 3 else CHIPS
        for j in range(first, last):
            own = pl.multiple_of(2 * BLOCK * j + BLOCK * core, BLOCK)
            other = pl.multiple_of(2 * BLOCK * j + BLOCK * (1 - core), BLOCK)
            send_out.ref[j, 0] = dk_s[pl.ds(other, BLOCK)].astype(BF16)
            send_out.ref[j, 1] = dv_s[pl.ds(other, BLOCK)].astype(BF16)
            send_out.push(j)
            keep_out.ref[j, 0] = dk_s[pl.ds(own, BLOCK)]
            keep_out.ref[j, 1] = dv_s[pl.ds(own, BLOCK)]
            keep_out.push(j)


def project_kernel(ins, outs, scratch, sems):
    core_ref, row_ref, valid_ref, up_in, own_in = ins[:5]
    mine, other = ins[5:12], ins[12:19]
    out = outs[0]
    core, row = core_ref[0], row_ref[0]
    half = up_in.ref.shape[1] // 2
    valid = valid_ref[...]
    up_ref = up_in.get()
    out.ref[row] = (dot_nt(up_ref[...], own_in.get()[...]) * valid).astype(BF16)
    out.push(row)
    up_mine = up_ref[:, pl.ds(pl.multiple_of(core * half, half), half)]
    up_other = up_ref[:, pl.ds(pl.multiple_of((1 - core) * half, half), half)]
    for s in range(1, HEADS):
        total = dot_nt(up_mine, mine[s - 1][...]) + dot_nt(up_other, other[s - 1][...])
        at = jnp.bitwise_xor(row, s)
        out.ref[at] = (total * valid).astype(BF16)
        out.push(at)


def attend_kernel(ins, outs, scratch, sems):
    core_ref, row_ref, ctx_in, own_in = ins[:4]
    mine, other = ins[4:11], ins[11:18]
    out = outs[0]
    core, row = core_ref[0], row_ref[0]
    ctx_ref, own_ref = ctx_in.get(), own_in.get()
    half = own_ref.shape[1] // 2
    ctx = jnp.concatenate([ctx_ref[jnp.bitwise_xor(row, s)] for s in range(HEADS)], axis=1)
    step = half // 4
    for side, parts in ((core, mine), (1 - core, other)):
        for n in range(4):
            at = pl.ds(pl.multiple_of(side * half + n * step, step), step)
            cols = slice(n * step, (n + 1) * step)
            weight = jnp.concatenate(
                [own_ref[:, at]] + [part[:, cols] for part in parts], axis=0
            )
            out.ref[0, :, at] = dot_nn(ctx, weight).astype(BF16)
            out.push(0, slice(None), at)


def weight_kernel(ins, outs, scratch, sems):
    out = outs[0]
    keep, pair, core, diag, ctx_ref, ctx_other_ref = [one.get() for one in ins]
    quarter = keep.shape[1]
    up = jnp.concatenate([keep[...], pair[...]], axis=0)
    up_other = jnp.concatenate([core[...], diag[...]], axis=0)
    for a in range(HEADS):
        total = dot_tn(ctx_ref[a].reshape(TILE, HS), up)
        total = total + dot_tn(ctx_other_ref[a].reshape(TILE, HS), up_other)
        part = pl.ds(4 * a, 4)
        out.ref[part] = total.reshape(4, HS // 4, quarter).astype(BF16)
        out.push(part)


def join_kernel(ins, outs, scratch, sems):
    dq_in, keep_in, came_in, terms_ref = ins
    out_ref = outs[0]
    total = terms_ref[0].astype(F32)
    for s in range(1, terms_ref.shape[0]):
        total = total + terms_ref[s].astype(F32)
    weight = total.astype(BF16)
    rows = weight.shape[0]
    for j in range(CHIPS):
        for t in range(4):
            out_ref[j, 3, t * rows : (t + 1) * rows] = weight[:, t * HS : (t + 1) * HS]
    dq_ref, keep_ref, came_ref = dq_in.get(), keep_in.get(), came_in.get()
    for j in range(CHIPS):
        out_ref[j, 0] = dq_ref[j]
        out_ref[j, 1] = (keep_ref[j, 0] + came_ref[j, 0].astype(F32)).astype(BF16)
        out_ref[j, 2] = (keep_ref[j, 1] + came_ref[j, 1].astype(F32)).astype(BF16)


def unpack_kernel(ins, outs, scratch, sems):
    core_ref, mine_ref, other_ref = ins
    dw_out = outs[3]
    core = core_ref[0]
    copies = []
    for a in range(HEADS):
        for i in range(3):
            dst = outs[i].at[0, :, pl.ds(a * HS, HS)]
            copies.append(pltpu.make_async_copy(mine_ref.at[a, i], dst, next(sems)))
            copies[-1].start()
    for y in range(4):
        rows = pl.ds(32 * y, 32)
        for x in range(2):
            a = 4 * x + y
            for t in range(4):
                part = slice(32 * t, 32 * t + 32)
                at = pl.multiple_of(1024 * x + 512 * core + HS * t, HS)
                dw_out.ref[rows, pl.ds(at, HS)] = mine_ref[a, 3, part].astype(F32)
                at = pl.multiple_of(1024 * x + 512 * (1 - core) + HS * t, HS)
                dw_out.ref[rows, pl.ds(at, HS)] = other_ref[a, part].astype(F32)
        dw_out.push(rows)
    return copies


def exchange(operand):
    return lax.all_to_all(
        operand, "ctx", split_axis=0, concat_axis=0, tiled=True, axis_index_groups=SAME_CORE
    )


def after(value, *others):
    return lax.optimization_barrier((value, *others))[0]


def shards(query_rows, key_rows, value_rows, session, lengths, out_weight, upstream):
    index = lax.axis_index("ctx").astype(jnp.int32)
    core = index & 1
    core_ref = core.reshape(1)
    high_ref = (index >> 3).reshape(1)
    row_ref = lax.axis_index("fsdp").astype(jnp.int32).reshape(1)
    valid_len = lengths[0]
    width = out_weight.shape[1]
    half = width // 2
    quarter = half // 2

    part = ("R", (BLOCK, quarter), BF16)
    packed, own_half, up_keep, up_core, up_pair, up_diag = call(
        pack_kernel,
        [
            ("S", core_ref), ("S", high_ref), ("H", query_rows, 0), ("H", key_rows, 0),
            ("H", value_rows, 0), ("H", out_weight), ("H", upstream, 0),
        ],
        [("R", (HEADS, 3, BLOCK, HS), BF16), ("R", (HS, half), BF16), part, part, part, part],
    )
    own = exchange(packed)

    session_ids = session[0]
    positions = jnp.arange(LEN, dtype=jnp.int32).reshape(CHIPS, 2, BLOCK)
    own_sessions = lax.dynamic_index_in_dim(session_ids.reshape(CHIPS, 2, BLOCK), core, 1, False)
    own_positions = lax.dynamic_index_in_dim(positions, core, 1, False)
    end = jnp.sum(
        (session_ids[:, None] <= own_sessions.reshape(1, -1)).astype(jnp.int32), axis=0
    )
    end = jnp.minimum(end, valid_len).reshape(4, 1, TILE)
    valid = (own_positions < valid_len).astype(F32).reshape(4, 1, TILE)
    rows_here = index * BLOCK + jnp.arange(BLOCK, dtype=jnp.int32)
    valid_here = (rows_here < valid_len).astype(F32)[:, None]

    def step(value, s):
        return lax.ppermute(value, "fsdp", [(i, i ^ s) for i in range(8)])

    own_half = after(own_half, end, valid, valid_here)
    over = step(own_half, 4)
    one, three = step(own_half, 1), step(own_half, 3)
    over_one, over_three = step(over, 1), step(over, 3)
    two, over_two = step(one, 3), step(over_three, 1)
    pieces = [one, two, three, over, over_one, over_two, over_three]
    mine = [("V", piece) for piece in pieces]
    other_half = [("V", lax.ppermute(piece, "ctx", CORE_SWAP)) for piece in pieces]

    own = after(own, end, valid, valid_here, over, one, three)
    other = lax.ppermute(own, "ctx", CORE_SWAP)
    pairs = 4 * TILE * SPAN * 5 // 2
    rows = ("H", (LEN, HS), BF16)
    context, lse, query, key, value = call(
        forward_kernel,
        [("S", core_ref), ("V", own), ("V", other), ("V", end), ("V", valid)],
        [
            ("H", (CHIPS, 2, BLOCK, HS), BF16),
            ("H", (4, 1, TILE), F32),
            ("H", (CHIPS, BLOCK, HS), BF16),
            rows,
            rows,
        ],
        scratch=(pltpu.VMEM((LEN, TILE), F32),),
        flops=4 * pairs * HS,
    )
    context_mine = exchange(context)
    up_pair = lax.ppermute(after(up_pair, context), "ctx", PAIR_SWAP)
    up_diag = lax.ppermute(after(up_diag, context), "ctx", DIAG_SWAP)
    up_core = lax.ppermute(after(up_core, context), "ctx", CORE_SWAP)
    grads = call(
        project_kernel,
        [
            ("S", core_ref), ("S", row_ref), ("V", valid_here), ("H", upstream, 0),
            ("H", out_weight), *mine, *other_half,
        ],
        [("H", (HEADS, BLOCK, HS), BF16)],
        flops=2 * 128 * 1024 * 2048,
    )
    grads = exchange(after(grads, context_mine))
    context_other = lax.ppermute(context_mine, "ctx", CORE_SWAP)
    terms = call(
        weight_kernel,
        [
            ("H", up_keep), ("A", up_pair), ("A", up_core), ("A", up_diag),
            ("A", context_mine), ("A", context_other),
        ],
        [("H", (32, 32, quarter), BF16)],
        flops=2 * 512 * 1024 * 512,
    )
    terms = lax.all_to_all(
        after(terms, grads),
        ("ctx", "fsdp"),
        split_axis=0,
        concat_axis=0,
        tiled=True,
        axis_index_groups=REDUCE,
    )
    dq, keep, send = call(
        backward_kernel,
        [
            ("S", core_ref), ("H", query), ("H", key), ("H", grads), ("H", value),
            ("H", context, (slice(None), 0)), ("A", end), ("H", lse),
        ],
        [
            ("H", (CHIPS, BLOCK, HS), BF16),
            ("H", (CHIPS, 2, BLOCK, HS), F32),
            ("H", (CHIPS, 2, BLOCK, HS), BF16),
        ],
        scratch=(pltpu.VMEM((LEN, HS), F32), pltpu.VMEM((LEN, HS), F32)),
        flops=10 * pairs * HS,
    )
    came = lax.ppermute(send, "ctx", CORE_SWAP)
    attended = call(
        attend_kernel,
        [
            ("S", core_ref), ("S", row_ref), ("A", context_mine, (slice(None), 0)),
            ("H", out_weight), *mine, *other_half,
        ],
        [("H", (1, BLOCK, width), BF16)],
        flops=2 * 128 * 1024 * 2048,
    )
    joined = call(
        join_kernel,
        [("H", after(dq, attended)), ("H", keep), ("H", came), ("V", terms)],
        [("V", (CHIPS, 4, BLOCK, HS), BF16)],
    )
    result = exchange(joined)
    weight_part = lax.ppermute(result[:, 3], "ctx", CORE_SWAP)
    grad = ("R", (1, BLOCK, HEADS * HS), BF16)
    query_grad, key_grad, value_grad, weight_grad = call(
        unpack_kernel,
        [("S", core_ref), ("V", result), ("V", weight_part)],
        [grad, grad, grad, ("H", (HS, width), F32)],
    )
    return (attended, query_grad, key_grad, value_grad, weight_grad)


def solution(mesh):
    rows = P("fsdp", "ctx", None)
    return jax.shard_map(
        shards,
        mesh=mesh,
        in_specs=(rows, rows, rows, P("fsdp", None), P("fsdp"), P("fsdp", None), rows),
        out_specs=(rows, rows, rows, rows, P("fsdp", None)),
        check_vma=False,
    )
```

```python
import functools
import math

import jax
import jax.numpy as jnp
from jax import lax
from jax.experimental import pallas as pl
from jax.experimental.pallas import tpu as pltpu
from jax.sharding import PartitionSpec as P

HEADS = 8
HS = 128
BLOCK = 128
TILE = 256
SPAN = 512
REACH = 128
CHIPS = 8
LEN = 2048
NEG = -1e30
SEMS = 48
SCALE = 1.0 / math.sqrt(HS)
SCALE2 = SCALE * math.log2(math.e)
F32 = jnp.float32
BF16 = jnp.bfloat16

CORE_SWAP = [(i, i ^ 1) for i in range(16)]
PAIR_SWAP = [(i, i ^ 2) for i in range(16)]
DIAG_SWAP = [(i, i ^ 3) for i in range(16)]
SAME_CORE = [[2 * j + c for j in range(CHIPS)] for c in range(2)]
REDUCE = [
    [(4 * p + 2 * h + c) * 8 + f for f in range(8) for p in range(4)]
    for h in range(2)
    for c in range(2)
]


def dot_nt(a, b):
    return lax.dot_general(a, b, (((1,), (1,)), ((), ())), preferred_element_type=F32)


def dot_tn(a, b):
    return lax.dot_general(a, b, (((0,), (0,)), ((), ())), preferred_element_type=F32)


def dot_nn(a, b):
    return lax.dot_general(a, b, (((1,), (0,)), ((), ())), preferred_element_type=F32)


class Load:
    def __init__(self, copy, ref):
        self.copy, self.ref, self.done = copy, ref, False

    def get(self):
        if not self.done:
            self.copy.wait()
            self.done = True
        return self.ref


class Store:
    def __init__(self, hbm, ref, sems):
        self.hbm, self.ref, self.sems, self.copies = hbm, ref, sems, []

    def push(self, *index):
        src = self.ref.at[index] if index else self.ref
        dst = self.hbm.at[index] if index else self.hbm
        copy = pltpu.make_async_copy(src, dst, next(self.sems))
        copy.start()
        self.copies.append(copy)


SPACES = {"S": pltpu.SMEM, "V": pltpu.VMEM, "H": pltpu.HBM, "A": pl.ANY, "R": pltpu.HBM}


def call(kernel, ins, outs, scratch=(), flops=0, mib=14):
    copied = [
        pltpu.VMEM(jax.eval_shape(lambda x: x[i[2]] if len(i) > 2 else x, i[1]).shape, i[1].dtype)
        for i in ins
        if i[0] in "HA"
    ] + [pltpu.VMEM(o[1], o[2]) for o in outs if o[0] == "H"]

    def body(*refs):
        refs = list(refs)
        in_refs = [refs.pop(0) for _ in ins]
        out_refs = [refs.pop(0) for _ in outs]
        sem_ref = refs.pop(0)
        buffers = [refs.pop(0) for _ in copied]
        sems = (sem_ref.at[n] for n in range(SEMS))
        given, made = [], []
        for one, ref in zip(ins, in_refs):
            if one[0] in "HA":
                buffer = buffers.pop(0)
                copy = pltpu.make_async_copy(
                    ref.at[one[2]] if len(one) > 2 else ref, buffer, next(sems)
                )
                copy.start()
                ref = Load(copy, buffer)
            given.append(ref)
        for one, ref in zip(outs, out_refs):
            made.append(Store(ref, buffers.pop(0), sems) if one[0] == "H" else ref)
        more = kernel(given, made, refs, sems) or []
        for one in given:
            if isinstance(one, Load):
                one.get()
        for one in made:
            if isinstance(one, Store):
                for copy in one.copies:
                    copy.wait()
        for copy in more:
            copy.wait()

    result = pl.pallas_call(
        body,
        out_shape=[
            SPACES[o[0]](o[1], o[2]) if o[0] in "HR" else jax.ShapeDtypeStruct(o[1], o[2])
            for o in outs
        ],
        in_specs=[pl.BlockSpec(memory_space=SPACES[i[0]]) for i in ins],
        out_specs=[pl.BlockSpec(memory_space=SPACES[o[0]]) for o in outs],
        scratch_shapes=[pltpu.SemaphoreType.DMA((SEMS,)), *copied, *scratch],
        compiler_params=pltpu.CompilerParams(vmem_limit_bytes=mib * 1024 * 1024),
        cost_estimate=pl.CostEstimate(flops=flops, bytes_accessed=2_000_000, transcendentals=0),
    )(*[
        pltpu.with_memory_space_constraint(i[1], pltpu.HBM) if i[0] in "HR" else i[1] for i in ins
    ])
    return result[0] if len(outs) == 1 else result


def pack_kernel(ins, outs, scratch, sems):
    core_ref, high_ref, *data = ins
    out_ref, half_ref, keep_ref, core_out_ref, pair_ref, diag_ref = outs
    core, high = core_ref[0], high_ref[0]
    half = half_ref.shape[1]
    quarter = half // 2
    copies = []

    def copy(src, dst):
        copies.append(pltpu.make_async_copy(src, dst, next(sems)))
        copies[-1].start()

    for i in range(3):
        ref = data[i].get()
        for a in range(HEADS):
            copy(ref.at[:, pl.ds(a * HS, HS)], out_ref.at[a, i])
    w_ref = data[3].get()
    copy(w_ref.at[:, pl.ds(pl.multiple_of(core * half, half), half)], half_ref)
    up_ref = data[4].get()
    for ref, x, c in (
        (keep_ref, high, core),
        (core_out_ref, high, 1 - core),
        (pair_ref, 1 - high, core),
        (diag_ref, 1 - high, 1 - core),
    ):
        at = pl.multiple_of(x * half + c * quarter, quarter)
        copy(up_ref.at[:, pl.ds(at, quarter)], ref)
    return copies


def in_order(core, own_ref, other_ref, slot, dst_ref):
    for j in range(CHIPS):
        own = pl.multiple_of(2 * BLOCK * j + BLOCK * core, BLOCK)
        other = pl.multiple_of(2 * BLOCK * j + BLOCK * (1 - core), BLOCK)
        dst_ref[pl.ds(own, BLOCK)] = own_ref[j, slot]
        dst_ref[pl.ds(other, BLOCK)] = other_ref[j, slot]


def chunks_of(m):
    stop = min(SPAN * (m + 1) + REACH, LEN)
    return [(start, min(start + SPAN, stop)) for start in range(0, stop, SPAN)]


def masked_scores(k_s, q, end, m, start, stop):
    scores = dot_nt(k_s[start:stop], q)
    if stop > SPAN * m:
        at = lax.broadcasted_iota(jnp.int32, scores.shape, 0) + start
        scores = jnp.where(at < end, scores, NEG)
    return scores


def forward_kernel(ins, outs, scratch, sems):
    core_ref, own_ref, other_ref, end_ref, valid_ref = ins
    ctx_out, lse_out, q_out, k_out, v_out = outs
    (s_s,) = scratch
    core = core_ref[0]
    k_s, v_s = k_out.ref, v_out.ref
    in_order(core, own_ref, other_ref, 1, k_s)
    k_out.push()
    in_order(core, own_ref, other_ref, 2, v_s)
    v_out.push()
    q_out.ref[...] = own_ref[:, 0]
    q_out.push()
    for m in range(4):
        q = own_ref[2 * m : 2 * m + 2, 0].reshape(TILE, HS)
        end = end_ref[m]
        top = jnp.full((1, TILE), NEG, F32)
        for start, stop in chunks_of(m):
            scores = masked_scores(k_s, q, end, m, start, stop)
            s_s[start:stop] = scores
            top = jnp.maximum(top, jnp.max(scores, axis=0, keepdims=True))
        top2 = top * SCALE2
        total = jnp.zeros((1, TILE), F32)
        acc = jnp.zeros((HS, TILE), F32)
        for start, stop in chunks_of(m):
            p = jnp.exp2(s_s[start:stop] * SCALE2 - top2)
            total = total + jnp.sum(p, axis=0, keepdims=True)
            acc = acc + dot_tn(v_s[start:stop], p.astype(BF16))
        lse_out.ref[m] = top2 + jnp.log2(total)
        ctx = (acc * (valid_ref[m] / total)).T.astype(BF16)
        for t in range(2):
            j = 2 * m + t
            block = ctx[t * BLOCK : (t + 1) * BLOCK]
            ctx_out.ref[j, 0] = block
            ctx_out.ref[j ^ 1, 1] = block
            ctx_out.push(j, 0)
            ctx_out.push(j ^ 1, 1)
    lse_out.push()


def backward_kernel(ins, outs, scratch, sems):
    core_ref, grad_ref, q_in, k_in, v_in, ctx_in, end_in, lse_in = ins
    dq_ref, keep_ref, send_ref = outs
    dk_s, dv_s = scratch
    core = core_ref[0]
    dk_s[...] = jnp.zeros(dk_s.shape, F32)
    dv_s[...] = jnp.zeros(dv_s.shape, F32)
    q_ref, k_s, v_s, ctx_ref = q_in.get(), k_in.get(), v_in.get(), ctx_in.get()
    end_ref, lse_ref = end_in.get(), lse_in.get()
    for m in range(4):
        rows = slice(2 * m, 2 * m + 2)
        q = q_ref[rows].reshape(TILE, HS)
        do = grad_ref[rows].reshape(TILE, HS)
        ctx = ctx_ref[rows].reshape(TILE, HS)
        delta = jnp.sum((do.astype(F32) * ctx.astype(F32)).T, axis=0, keepdims=True)
        end = end_ref[m]
        lse = lse_ref[m]
        dq = jnp.zeros((HS, TILE), F32)
        for start, stop in chunks_of(m):
            scores = masked_scores(k_s, q, end, m, start, stop)
            p = jnp.exp2(scores * SCALE2 - lse)
            dp = dot_nt(v_s[start:stop], do)
            ds = (p * (dp - delta) * SCALE).astype(BF16)
            dv_s[start:stop] += dot_nn(p.astype(BF16), do)
            dk_s[start:stop] += dot_nn(ds, q)
            dq = dq + dot_tn(k_s[start:stop], ds)
        dq_rows = dq.T.astype(BF16)
        dq_ref[2 * m] = dq_rows[:BLOCK]
        dq_ref[2 * m + 1] = dq_rows[BLOCK:]
    for j in range(CHIPS):
        own = pl.multiple_of(2 * BLOCK * j + BLOCK * core, BLOCK)
        other = pl.multiple_of(2 * BLOCK * j + BLOCK * (1 - core), BLOCK)
        send_ref[j, 0] = dk_s[pl.ds(other, BLOCK)].astype(BF16)
        send_ref[j, 1] = dv_s[pl.ds(other, BLOCK)].astype(BF16)
        keep_ref[j, 0] = dk_s[pl.ds(own, BLOCK)]
        keep_ref[j, 1] = dv_s[pl.ds(own, BLOCK)]


def project_kernel(ins, outs, scratch, sems):
    core_ref, valid_ref, up_in, mine_in, other_in = ins
    out = outs[0]
    core = core_ref[0]
    half = up_in.ref.shape[1] // 2
    valid = valid_ref[...]
    up_ref = up_in.get()
    up_mine = up_ref[:, pl.ds(pl.multiple_of(core * half, half), half)]
    up_other = up_ref[:, pl.ds(pl.multiple_of((1 - core) * half, half), half)]
    mine, other = mine_in.get(), other_in.get()
    for a in range(HEADS):
        rows = slice(a * HS, (a + 1) * HS)
        total = dot_nt(up_mine, mine[rows]) + dot_nt(up_other, other[rows])
        out.ref[a] = (total * valid).astype(BF16)
        out.push(a)


def attend_kernel(ins, outs, scratch, sems):
    core_ref, ctx_in, mine_in, other_in = ins
    out = outs[0]
    core = core_ref[0]
    ctx_ref = ctx_in.get()
    half = mine_in.ref.shape[1]
    ctx = jnp.concatenate([ctx_ref[a] for a in range(HEADS)], axis=1)
    step = half // 4
    for side, part in ((core, mine_in), (1 - core, other_in)):
        weight = part.get()
        for n in range(4):
            at = pl.ds(pl.multiple_of(side * half + n * step, step), step)
            cols = slice(n * step, (n + 1) * step)
            out.ref[0, :, at] = dot_nn(ctx, weight[:, cols]).astype(BF16)
            out.push(0, slice(None), at)


def weight_kernel(ins, outs, scratch, sems):
    out = outs[0]
    keep, pair, core, diag, ctx_ref, ctx_other_ref = [one.get() for one in ins]
    quarter = keep.shape[1]
    up = jnp.concatenate([keep[...], pair[...]], axis=0)
    up_other = jnp.concatenate([core[...], diag[...]], axis=0)
    for a in range(HEADS):
        total = dot_tn(ctx_ref[a].reshape(TILE, HS), up)
        total = total + dot_tn(ctx_other_ref[a].reshape(TILE, HS), up_other)
        part = pl.ds(4 * a, 4)
        out.ref[part] = total.reshape(4, HS // 4, quarter).astype(BF16)
        out.push(part)


def join_kernel(ins, outs, scratch, sems):
    dq_ref, keep_ref, came_ref, terms_ref = ins
    out_ref = outs[0]
    total = terms_ref[0].astype(F32)
    for s in range(1, terms_ref.shape[0]):
        total = total + terms_ref[s].astype(F32)
    weight = total.astype(BF16)
    rows = weight.shape[0]
    for j in range(CHIPS):
        for t in range(4):
            out_ref[j, 3, t * rows : (t + 1) * rows] = weight[:, t * HS : (t + 1) * HS]
    for j in range(CHIPS):
        out_ref[j, 0] = dq_ref[j]
        out_ref[j, 1] = (keep_ref[j, 0] + came_ref[j, 0].astype(F32)).astype(BF16)
        out_ref[j, 2] = (keep_ref[j, 1] + came_ref[j, 1].astype(F32)).astype(BF16)


def unpack_kernel(ins, outs, scratch, sems):
    core_ref, mine_ref, other_ref = ins
    dw_out = outs[3]
    core = core_ref[0]
    copies = []
    for a in range(HEADS):
        for i in range(3):
            dst = outs[i].at[0, :, pl.ds(a * HS, HS)]
            copies.append(pltpu.make_async_copy(mine_ref.at[a, i], dst, next(sems)))
            copies[-1].start()
    for p in range(4):
        rows = pl.ds(32 * p, 32)
        for h in range(2):
            a = 2 * p + h
            for t in range(4):
                part = slice(32 * t, 32 * t + 32)
                at = pl.multiple_of(1024 * h + 512 * core + HS * t, HS)
                dw_out.ref[rows, pl.ds(at, HS)] = mine_ref[a, 3, part].astype(F32)
                at = pl.multiple_of(1024 * h + 512 * (1 - core) + HS * t, HS)
                dw_out.ref[rows, pl.ds(at, HS)] = other_ref[a, part].astype(F32)
        dw_out.push(rows)
    return copies


def exchange(operand):
    return lax.all_to_all(
        operand, "ctx", split_axis=0, concat_axis=0, tiled=True, axis_index_groups=SAME_CORE
    )


def after(value, *others):
    return lax.optimization_barrier((value, *others))[0]


def shards(query_rows, key_rows, value_rows, session, lengths, out_weight, upstream):
    index = lax.axis_index("ctx").astype(jnp.int32)
    core = index & 1
    core_ref = core.reshape(1)
    high_ref = ((index >> 1) & 1).reshape(1)
    valid_len = lengths[0]
    width = out_weight.shape[1]
    half = width // 2
    quarter = half // 2

    part = ("R", (BLOCK, quarter), BF16)
    packed, own_half, up_keep, up_core, up_pair, up_diag = call(
        pack_kernel,
        [
            ("S", core_ref), ("S", high_ref), ("H", query_rows, 0), ("H", key_rows, 0),
            ("H", value_rows, 0), ("H", out_weight), ("H", upstream, 0),
        ],
        [("R", (HEADS, 3, BLOCK, HS), BF16), ("R", (HS, half), BF16), part, part, part, part],
    )
    own = exchange(packed)

    session_ids = session[0]
    positions = jnp.arange(LEN, dtype=jnp.int32).reshape(CHIPS, 2, BLOCK)
    own_sessions = lax.dynamic_index_in_dim(session_ids.reshape(CHIPS, 2, BLOCK), core, 1, False)
    own_positions = lax.dynamic_index_in_dim(positions, core, 1, False)
    end = jnp.sum(
        (session_ids[:, None] <= own_sessions.reshape(1, -1)).astype(jnp.int32), axis=0
    )
    end = jnp.minimum(end, valid_len).reshape(4, 1, TILE)
    valid = (own_positions < valid_len).astype(F32).reshape(4, 1, TILE)
    rows_here = index * BLOCK + jnp.arange(BLOCK, dtype=jnp.int32)
    valid_here = (rows_here < valid_len).astype(F32)[:, None]

    weight_mine = lax.all_gather(own_half, "fsdp", axis=0, tiled=True)

    own = after(own, end, valid, valid_here)
    other = lax.ppermute(own, "ctx", CORE_SWAP)
    pairs = 4 * TILE * SPAN * 5 // 2
    rows = ("H", (LEN, HS), BF16)
    context, lse, query, key, value = call(
        forward_kernel,
        [("S", core_ref), ("V", own), ("V", other), ("V", end), ("V", valid)],
        [
            ("H", (CHIPS, 2, BLOCK, HS), BF16),
            ("H", (4, 1, TILE), F32),
            ("H", (CHIPS, BLOCK, HS), BF16),
            rows,
            rows,
        ],
        scratch=(pltpu.VMEM((LEN, TILE), F32),),
        flops=4 * pairs * HS,
    )
    context_mine = exchange(context)
    up_pair = lax.ppermute(after(up_pair, context), "ctx", PAIR_SWAP)
    up_diag = lax.ppermute(after(up_diag, context), "ctx", DIAG_SWAP)
    up_core = lax.ppermute(after(up_core, context), "ctx", CORE_SWAP)
    context_mine = after(context_mine, up_pair, up_diag, up_core)
    context_other = lax.ppermute(context_mine, "ctx", CORE_SWAP)
    terms = call(
        weight_kernel,
        [
            ("H", up_keep), ("A", up_pair), ("A", up_core), ("A", up_diag),
            ("A", context_mine), ("A", context_other),
        ],
        [("H", (32, 32, quarter), BF16)],
        flops=2 * 512 * 1024 * 512,
    )
    weight_mine = after(weight_mine, terms)
    terms = lax.all_to_all(
        terms,
        ("ctx", "fsdp"),
        split_axis=0,
        concat_axis=0,
        tiled=True,
        axis_index_groups=REDUCE,
    )
    weight_other = lax.ppermute(weight_mine, "ctx", CORE_SWAP)
    grads = call(
        project_kernel,
        [
            ("S", core_ref), ("V", valid_here), ("H", upstream, 0), ("H", weight_mine),
            ("H", weight_other),
        ],
        [("H", (HEADS, BLOCK, HS), BF16)],
        flops=2 * 128 * 1024 * 2048,
    )
    grads = exchange(after(grads, terms))
    attended = call(
        attend_kernel,
        [
            ("S", core_ref), ("A", context_mine, (slice(None), 0)), ("H", weight_mine),
            ("H", weight_other),
        ],
        [("H", (1, BLOCK, width), BF16)],
        flops=2 * 128 * 1024 * 2048,
    )
    dq, keep, send = call(
        backward_kernel,
        [
            ("S", core_ref), ("V", after(grads, attended)), ("H", query), ("H", key), ("H", value),
            ("H", context, (slice(None), 0)), ("A", end), ("H", lse),
        ],
        [
            ("V", (CHIPS, BLOCK, HS), BF16),
            ("V", (CHIPS, 2, BLOCK, HS), F32),
            ("V", (CHIPS, 2, BLOCK, HS), BF16),
        ],
        scratch=(pltpu.VMEM((LEN, HS), F32), pltpu.VMEM((LEN, HS), F32)),
        flops=10 * pairs * HS,
    )
    came = lax.ppermute(send, "ctx", CORE_SWAP)
    joined = call(
        join_kernel,
        [("V", dq), ("V", keep), ("V", came), ("V", terms)],
        [("V", (CHIPS, 4, BLOCK, HS), BF16)],
    )
    result = exchange(joined)
    weight_part = lax.ppermute(result[:, 3], "ctx", CORE_SWAP)
    grad = ("R", (1, BLOCK, HEADS * HS), BF16)
    query_grad, key_grad, value_grad, weight_grad = call(
        unpack_kernel,
        [("S", core_ref), ("V", result), ("V", weight_part)],
        [grad, grad, grad, ("H", (HS, width), F32)],
    )
    return (attended, query_grad, key_grad, value_grad, weight_grad)


def solution(mesh):
    rows = P("fsdp", "ctx", None)
    return jax.shard_map(
        shards,
        mesh=mesh,
        in_specs=(rows, rows, rows, P("fsdp", None), P("fsdp"), P("fsdp", None), rows),
        out_specs=(rows, rows, rows, rows, P("fsdp", None)),
        check_vma=False,
    )
```

```python
import functools
import math

import jax
import jax.numpy as jnp
from jax import lax
from jax.experimental import pallas as pl
from jax.experimental.pallas import tpu as pltpu
from jax.sharding import PartitionSpec as P

HEADS = 8
HS = 128
BLOCK = 128
TILE = 256
SPAN = 512
REACH = 128
CHIPS = 8
LEN = 2048
NEG = -1e30
SEMS = 48
SCALE = 1.0 / math.sqrt(HS)
SCALE2 = SCALE * math.log2(math.e)
F32 = jnp.float32
BF16 = jnp.bfloat16

CORE_SWAP = [(i, i ^ 1) for i in range(16)]
PAIR_SWAP = [(i, i ^ 8) for i in range(16)]
DIAG_SWAP = [(i, i ^ 9) for i in range(16)]
SAME_CORE = [[2 * j + c for j in range(CHIPS)] for c in range(2)]
REDUCE = [
    [(8 * h + 2 * y + c) * 8 + f for f in range(8) for y in range(4)]
    for h in range(2)
    for c in range(2)
]


def dot_nt(a, b):
    return lax.dot_general(a, b, (((1,), (1,)), ((), ())), preferred_element_type=F32)


def dot_tn(a, b):
    return lax.dot_general(a, b, (((0,), (0,)), ((), ())), preferred_element_type=F32)


def dot_nn(a, b):
    return lax.dot_general(a, b, (((1,), (0,)), ((), ())), preferred_element_type=F32)


class Load:
    def __init__(self, copy, ref):
        self.copy, self.ref, self.done = copy, ref, False

    def get(self):
        if not self.done:
            self.copy.wait()
            self.done = True
        return self.ref


class Store:
    def __init__(self, hbm, ref, sems):
        self.hbm, self.ref, self.sems, self.copies = hbm, ref, sems, []

    def push(self, *index):
        src = self.ref.at[index] if index else self.ref
        dst = self.hbm.at[index] if index else self.hbm
        copy = pltpu.make_async_copy(src, dst, next(self.sems))
        copy.start()
        self.copies.append(copy)


SPACES = {"S": pltpu.SMEM, "V": pltpu.VMEM, "H": pltpu.HBM, "A": pl.ANY, "R": pltpu.HBM}


def call(kernel, ins, outs, scratch=(), flops=0, mib=14, aliases=None):
    copied = [
        pltpu.VMEM(jax.eval_shape(lambda x: x[i[2]] if len(i) > 2 else x, i[1]).shape, i[1].dtype)
        for i in ins
        if i[0] in "HA"
    ] + [pltpu.VMEM(o[1], o[2]) for o in outs if o[0] == "H"]

    def body(*refs):
        refs = list(refs)
        in_refs = [refs.pop(0) for _ in ins]
        out_refs = [refs.pop(0) for _ in outs]
        sem_ref = refs.pop(0)
        buffers = [refs.pop(0) for _ in copied]
        sems = (sem_ref.at[n] for n in range(SEMS))
        given, made = [], []
        for one, ref in zip(ins, in_refs):
            if one[0] in "HA":
                buffer = buffers.pop(0)
                copy = pltpu.make_async_copy(
                    ref.at[one[2]] if len(one) > 2 else ref, buffer, next(sems)
                )
                copy.start()
                ref = Load(copy, buffer)
            given.append(ref)
        for one, ref in zip(outs, out_refs):
            made.append(Store(ref, buffers.pop(0), sems) if one[0] == "H" else ref)
        more = kernel(given, made, refs, sems) or []
        for one in given:
            if isinstance(one, Load):
                one.get()
        for one in made:
            if isinstance(one, Store):
                for copy in one.copies:
                    copy.wait()
        for copy in more:
            copy.wait()

    result = pl.pallas_call(
        body,
        out_shape=[
            SPACES[o[0]](o[1], o[2]) if o[0] in "HR" else jax.ShapeDtypeStruct(o[1], o[2])
            for o in outs
        ],
        in_specs=[pl.BlockSpec(memory_space=SPACES[i[0]]) for i in ins],
        out_specs=[pl.BlockSpec(memory_space=SPACES[o[0]]) for o in outs],
        scratch_shapes=[pltpu.SemaphoreType.DMA((SEMS,)), *copied, *scratch],
        input_output_aliases=aliases or {},
        compiler_params=pltpu.CompilerParams(vmem_limit_bytes=mib * 1024 * 1024),
        cost_estimate=pl.CostEstimate(flops=flops, bytes_accessed=2_000_000, transcendentals=0),
    )(*[
        pltpu.with_memory_space_constraint(i[1], pltpu.HBM) if i[0] in "HR" else i[1] for i in ins
    ])
    return result[0] if len(outs) == 1 else result


def pack_kernel(ins, outs, scratch, sems):
    core_ref, high_ref, *data = ins
    out_ref, half_ref, up_mine_ref, up_send_ref, pair_ref, diag_ref = outs
    core, high = core_ref[0], high_ref[0]
    half = half_ref.shape[1]
    quarter = half // 2
    copies = []

    def copy(src, dst):
        copies.append(pltpu.make_async_copy(src, dst, next(sems)))
        copies[-1].start()

    mine = pl.ds(pl.multiple_of(core * half, half), half)
    other = pl.ds(pl.multiple_of((1 - core) * half, half), half)
    copy(data[3].get().at[:, mine], half_ref)
    for i in range(3):
        ref = data[i].get()
        for a in range(HEADS):
            copy(ref.at[:, pl.ds(a * HS, HS)], out_ref.at[a, i])
    up_ref = data[4].get()
    copy(up_ref.at[:, mine], up_mine_ref)
    copy(up_ref.at[:, other], up_send_ref)
    for ref, c in ((pair_ref, core), (diag_ref, 1 - core)):
        at = pl.multiple_of(c * half + (1 - high) * quarter, quarter)
        copy(up_ref.at[:, pl.ds(at, quarter)], ref)
    return copies


def in_order(core, own_ref, other_ref, slot, dst_ref):
    for j in range(CHIPS):
        own = pl.multiple_of(2 * BLOCK * j + BLOCK * core, BLOCK)
        other = pl.multiple_of(2 * BLOCK * j + BLOCK * (1 - core), BLOCK)
        dst_ref[pl.ds(own, BLOCK)] = own_ref[j, slot]
        dst_ref[pl.ds(other, BLOCK)] = other_ref[j, slot]


def chunks_of(m):
    stop = min(SPAN * (m + 1) + REACH, LEN)
    return [(start, min(start + SPAN, stop)) for start in range(0, stop, SPAN)]


def masked_scores(k_s, q, end, m, start, stop):
    scores = dot_nt(k_s[start:stop], q)
    if stop > SPAN * m:
        at = lax.broadcasted_iota(jnp.int32, scores.shape, 0) + start
        scores = jnp.where(at < end, scores, NEG)
    return scores


def forward_kernel(ins, outs, scratch, sems):
    core_ref, own_ref, other_ref, end_ref, valid_ref = ins
    ctx_out, lse_out, q_out, k_out, v_out = outs
    (s_s,) = scratch
    core = core_ref[0]
    k_s, v_s = k_out.ref, v_out.ref
    in_order(core, own_ref, other_ref, 1, k_s)
    k_out.push()
    in_order(core, own_ref, other_ref, 2, v_s)
    v_out.push()
    q_out.ref[...] = own_ref[:, 0]
    q_out.push()
    for m in range(4):
        q = own_ref[2 * m : 2 * m + 2, 0].reshape(TILE, HS)
        end = end_ref[m]
        top = jnp.full((1, TILE), NEG, F32)
        for start, stop in chunks_of(m):
            scores = masked_scores(k_s, q, end, m, start, stop)
            s_s[start:stop] = scores
            top = jnp.maximum(top, jnp.max(scores, axis=0, keepdims=True))
        top2 = top * SCALE2
        total = jnp.zeros((1, TILE), F32)
        acc = jnp.zeros((HS, TILE), F32)
        for start, stop in chunks_of(m):
            p = jnp.exp2(s_s[start:stop] * SCALE2 - top2)
            total = total + jnp.sum(p, axis=0, keepdims=True)
            acc = acc + dot_tn(v_s[start:stop], p.astype(BF16))
        lse_out.ref[m] = top2 + jnp.log2(total)
        ctx = (acc * (valid_ref[m] / total)).T.astype(BF16)
        for t in range(2):
            j = 2 * m + t
            block = ctx[t * BLOCK : (t + 1) * BLOCK]
            ctx_out.ref[j, 0] = block
            ctx_out.ref[j ^ 4, 1] = block
            ctx_out.push(j, 0)
            ctx_out.push(j ^ 4, 1)
    lse_out.push()


def backward_kernel(ins, outs, scratch, sems):
    core_ref, q_in, k_in, grad_in, v_in, ctx_in, end_in, lse_in = ins
    dq_out, keep_out, send_out = outs
    dk_s, dv_s = scratch
    core = core_ref[0]
    dk_s[...] = jnp.zeros(dk_s.shape, F32)
    dv_s[...] = jnp.zeros(dv_s.shape, F32)
    end_ref, lse_ref = end_in.get(), lse_in.get()
    q_ref, k_s = q_in.get(), k_in.get()
    grad_ref, v_s, ctx_ref = grad_in.get(), v_in.get(), ctx_in.get()
    for m in range(3, -1, -1):
        rows = slice(2 * m, 2 * m + 2)
        q = q_ref[rows].reshape(TILE, HS)
        do = grad_ref[rows].reshape(TILE, HS)
        ctx = ctx_ref[rows].reshape(TILE, HS)
        delta = jnp.sum((do.astype(F32) * ctx.astype(F32)).T, axis=0, keepdims=True)
        end = end_ref[m]
        lse = lse_ref[m]
        dq = jnp.zeros((HS, TILE), F32)
        for start, stop in chunks_of(m):
            scores = masked_scores(k_s, q, end, m, start, stop)
            p = jnp.exp2(scores * SCALE2 - lse)
            dp = dot_nt(v_s[start:stop], do)
            ds = (p * (dp - delta) * SCALE).astype(BF16)
            dv_s[start:stop] += dot_nn(p.astype(BF16), do)
            dk_s[start:stop] += dot_nn(ds, q)
            dq = dq + dot_tn(k_s[start:stop], ds)
        dq_rows = dq.T.astype(BF16)
        dq_out.ref[2 * m] = dq_rows[:BLOCK]
        dq_out.ref[2 * m + 1] = dq_rows[BLOCK:]
        dq_out.push(pl.ds(2 * m, 2))
        first = 2 * m + 1 if m else 0
        last = 2 * m + 3 if m < 3 else CHIPS
        for j in range(first, last):
            own = pl.multiple_of(2 * BLOCK * j + BLOCK * core, BLOCK)
            other = pl.multiple_of(2 * BLOCK * j + BLOCK * (1 - core), BLOCK)
            send_out.ref[j, 0] = dk_s[pl.ds(other, BLOCK)].astype(BF16)
            send_out.ref[j, 1] = dv_s[pl.ds(other, BLOCK)].astype(BF16)
            send_out.push(j)
            keep_out.ref[j, 0] = dk_s[pl.ds(own, BLOCK)]
            keep_out.ref[j, 1] = dv_s[pl.ds(own, BLOCK)]
            keep_out.push(j)


def project_kernel(ins, outs, scratch, sems):
    row_ref, up_in, up_other_in, *pieces = ins
    keep_ref, send_ref = outs
    row = row_ref[0]
    up = jnp.concatenate([up_in.get()[...], up_other_in.get()[...]], axis=0)
    for s in range(HEADS):
        total = dot_nt(up, pieces[s][...])
        at = jnp.bitwise_xor(row, s)
        keep_ref[at] = total[:BLOCK]
        send_ref[at] = total[BLOCK:].astype(BF16)


def add_kernel(ins, outs, scratch, sems):
    valid_ref, keep_ref, came_ref = ins
    outs[0][...] = ((keep_ref[...] + came_ref[...].astype(F32)) * valid_ref[...]).astype(BF16)


def attend_kernel(ins, outs, scratch, sems):
    row_ref, ctx_in, ctx_other_in, *pieces = ins
    keep, send = outs
    row = row_ref[0]
    order = [jnp.bitwise_xor(row, s) for s in range(HEADS)]
    ctx_ref, ctx_other_ref = ctx_in.get(), ctx_other_in.get()
    ctx = jnp.concatenate(
        [
            jnp.concatenate([ctx_ref[a] for a in order], axis=1),
            jnp.concatenate([ctx_other_ref[a] for a in order], axis=1),
        ],
        axis=0,
    )
    pieces = [piece.get() for piece in pieces]
    for n in range(4):
        cols = slice(n * TILE, (n + 1) * TILE)
        weight = jnp.concatenate([piece[:, cols] for piece in pieces], axis=0)
        total = dot_nn(ctx, weight).astype(BF16)
        keep.ref[:, cols] = total[:BLOCK]
        send.ref[:, cols] = total[BLOCK:]
    send.push()
    keep.push()


def place_kernel(ins, outs, scratch, sems):
    core_ref, keep_in, came_in = ins
    core = core_ref[0]
    half = keep_in.ref.shape[1]
    copies = []
    for one, c in ((keep_in, core), (came_in, 1 - core)):
        at = pl.ds(pl.multiple_of(c * half, half), half)
        copies.append(pltpu.make_async_copy(one.get(), outs[0].at[0, :, at], next(sems)))
        copies[-1].start()
    return copies


def weight_kernel(ins, outs, scratch, sems):
    out = outs[0]
    high_ref = ins[0]
    mine, other, pair, diag, ctx_ref, ctx_other_ref = [one.get() for one in ins[1:]]
    quarter = pair.shape[1]
    at = pl.ds(pl.multiple_of(high_ref[0] * quarter, quarter), quarter)
    up = jnp.concatenate([mine[:, at], pair[...]], axis=0)
    up_other = jnp.concatenate([other[:, at], diag[...]], axis=0)
    for a in range(HEADS):
        total = dot_tn(ctx_ref[a].reshape(TILE, HS), up)
        total = total + dot_tn(ctx_other_ref[a].reshape(TILE, HS), up_other)
        part = pl.ds(4 * a, 4)
        out.ref[part] = total.reshape(4, HS // 4, quarter).astype(BF16)
        out.push(part)


def join_kernel(ins, outs, scratch, sems):
    dq_in, keep_in, came_in = ins
    (made,) = scratch
    copies = []
    dq_ref, keep_ref, came_ref = dq_in.get(), keep_in.get(), came_in.get()
    for j in range(CHIPS):
        made[j, 0] = dq_ref[j]
        made[j, 1] = (keep_ref[j, 0] + came_ref[j, 0].astype(F32)).astype(BF16)
        made[j, 2] = (keep_ref[j, 1] + came_ref[j, 1].astype(F32)).astype(BF16)
        copies.append(
            pltpu.make_async_copy(made.at[j], outs[0].at[j, pl.ds(0, 3)], next(sems))
        )
        copies[-1].start()
    return copies


def total_kernel(ins, outs, scratch, sems):
    terms_ref = ins[1]
    (made,) = scratch
    total = terms_ref[0].astype(F32)
    for s in range(1, terms_ref.shape[0]):
        total = total + terms_ref[s].astype(F32)
    weight = total.astype(BF16)
    rows = weight.shape[0]
    for t in range(4):
        made[t * rows : (t + 1) * rows] = weight[:, t * HS : (t + 1) * HS]
    copies = []
    for j in range(CHIPS):
        copies.append(pltpu.make_async_copy(made, outs[0].at[j, 3], next(sems)))
        copies[-1].start()
    return copies


def unpack_kernel(ins, outs, scratch, sems):
    mine_ref = ins[0]
    copies = []
    for a in range(HEADS):
        for i in range(3):
            dst = outs[i].at[0, :, pl.ds(a * HS, HS)]
            copies.append(pltpu.make_async_copy(mine_ref.at[a, i], dst, next(sems)))
            copies[-1].start()
    return copies


def widen_kernel(ins, outs, scratch, sems):
    core_ref, mine_ref, other_ref = ins
    out = outs[0]
    core = core_ref[0]
    for y in range(4):
        rows = pl.ds(32 * y, 32)
        for x in range(2):
            a = 4 * x + y
            for t in range(4):
                part = slice(32 * t, 32 * t + 32)
                at = pl.multiple_of(1024 * core + 512 * x + HS * t, HS)
                out.ref[rows, pl.ds(at, HS)] = mine_ref[a, part].astype(F32)
                at = pl.multiple_of(1024 * (1 - core) + 512 * x + HS * t, HS)
                out.ref[rows, pl.ds(at, HS)] = other_ref[a, part].astype(F32)
        out.push(rows)


def exchange(operand):
    return lax.all_to_all(
        operand, "ctx", split_axis=0, concat_axis=0, tiled=True, axis_index_groups=SAME_CORE
    )


def after(value, *others):
    return lax.optimization_barrier((value, *others))[0]


def shards(query_rows, key_rows, value_rows, session, lengths, out_weight, upstream):
    index = lax.axis_index("ctx").astype(jnp.int32)
    core = index & 1
    core_ref = core.reshape(1)
    high_ref = (index >> 3).reshape(1)
    row_ref = lax.axis_index("fsdp").astype(jnp.int32).reshape(1)
    valid_len = lengths[0]
    width = out_weight.shape[1]
    half = width // 2
    quarter = half // 2

    side = ("R", (BLOCK, half), BF16)
    part = ("R", (BLOCK, quarter), BF16)
    packed, own_half, up_mine, up_send, up_pair, up_diag = call(
        pack_kernel,
        [
            ("S", core_ref), ("S", high_ref), ("H", query_rows, 0), ("H", key_rows, 0),
            ("H", value_rows, 0), ("H", out_weight), ("H", upstream, 0),
        ],
        [("R", (HEADS, 3, BLOCK, HS), BF16), ("R", (HS, half), BF16), side, side, part, part],
    )
    own = exchange(packed)

    session_ids = session[0]
    positions = jnp.arange(LEN, dtype=jnp.int32).reshape(CHIPS, 2, BLOCK)
    own_sessions = lax.dynamic_index_in_dim(session_ids.reshape(CHIPS, 2, BLOCK), core, 1, False)
    own_positions = lax.dynamic_index_in_dim(positions, core, 1, False)
    end = jnp.sum(
        (session_ids[:, None] <= own_sessions.reshape(1, -1)).astype(jnp.int32), axis=0
    )
    end = jnp.minimum(end, valid_len).reshape(4, 1, TILE)
    valid = (own_positions < valid_len).astype(F32).reshape(4, 1, TILE)
    rows_here = index * BLOCK + jnp.arange(BLOCK, dtype=jnp.int32)
    valid_here = (rows_here < valid_len).astype(F32)[:, None]

    def step(value, s):
        return lax.ppermute(value, "fsdp", [(i, i ^ s) for i in range(8)])

    over = step(own_half, 4)
    one, three = step(own_half, 1), step(own_half, 3)
    over_one, over_three = step(over, 1), step(over, 3)
    two, over_two = step(one, 3), step(over_three, 1)
    pieces = [own_half, one, two, three, over, over_one, over_two, over_three]
    up_other = lax.ppermute(up_send, "ctx", CORE_SWAP)

    own = after(own, end, valid, valid_here, one, three, over_one, over_three, up_other)
    other = lax.ppermute(own, "ctx", CORE_SWAP)
    pairs = 4 * TILE * SPAN * 5 // 2
    rows = ("H", (LEN, HS), BF16)
    context, lse, query, key, value = call(
        forward_kernel,
        [("S", core_ref), ("V", own), ("V", other), ("V", end), ("V", valid)],
        [
            ("H", (CHIPS, 2, BLOCK, HS), BF16),
            ("H", (4, 1, TILE), F32),
            ("H", (CHIPS, BLOCK, HS), BF16),
            rows,
            rows,
        ],
        scratch=(pltpu.VMEM((LEN, TILE), F32),),
        flops=4 * pairs * HS,
    )
    context_mine = exchange(context)
    up_pair = lax.ppermute(after(up_pair, context), "ctx", PAIR_SWAP)
    up_diag = lax.ppermute(after(up_diag, context), "ctx", DIAG_SWAP)
    context_other = lax.ppermute(after(context_mine, up_pair, up_diag), "ctx", CORE_SWAP)
    grads_keep, grads_send = call(
        project_kernel,
        [("S", row_ref), ("A", up_mine), ("A", up_other), *[("V", piece) for piece in pieces]],
        [("V", (HEADS, BLOCK, HS), F32), ("V", (HEADS, BLOCK, HS), BF16)],
        flops=2 * 256 * 1024 * 1024,
    )
    grads_came = lax.ppermute(grads_send, "ctx", CORE_SWAP)
    terms = call(
        weight_kernel,
        [
            ("S", high_ref), ("A", up_mine), ("A", up_other), ("A", up_pair), ("A", up_diag),
            ("A", context_mine), ("A", context_other),
        ],
        [("H", (32, 32, quarter), BF16)],
        flops=2 * 512 * 1024 * 512,
    )
    grads = call(
        add_kernel,
        [("V", valid_here), ("V", grads_keep), ("V", grads_came)],
        [("V", (HEADS, BLOCK, HS), BF16)],
    )
    grads = exchange(after(grads, context_mine, up_pair, up_diag))
    terms = lax.all_to_all(
        after(terms, grads),
        ("ctx", "fsdp"),
        split_axis=0,
        concat_axis=0,
        tiled=True,
        axis_index_groups=REDUCE,
    )
    dq, keep, send = call(
        backward_kernel,
        [
            ("S", core_ref), ("H", query), ("H", key), ("H", grads), ("H", value),
            ("H", context, (slice(None), 0)), ("A", end), ("H", lse),
        ],
        [
            ("H", (CHIPS, BLOCK, HS), BF16),
            ("H", (CHIPS, 2, BLOCK, HS), F32),
            ("H", (CHIPS, 2, BLOCK, HS), BF16),
        ],
        scratch=(pltpu.VMEM((LEN, HS), F32), pltpu.VMEM((LEN, HS), F32)),
        flops=10 * pairs * HS,
    )
    came = lax.ppermute(send, "ctx", CORE_SWAP)
    side = ("H", (BLOCK, half), BF16)
    attended_keep, attended_send = call(
        attend_kernel,
        [
            ("S", row_ref), ("A", after(context_mine, grads), (slice(None), 0)),
            ("A", context_other, (slice(None), 0)), *[("A", piece) for piece in pieces],
        ],
        [side, side],
        flops=2 * 256 * 1024 * 1024,
    )
    attended_came = lax.ppermute(attended_send, "ctx", CORE_SWAP)
    attended = call(
        place_kernel,
        [("S", core_ref), ("A", attended_keep), ("A", attended_came)],
        [("R", (1, BLOCK, width), BF16)],
    )
    joined = call(
        join_kernel,
        [("A", dq), ("A", keep), ("A", came)],
        [("R", (CHIPS, 4, BLOCK, HS), BF16)],
        scratch=(pltpu.VMEM((CHIPS, 3, BLOCK, HS), BF16),),
    )
    joined = call(
        total_kernel,
        [("R", after(joined, attended)), ("V", terms)],
        [("R", (CHIPS, 4, BLOCK, HS), BF16)],
        scratch=(pltpu.VMEM((BLOCK, HS), BF16),),
        aliases={0: 0},
    )
    result = exchange(joined)
    weight_mine = result[:, 3]
    weight_other = lax.ppermute(weight_mine, "ctx", CORE_SWAP)
    grad = ("R", (1, BLOCK, HEADS * HS), BF16)
    query_grad, key_grad, value_grad = call(unpack_kernel, [("V", result)], [grad, grad, grad])
    weight_grad = call(
        widen_kernel,
        [("S", core_ref), ("V", weight_mine), ("V", weight_other)],
        [("H", (HS, width), F32)],
    )
    return (attended, query_grad, key_grad, value_grad, weight_grad)


def solution(mesh):
    rows = P("fsdp", "ctx", None)
    return jax.shard_map(
        shards,
        mesh=mesh,
        in_specs=(rows, rows, rows, P("fsdp", None), P("fsdp"), P("fsdp", None), rows),
        out_specs=(rows, rows, rows, rows, P("fsdp", None)),
        check_vma=False,
    )
```

```python
import functools
import math

import jax
import jax.numpy as jnp
from jax import lax
from jax.experimental import pallas as pl
from jax.experimental.pallas import tpu as pltpu
from jax.sharding import PartitionSpec as P

HEADS = 8
HS = 128
BLOCK = 128
TILE = 256
SPAN = 512
REACH = 128
CHIPS = 8
LEN = 2048
NEG = -1e30
SEMS = 48
SCALE = 1.0 / math.sqrt(HS)
SCALE2 = SCALE * math.log2(math.e)
F32 = jnp.float32
BF16 = jnp.bfloat16

CORE_SWAP = [(i, i ^ 1) for i in range(16)]
PAIR_SWAP = [(i, i ^ 8) for i in range(16)]
DIAG_SWAP = [(i, i ^ 9) for i in range(16)]
SAME_CORE = [[2 * j + c for j in range(CHIPS)] for c in range(2)]
REDUCE = [
    [(8 * h + 2 * y + c) * 8 + f for f in range(8) for y in range(4)]
    for h in range(2)
    for c in range(2)
]


def dot_nt(a, b):
    return lax.dot_general(a, b, (((1,), (1,)), ((), ())), preferred_element_type=F32)


def dot_tn(a, b):
    return lax.dot_general(a, b, (((0,), (0,)), ((), ())), preferred_element_type=F32)


def dot_nn(a, b):
    return lax.dot_general(a, b, (((1,), (0,)), ((), ())), preferred_element_type=F32)


class Load:
    def __init__(self, copy, ref):
        self.copy, self.ref, self.done = copy, ref, False

    def get(self):
        if not self.done:
            self.copy.wait()
            self.done = True
        return self.ref


class Store:
    def __init__(self, hbm, ref, sems):
        self.hbm, self.ref, self.sems, self.copies = hbm, ref, sems, []

    def push(self, *index):
        src = self.ref.at[index] if index else self.ref
        dst = self.hbm.at[index] if index else self.hbm
        copy = pltpu.make_async_copy(src, dst, next(self.sems))
        copy.start()
        self.copies.append(copy)


SPACES = {"S": pltpu.SMEM, "V": pltpu.VMEM, "H": pltpu.HBM, "A": pl.ANY, "R": pltpu.HBM}


def call(kernel, ins, outs, scratch=(), flops=0, mib=14, aliases=None):
    copied = [
        pltpu.VMEM(jax.eval_shape(lambda x: x[i[2]] if len(i) > 2 else x, i[1]).shape, i[1].dtype)
        for i in ins
        if i[0] in "HA"
    ] + [pltpu.VMEM(o[1], o[2]) for o in outs if o[0] == "H"]

    def body(*refs):
        refs = list(refs)
        in_refs = [refs.pop(0) for _ in ins]
        out_refs = [refs.pop(0) for _ in outs]
        sem_ref = refs.pop(0)
        buffers = [refs.pop(0) for _ in copied]
        sems = (sem_ref.at[n] for n in range(SEMS))
        given, made = [], []
        for one, ref in zip(ins, in_refs):
            if one[0] in "HA":
                buffer = buffers.pop(0)
                copy = pltpu.make_async_copy(
                    ref.at[one[2]] if len(one) > 2 else ref, buffer, next(sems)
                )
                copy.start()
                ref = Load(copy, buffer)
            given.append(ref)
        for one, ref in zip(outs, out_refs):
            made.append(Store(ref, buffers.pop(0), sems) if one[0] == "H" else ref)
        more = kernel(given, made, refs, sems) or []
        for one in given:
            if isinstance(one, Load):
                one.get()
        for one in made:
            if isinstance(one, Store):
                for copy in one.copies:
                    copy.wait()
        for copy in more:
            copy.wait()

    result = pl.pallas_call(
        body,
        out_shape=[
            SPACES[o[0]](o[1], o[2]) if o[0] in "HR" else jax.ShapeDtypeStruct(o[1], o[2])
            for o in outs
        ],
        in_specs=[pl.BlockSpec(memory_space=SPACES[i[0]]) for i in ins],
        out_specs=[pl.BlockSpec(memory_space=SPACES[o[0]]) for o in outs],
        scratch_shapes=[pltpu.SemaphoreType.DMA((SEMS,)), *copied, *scratch],
        input_output_aliases=aliases or {},
        compiler_params=pltpu.CompilerParams(vmem_limit_bytes=mib * 1024 * 1024),
        cost_estimate=pl.CostEstimate(flops=flops, bytes_accessed=2_000_000, transcendentals=0),
    )(*[
        pltpu.with_memory_space_constraint(i[1], pltpu.HBM) if i[0] in "HR" else i[1] for i in ins
    ])
    return result[0] if len(outs) == 1 else result


def pack_kernel(ins, outs, scratch, sems):
    core_ref, high_ref, *data = ins
    out_ref, half_ref, up_mine_ref, up_send_ref, pair_ref, diag_ref = outs
    core, high = core_ref[0], high_ref[0]
    half = half_ref.shape[1]
    quarter = half // 2
    copies = []

    def copy(src, dst):
        copies.append(pltpu.make_async_copy(src, dst, next(sems)))
        copies[-1].start()

    mine = pl.ds(pl.multiple_of(core * half, half), half)
    other = pl.ds(pl.multiple_of((1 - core) * half, half), half)
    copy(data[3].get().at[:, mine], half_ref)
    for i in range(3):
        ref = data[i].get()
        for a in range(HEADS):
            copy(ref.at[:, pl.ds(a * HS, HS)], out_ref.at[a, i])
    up_ref = data[4].get()
    copy(up_ref.at[:, mine], up_mine_ref)
    copy(up_ref.at[:, other], up_send_ref)
    for ref, c in ((pair_ref, core), (diag_ref, 1 - core)):
        at = pl.multiple_of(c * half + (1 - high) * quarter, quarter)
        copy(up_ref.at[:, pl.ds(at, quarter)], ref)
    return copies


def in_order(core, own_ref, other_ref, slot, dst_ref):
    for j in range(CHIPS):
        own = pl.multiple_of(2 * BLOCK * j + BLOCK * core, BLOCK)
        other = pl.multiple_of(2 * BLOCK * j + BLOCK * (1 - core), BLOCK)
        dst_ref[pl.ds(own, BLOCK)] = own_ref[j, slot]
        dst_ref[pl.ds(other, BLOCK)] = other_ref[j, slot]


def chunks_of(m):
    stop = min(SPAN * (m + 1) + REACH, LEN)
    return [(start, min(start + SPAN, stop)) for start in range(0, stop, SPAN)]


def masked_scores(k_s, q, end, m, start, stop):
    scores = dot_nt(k_s[start:stop], q)
    if stop > SPAN * m:
        at = lax.broadcasted_iota(jnp.int32, scores.shape, 0) + start
        scores = jnp.where(at < end, scores, NEG)
    return scores


def forward_kernel(ins, outs, scratch, sems):
    core_ref, own_ref, other_ref, end_ref, valid_ref = ins
    ctx_out, lse_out, q_out, k_out, v_out = outs
    (s_s,) = scratch
    core = core_ref[0]
    k_s, v_s = k_out.ref, v_out.ref
    in_order(core, own_ref, other_ref, 1, k_s)
    k_out.push()
    in_order(core, own_ref, other_ref, 2, v_s)
    v_out.push()
    q_out.ref[...] = own_ref[:, 0]
    q_out.push()
    for m in range(4):
        q = own_ref[2 * m : 2 * m + 2, 0].reshape(TILE, HS)
        end = end_ref[m]
        top = jnp.full((1, TILE), NEG, F32)
        for start, stop in chunks_of(m):
            scores = masked_scores(k_s, q, end, m, start, stop)
            s_s[start:stop] = scores
            top = jnp.maximum(top, jnp.max(scores, axis=0, keepdims=True))
        top2 = top * SCALE2
        total = jnp.zeros((1, TILE), F32)
        acc = jnp.zeros((HS, TILE), F32)
        for start, stop in chunks_of(m):
            p = jnp.exp2(s_s[start:stop] * SCALE2 - top2)
            total = total + jnp.sum(p, axis=0, keepdims=True)
            acc = acc + dot_tn(v_s[start:stop], p.astype(BF16))
        lse_out.ref[m] = top2 + jnp.log2(total)
        ctx = (acc * (valid_ref[m] / total)).T.astype(BF16)
        for t in range(2):
            j = 2 * m + t
            block = ctx[t * BLOCK : (t + 1) * BLOCK]
            ctx_out.ref[j, 0] = block
            ctx_out.ref[j ^ 4, 1] = block
            ctx_out.push(j, 0)
            ctx_out.push(j ^ 4, 1)
    lse_out.push()


def backward_kernel(ins, outs, scratch, sems):
    core_ref, q_in, k_in, grad_in, v_in, ctx_in, end_in, lse_in = ins
    dq_out, keep_out, send_out = outs
    dk_s, dv_s = scratch
    core = core_ref[0]
    dk_s[...] = jnp.zeros(dk_s.shape, F32)
    dv_s[...] = jnp.zeros(dv_s.shape, F32)
    end_ref, lse_ref = end_in.get(), lse_in.get()
    q_ref, k_s = q_in.get(), k_in.get()
    grad_ref, v_s, ctx_ref = grad_in.get(), v_in.get(), ctx_in.get()
    for m in range(3, -1, -1):
        rows = slice(2 * m, 2 * m + 2)
        q = q_ref[rows].reshape(TILE, HS)
        do = grad_ref[rows].reshape(TILE, HS)
        ctx = ctx_ref[rows].reshape(TILE, HS)
        delta = jnp.sum((do.astype(F32) * ctx.astype(F32)).T, axis=0, keepdims=True)
        end = end_ref[m]
        lse = lse_ref[m]
        dq = jnp.zeros((HS, TILE), F32)
        for start, stop in chunks_of(m):
            scores = masked_scores(k_s, q, end, m, start, stop)
            p = jnp.exp2(scores * SCALE2 - lse)
            dp = dot_nt(v_s[start:stop], do)
            ds = (p * (dp - delta) * SCALE).astype(BF16)
            dv_s[start:stop] += dot_nn(p.astype(BF16), do)
            dk_s[start:stop] += dot_nn(ds, q)
            dq = dq + dot_tn(k_s[start:stop], ds)
        dq_rows = dq.T.astype(BF16)
        dq_out.ref[2 * m] = dq_rows[:BLOCK]
        dq_out.ref[2 * m + 1] = dq_rows[BLOCK:]
        dq_out.push(pl.ds(2 * m, 2))
        first = 2 * m + 1 if m else 0
        last = 2 * m + 3 if m < 3 else CHIPS
        for j in range(first, last):
            own = pl.multiple_of(2 * BLOCK * j + BLOCK * core, BLOCK)
            other = pl.multiple_of(2 * BLOCK * j + BLOCK * (1 - core), BLOCK)
            send_out.ref[j, 0] = dk_s[pl.ds(other, BLOCK)].astype(BF16)
            send_out.ref[j, 1] = dv_s[pl.ds(other, BLOCK)].astype(BF16)
            send_out.push(j)
            keep_out.ref[j, 0] = dk_s[pl.ds(own, BLOCK)]
            keep_out.ref[j, 1] = dv_s[pl.ds(own, BLOCK)]
            keep_out.push(j)


def project_kernel(ins, outs, scratch, sems):
    row_ref, up_in, up_other_in, *pieces = ins
    keep_ref, send_ref = outs
    row = row_ref[0]
    up = jnp.concatenate([up_in.get()[...], up_other_in.get()[...]], axis=0)
    for s in range(HEADS):
        total = dot_nt(up, pieces[s][...])
        at = jnp.bitwise_xor(row, s)
        keep_ref[at] = total[:BLOCK]
        send_ref[at] = total[BLOCK:].astype(BF16)


def add_kernel(ins, outs, scratch, sems):
    valid_ref, keep_ref, came_ref = ins
    outs[0][...] = ((keep_ref[...] + came_ref[...].astype(F32)) * valid_ref[...]).astype(BF16)


def attend_kernel(ins, outs, scratch, sems):
    row_ref, ctx_in, ctx_other_in, *pieces = ins
    keep, send = outs
    row = row_ref[0]
    order = [jnp.bitwise_xor(row, s) for s in range(HEADS)]
    ctx_ref, ctx_other_ref = ctx_in.get(), ctx_other_in.get()
    ctx = jnp.concatenate(
        [
            jnp.concatenate([ctx_ref[a] for a in order], axis=1),
            jnp.concatenate([ctx_other_ref[a] for a in order], axis=1),
        ],
        axis=0,
    )
    pieces = [piece.get() for piece in pieces]
    for n in range(4):
        cols = slice(n * TILE, (n + 1) * TILE)
        weight = jnp.concatenate([piece[:, cols] for piece in pieces], axis=0)
        total = dot_nn(ctx, weight).astype(BF16)
        keep.ref[:, cols] = total[:BLOCK]
        send.ref[:, cols] = total[BLOCK:]
    send.push()
    keep.push()


def place_kernel(ins, outs, scratch, sems):
    core_ref, keep_in, came_in = ins
    core = core_ref[0]
    half = keep_in.ref.shape[1]
    copies = []
    for one, c in ((keep_in, core), (came_in, 1 - core)):
        at = pl.ds(pl.multiple_of(c * half, half), half)
        copies.append(pltpu.make_async_copy(one.get(), outs[0].at[0, :, at], next(sems)))
        copies[-1].start()
    return copies


def weight_kernel(ins, outs, scratch, sems):
    out = outs[0]
    high_ref = ins[0]
    mine, other, pair, diag, ctx_ref, ctx_other_ref = [one.get() for one in ins[1:]]
    quarter = pair.shape[1]
    at = pl.ds(pl.multiple_of(high_ref[0] * quarter, quarter), quarter)
    up = jnp.concatenate([mine[:, at], pair[...]], axis=0)
    up_other = jnp.concatenate([other[:, at], diag[...]], axis=0)
    for a in range(HEADS):
        total = dot_tn(ctx_ref[a].reshape(TILE, HS), up)
        total = total + dot_tn(ctx_other_ref[a].reshape(TILE, HS), up_other)
        part = pl.ds(4 * a, 4)
        out.ref[part] = total.reshape(4, HS // 4, quarter).astype(BF16)
        out.push(part)


def join_kernel(ins, outs, scratch, sems):
    dq_in, keep_in, came_in = ins
    (made,) = scratch
    copies = []
    dq_ref, keep_ref, came_ref = dq_in.get(), keep_in.get(), came_in.get()
    for j in range(CHIPS):
        made[j, 0] = dq_ref[j]
        made[j, 1] = (keep_ref[j, 0] + came_ref[j, 0].astype(F32)).astype(BF16)
        made[j, 2] = (keep_ref[j, 1] + came_ref[j, 1].astype(F32)).astype(BF16)
        copies.append(
            pltpu.make_async_copy(made.at[j], outs[0].at[j, pl.ds(0, 3)], next(sems))
        )
        copies[-1].start()
    return copies


def total_kernel(ins, outs, scratch, sems):
    terms_ref = ins[1]
    (made,) = scratch
    total = terms_ref[0].astype(F32)
    for s in range(1, terms_ref.shape[0]):
        total = total + terms_ref[s].astype(F32)
    weight = total.astype(BF16)
    rows = weight.shape[0]
    for t in range(4):
        made[t * rows : (t + 1) * rows] = weight[:, t * HS : (t + 1) * HS]
    copies = []
    for j in range(CHIPS):
        copies.append(pltpu.make_async_copy(made, outs[0].at[j, 3], next(sems)))
        copies[-1].start()
    return copies


def unpack_kernel(ins, outs, scratch, sems):
    mine_ref = ins[0]
    copies = []
    for a in range(HEADS):
        for i in range(3):
            dst = outs[i].at[0, :, pl.ds(a * HS, HS)]
            copies.append(pltpu.make_async_copy(mine_ref.at[a, i], dst, next(sems)))
            copies[-1].start()
    return copies


def widen_kernel(ins, outs, scratch, sems):
    core_ref, mine_ref, other_ref = ins
    out = outs[0]
    core = core_ref[0]
    for y in range(4):
        rows = pl.ds(32 * y, 32)
        for x in range(2):
            a = 4 * x + y
            for t in range(4):
                part = slice(32 * t, 32 * t + 32)
                at = pl.multiple_of(1024 * core + 512 * x + HS * t, HS)
                out.ref[rows, pl.ds(at, HS)] = mine_ref[a, part].astype(F32)
                at = pl.multiple_of(1024 * (1 - core) + 512 * x + HS * t, HS)
                out.ref[rows, pl.ds(at, HS)] = other_ref[a, part].astype(F32)
        out.push(rows)


def exchange(operand):
    return lax.all_to_all(
        operand, "ctx", split_axis=0, concat_axis=0, tiled=True, axis_index_groups=SAME_CORE
    )


def after(value, *others):
    return lax.optimization_barrier((value, *others))[0]


def shards(query_rows, key_rows, value_rows, session, lengths, out_weight, upstream):
    index = lax.axis_index("ctx").astype(jnp.int32)
    core = index & 1
    core_ref = core.reshape(1)
    high_ref = (index >> 3).reshape(1)
    row_ref = lax.axis_index("fsdp").astype(jnp.int32).reshape(1)
    valid_len = lengths[0]
    width = out_weight.shape[1]
    half = width // 2
    quarter = half // 2

    side = ("R", (BLOCK, half), BF16)
    part = ("R", (BLOCK, quarter), BF16)
    packed, own_half, up_mine, up_send, up_pair, up_diag = call(
        pack_kernel,
        [
            ("S", core_ref), ("S", high_ref), ("H", query_rows, 0), ("H", key_rows, 0),
            ("H", value_rows, 0), ("H", out_weight), ("H", upstream, 0),
        ],
        [("R", (HEADS, 3, BLOCK, HS), BF16), ("R", (HS, half), BF16), side, side, part, part],
    )
    own = exchange(packed)

    session_ids = session[0]
    positions = jnp.arange(LEN, dtype=jnp.int32).reshape(CHIPS, 2, BLOCK)
    own_sessions = lax.dynamic_index_in_dim(session_ids.reshape(CHIPS, 2, BLOCK), core, 1, False)
    own_positions = lax.dynamic_index_in_dim(positions, core, 1, False)
    end = jnp.sum(
        (session_ids[:, None] <= own_sessions.reshape(1, -1)).astype(jnp.int32), axis=0
    )
    end = jnp.minimum(end, valid_len).reshape(4, 1, TILE)
    valid = (own_positions < valid_len).astype(F32).reshape(4, 1, TILE)
    rows_here = index * BLOCK + jnp.arange(BLOCK, dtype=jnp.int32)
    valid_here = (rows_here < valid_len).astype(F32)[:, None]

    def step(value, s):
        return lax.ppermute(value, "fsdp", [(i, i ^ s) for i in range(8)])

    over = step(own_half, 4)
    one, three = step(own_half, 1), step(own_half, 3)
    over_one, over_three = step(over, 1), step(over, 3)
    two, over_two = step(one, 3), step(over_three, 1)
    pieces = [own_half, one, two, three, over, over_one, over_two, over_three]
    up_other = lax.ppermute(up_send, "ctx", CORE_SWAP)

    own = after(own, end, valid, valid_here, one, three, over_one, over_three, up_other)
    other = lax.ppermute(own, "ctx", CORE_SWAP)
    pairs = 4 * TILE * SPAN * 5 // 2
    rows = ("H", (LEN, HS), BF16)
    context, lse, query, key, value = call(
        forward_kernel,
        [("S", core_ref), ("V", own), ("V", other), ("V", end), ("V", valid)],
        [
            ("H", (CHIPS, 2, BLOCK, HS), BF16),
            ("H", (4, 1, TILE), F32),
            ("H", (CHIPS, BLOCK, HS), BF16),
            rows,
            rows,
        ],
        scratch=(pltpu.VMEM((LEN, TILE), F32),),
        flops=4 * pairs * HS,
    )
    context_mine = exchange(context)
    up_pair = lax.ppermute(after(up_pair, context), "ctx", PAIR_SWAP)
    up_diag = lax.ppermute(after(up_diag, context), "ctx", DIAG_SWAP)
    grads_keep, grads_send = call(
        project_kernel,
        [("S", row_ref), ("A", up_mine), ("A", up_other), *[("V", piece) for piece in pieces]],
        [("V", (HEADS, BLOCK, HS), F32), ("V", (HEADS, BLOCK, HS), BF16)],
        flops=2 * 256 * 1024 * 1024,
    )
    grads_came = lax.ppermute(grads_send, "ctx", CORE_SWAP)
    grads = call(
        add_kernel,
        [("V", valid_here), ("V", grads_keep), ("V", grads_came)],
        [("V", (HEADS, BLOCK, HS), BF16)],
    )
    context_mine = after(context_mine, grads, up_pair, up_diag)
    context_other = lax.ppermute(context_mine, "ctx", CORE_SWAP)
    terms = call(
        weight_kernel,
        [
            ("S", high_ref), ("A", up_mine), ("A", up_other), ("A", up_pair), ("A", up_diag),
            ("A", context_mine), ("A", context_other),
        ],
        [("H", (32, 32, quarter), BF16)],
        flops=2 * 512 * 1024 * 512,
    )
    grads = exchange(after(grads, context_mine))
    terms = lax.all_to_all(
        after(terms, grads),
        ("ctx", "fsdp"),
        split_axis=0,
        concat_axis=0,
        tiled=True,
        axis_index_groups=REDUCE,
    )
    dq, keep, send = call(
        backward_kernel,
        [
            ("S", core_ref), ("H", query), ("H", key), ("H", grads), ("H", value),
            ("H", context, (slice(None), 0)), ("A", end), ("H", lse),
        ],
        [
            ("H", (CHIPS, BLOCK, HS), BF16),
            ("H", (CHIPS, 2, BLOCK, HS), F32),
            ("H", (CHIPS, 2, BLOCK, HS), BF16),
        ],
        scratch=(pltpu.VMEM((LEN, HS), F32), pltpu.VMEM((LEN, HS), F32)),
        flops=10 * pairs * HS,
    )
    came = lax.ppermute(send, "ctx", CORE_SWAP)
    joined = call(
        join_kernel,
        [("A", dq), ("A", keep), ("A", came)],
        [("R", (CHIPS, 4, BLOCK, HS), BF16)],
        scratch=(pltpu.VMEM((CHIPS, 3, BLOCK, HS), BF16),),
    )
    joined = call(
        total_kernel,
        [("R", joined), ("V", terms)],
        [("R", (CHIPS, 4, BLOCK, HS), BF16)],
        scratch=(pltpu.VMEM((BLOCK, HS), BF16),),
        aliases={0: 0},
    )
    side = ("H", (BLOCK, half), BF16)
    attended_keep, attended_send = call(
        attend_kernel,
        [
            ("S", row_ref), ("A", after(context_mine, joined), (slice(None), 0)),
            ("A", context_other, (slice(None), 0)), *[("A", piece) for piece in pieces],
        ],
        [side, side],
        flops=2 * 256 * 1024 * 1024,
    )
    attended_came = lax.ppermute(attended_send, "ctx", CORE_SWAP)
    attended = call(
        place_kernel,
        [("S", core_ref), ("A", attended_keep), ("A", attended_came)],
        [("R", (1, BLOCK, width), BF16)],
    )
    result = after(exchange(joined), attended)
    weight_mine = result[:, 3]
    weight_other = lax.ppermute(weight_mine, "ctx", CORE_SWAP)
    grad = ("R", (1, BLOCK, HEADS * HS), BF16)
    query_grad, key_grad, value_grad = call(unpack_kernel, [("V", result)], [grad, grad, grad])
    weight_grad = call(
        widen_kernel,
        [("S", core_ref), ("V", weight_mine), ("V", weight_other)],
        [("H", (HS, width), F32)],
    )
    return (attended, query_grad, key_grad, value_grad, weight_grad)


def solution(mesh):
    rows = P("fsdp", "ctx", None)
    return jax.shard_map(
        shards,
        mesh=mesh,
        in_specs=(rows, rows, rows, P("fsdp", None), P("fsdp"), P("fsdp", None), rows),
        out_specs=(rows, rows, rows, rows, P("fsdp", None)),
        check_vma=False,
    )
```

```python
import functools
import math

import jax
import jax.numpy as jnp
from jax import lax
from jax.experimental import pallas as pl
from jax.experimental.pallas import tpu as pltpu
from jax.sharding import PartitionSpec as P

HEADS = 8
HS = 128
BLOCK = 128
TILE = 256
SPAN = 512
REACH = 128
CHIPS = 8
LEN = 2048
NEG = -1e30
SEMS = 48
SCALE = 1.0 / math.sqrt(HS)
SCALE2 = SCALE * math.log2(math.e)
F32 = jnp.float32
BF16 = jnp.bfloat16

CORE_SWAP = [(i, i ^ 1) for i in range(16)]
PAIR_SWAP = [(i, i ^ 8) for i in range(16)]
DIAG_SWAP = [(i, i ^ 9) for i in range(16)]
SAME_CORE = [[2 * j + c for j in range(CHIPS)] for c in range(2)]
REDUCE = [
    [(8 * h + 2 * y + c) * 8 + f for f in range(8) for y in range(4)]
    for h in range(2)
    for c in range(2)
]


def dot_nt(a, b):
    return lax.dot_general(a, b, (((1,), (1,)), ((), ())), preferred_element_type=F32)


def dot_tn(a, b):
    return lax.dot_general(a, b, (((0,), (0,)), ((), ())), preferred_element_type=F32)


def dot_nn(a, b):
    return lax.dot_general(a, b, (((1,), (0,)), ((), ())), preferred_element_type=F32)


class Load:
    def __init__(self, copy, ref):
        self.copy, self.ref, self.done = copy, ref, False

    def get(self):
        if not self.done:
            self.copy.wait()
            self.done = True
        return self.ref


class Store:
    def __init__(self, hbm, ref, sems):
        self.hbm, self.ref, self.sems, self.copies = hbm, ref, sems, []

    def push(self, *index):
        src = self.ref.at[index] if index else self.ref
        dst = self.hbm.at[index] if index else self.hbm
        copy = pltpu.make_async_copy(src, dst, next(self.sems))
        copy.start()
        self.copies.append(copy)


SPACES = {"S": pltpu.SMEM, "V": pltpu.VMEM, "H": pltpu.HBM, "A": pl.ANY, "R": pltpu.HBM}


def call(kernel, ins, outs, scratch=(), flops=0, mib=14, aliases=None):
    copied = [
        pltpu.VMEM(jax.eval_shape(lambda x: x[i[2]] if len(i) > 2 else x, i[1]).shape, i[1].dtype)
        for i in ins
        if i[0] in "HA"
    ] + [pltpu.VMEM(o[1], o[2]) for o in outs if o[0] == "H"]

    def body(*refs):
        refs = list(refs)
        in_refs = [refs.pop(0) for _ in ins]
        out_refs = [refs.pop(0) for _ in outs]
        sem_ref = refs.pop(0)
        buffers = [refs.pop(0) for _ in copied]
        sems = (sem_ref.at[n] for n in range(SEMS))
        given, made = [], []
        for one, ref in zip(ins, in_refs):
            if one[0] in "HA":
                buffer = buffers.pop(0)
                copy = pltpu.make_async_copy(
                    ref.at[one[2]] if len(one) > 2 else ref, buffer, next(sems)
                )
                copy.start()
                ref = Load(copy, buffer)
            given.append(ref)
        for one, ref in zip(outs, out_refs):
            made.append(Store(ref, buffers.pop(0), sems) if one[0] == "H" else ref)
        more = kernel(given, made, refs, sems) or []
        for one in given:
            if isinstance(one, Load):
                one.get()
        for one in made:
            if isinstance(one, Store):
                for copy in one.copies:
                    copy.wait()
        for copy in more:
            copy.wait()

    result = pl.pallas_call(
        body,
        out_shape=[
            SPACES[o[0]](o[1], o[2]) if o[0] in "HR" else jax.ShapeDtypeStruct(o[1], o[2])
            for o in outs
        ],
        in_specs=[pl.BlockSpec(memory_space=SPACES[i[0]]) for i in ins],
        out_specs=[pl.BlockSpec(memory_space=SPACES[o[0]]) for o in outs],
        scratch_shapes=[pltpu.SemaphoreType.DMA((SEMS,)), *copied, *scratch],
        input_output_aliases=aliases or {},
        compiler_params=pltpu.CompilerParams(vmem_limit_bytes=mib * 1024 * 1024),
        cost_estimate=pl.CostEstimate(flops=flops, bytes_accessed=2_000_000, transcendentals=0),
    )(*[
        pltpu.with_memory_space_constraint(i[1], pltpu.HBM) if i[0] in "HR" else i[1] for i in ins
    ])
    return result[0] if len(outs) == 1 else result


def pack_kernel(ins, outs, scratch, sems):
    core_ref, high_ref, *data = ins
    out_ref, half_ref, up_mine_ref, up_send_ref, pair_ref, diag_ref = outs
    core, high = core_ref[0], high_ref[0]
    half = half_ref.shape[1]
    quarter = half // 2
    copies = []

    def copy(src, dst):
        copies.append(pltpu.make_async_copy(src, dst, next(sems)))
        copies[-1].start()

    mine = pl.ds(pl.multiple_of(core * half, half), half)
    other = pl.ds(pl.multiple_of((1 - core) * half, half), half)
    copy(data[3].get().at[:, mine], half_ref)
    for i in range(3):
        ref = data[i].get()
        for a in range(HEADS):
            copy(ref.at[:, pl.ds(a * HS, HS)], out_ref.at[a, i])
    up_ref = data[4].get()
    copy(up_ref.at[:, mine], up_mine_ref)
    copy(up_ref.at[:, other], up_send_ref)
    for ref, c in ((pair_ref, core), (diag_ref, 1 - core)):
        at = pl.multiple_of(c * half + (1 - high) * quarter, quarter)
        copy(up_ref.at[:, pl.ds(at, quarter)], ref)
    return copies


def in_order(core, own_ref, other_ref, slot, dst_ref):
    for j in range(CHIPS):
        own = pl.multiple_of(2 * BLOCK * j + BLOCK * core, BLOCK)
        other = pl.multiple_of(2 * BLOCK * j + BLOCK * (1 - core), BLOCK)
        dst_ref[pl.ds(own, BLOCK)] = own_ref[j]
        dst_ref[pl.ds(other, BLOCK)] = other_ref[j, slot]


def chunks_of(m):
    stop = min(SPAN * (m + 1) + REACH, LEN)
    return [(start, min(start + SPAN, stop)) for start in range(0, stop, SPAN)]


def masked_scores(k_s, q, end, m, start, stop):
    scores = dot_nt(k_s[start:stop], q)
    if stop > SPAN * m:
        at = lax.broadcasted_iota(jnp.int32, scores.shape, 0) + start
        scores = jnp.where(at < end, scores, NEG)
    return scores


def forward_kernel(ins, outs, scratch, sems):
    core_ref, q_in, k_in, v_in, other_ref, end_ref, valid_ref = ins
    ctx_out, lse_out, q_out, k_out, v_out = outs
    (s_s,) = scratch
    core = core_ref[0]
    k_s, v_s = k_out.ref, v_out.ref
    in_order(core, k_in.get(), other_ref, 1, k_s)
    k_out.push()
    q_ref = q_in.get()
    q_out.ref[...] = q_ref[...]
    q_out.push()
    in_order(core, v_in.get(), other_ref, 2, v_s)
    v_out.push()
    for m in range(4):
        q = q_ref[2 * m : 2 * m + 2].reshape(TILE, HS)
        end = end_ref[m]
        top = jnp.full((1, TILE), NEG, F32)
        for start, stop in chunks_of(m):
            scores = masked_scores(k_s, q, end, m, start, stop)
            s_s[start:stop] = scores
            top = jnp.maximum(top, jnp.max(scores, axis=0, keepdims=True))
        top2 = top * SCALE2
        total = jnp.zeros((1, TILE), F32)
        acc = jnp.zeros((HS, TILE), F32)
        for start, stop in chunks_of(m):
            p = jnp.exp2(s_s[start:stop] * SCALE2 - top2)
            total = total + jnp.sum(p, axis=0, keepdims=True)
            acc = acc + dot_tn(v_s[start:stop], p.astype(BF16))
        lse_out.ref[m] = top2 + jnp.log2(total)
        ctx = (acc * (valid_ref[m] / total)).T.astype(BF16)
        for t in range(2):
            j = 2 * m + t
            block = ctx[t * BLOCK : (t + 1) * BLOCK]
            ctx_out.ref[j, 0] = block
            ctx_out.ref[j ^ 4, 1] = block
            ctx_out.push(j, 0)
            ctx_out.push(j ^ 4, 1)
    lse_out.push()


def backward_kernel(ins, outs, scratch, sems):
    core_ref, q_in, k_in, grad_in, v_in, ctx_in, end_in, lse_in = ins
    dq_out, keep_out, send_out = outs
    dk_s, dv_s = scratch
    core = core_ref[0]
    dk_s[...] = jnp.zeros(dk_s.shape, F32)
    dv_s[...] = jnp.zeros(dv_s.shape, F32)
    end_ref, lse_ref = end_in.get(), lse_in.get()
    q_ref, k_s = q_in.get(), k_in.get()
    grad_ref, v_s, ctx_ref = grad_in.get(), v_in.get(), ctx_in.get()
    for m in range(3, -1, -1):
        rows = slice(2 * m, 2 * m + 2)
        q = q_ref[rows].reshape(TILE, HS)
        do = grad_ref[rows].reshape(TILE, HS)
        ctx = ctx_ref[rows].reshape(TILE, HS)
        delta = jnp.sum((do.astype(F32) * ctx.astype(F32)).T, axis=0, keepdims=True)
        end = end_ref[m]
        lse = lse_ref[m]
        dq = jnp.zeros((HS, TILE), F32)
        for start, stop in chunks_of(m):
            scores = masked_scores(k_s, q, end, m, start, stop)
            p = jnp.exp2(scores * SCALE2 - lse)
            dp = dot_nt(v_s[start:stop], do)
            ds = (p * (dp - delta) * SCALE).astype(BF16)
            dv_s[start:stop] += dot_nn(p.astype(BF16), do)
            dk_s[start:stop] += dot_nn(ds, q)
            dq = dq + dot_tn(k_s[start:stop], ds)
        dq_rows = dq.T.astype(BF16)
        dq_out.ref[2 * m] = dq_rows[:BLOCK]
        dq_out.ref[2 * m + 1] = dq_rows[BLOCK:]
        dq_out.push(pl.ds(2 * m, 2))
        first = 2 * m + 1 if m else 0
        last = 2 * m + 3 if m < 3 else CHIPS
        for j in range(first, last):
            own = pl.multiple_of(2 * BLOCK * j + BLOCK * core, BLOCK)
            other = pl.multiple_of(2 * BLOCK * j + BLOCK * (1 - core), BLOCK)
            send_out.ref[j, 0] = dk_s[pl.ds(other, BLOCK)].astype(BF16)
            send_out.ref[j, 1] = dv_s[pl.ds(other, BLOCK)].astype(BF16)
            send_out.push(j)
            keep_out.ref[j, 0] = dk_s[pl.ds(own, BLOCK)]
            keep_out.ref[j, 1] = dv_s[pl.ds(own, BLOCK)]
            keep_out.push(j)


def project_kernel(ins, outs, scratch, sems):
    row_ref, up_in, up_other_in, *pieces = ins
    keep_ref, send_ref = outs
    row = row_ref[0]
    up = jnp.concatenate([up_in.get()[...], up_other_in.get()[...]], axis=0)
    for s in range(HEADS):
        total = dot_nt(up, pieces[s][...])
        at = jnp.bitwise_xor(row, s)
        keep_ref[at] = total[:BLOCK]
        send_ref[at] = total[BLOCK:].astype(BF16)


def add_kernel(ins, outs, scratch, sems):
    valid_ref, keep_ref, came_ref = ins
    outs[0][...] = ((keep_ref[...] + came_ref[...].astype(F32)) * valid_ref[...]).astype(BF16)


def attend_kernel(ins, outs, scratch, sems):
    row_ref, ctx_in, ctx_other_in, *pieces = ins
    keep, send = outs
    row = row_ref[0]
    order = [jnp.bitwise_xor(row, s) for s in range(HEADS)]
    ctx_ref, ctx_other_ref = ctx_in.get(), ctx_other_in.get()
    ctx = jnp.concatenate(
        [
            jnp.concatenate([ctx_ref[a] for a in order], axis=1),
            jnp.concatenate([ctx_other_ref[a] for a in order], axis=1),
        ],
        axis=0,
    )
    pieces = [piece.get() for piece in pieces]
    for n in range(4):
        cols = slice(n * TILE, (n + 1) * TILE)
        weight = jnp.concatenate([piece[:, cols] for piece in pieces], axis=0)
        total = dot_nn(ctx, weight).astype(BF16)
        keep.ref[:, cols] = total[:BLOCK]
        send.ref[:, cols] = total[BLOCK:]
    send.push()
    keep.push()


def place_kernel(ins, outs, scratch, sems):
    core_ref, keep_in, came_in = ins
    core = core_ref[0]
    half = keep_in.ref.shape[1]
    copies = []
    for one, c in ((keep_in, core), (came_in, 1 - core)):
        at = pl.ds(pl.multiple_of(c * half, half), half)
        copies.append(pltpu.make_async_copy(one.get(), outs[0].at[0, :, at], next(sems)))
        copies[-1].start()
    return copies


def weight_kernel(ins, outs, scratch, sems):
    out = outs[0]
    high_ref = ins[0]
    mine, other, pair, diag, ctx_ref, ctx_other_ref = [one.get() for one in ins[1:]]
    quarter = pair.shape[1]
    at = pl.ds(pl.multiple_of(high_ref[0] * quarter, quarter), quarter)
    up = jnp.concatenate([mine[:, at], pair[...]], axis=0)
    up_other = jnp.concatenate([other[:, at], diag[...]], axis=0)
    for a in range(HEADS):
        total = dot_tn(ctx_ref[a].reshape(TILE, HS), up)
        total = total + dot_tn(ctx_other_ref[a].reshape(TILE, HS), up_other)
        part = pl.ds(4 * a, 4)
        out.ref[part] = total.reshape(4, HS // 4, quarter).astype(BF16)
        out.push(part)


def join_kernel(ins, outs, scratch, sems):
    dq_in, keep_in, came_in = ins
    (made,) = scratch
    copies = []
    dq_ref, keep_ref, came_ref = dq_in.get(), keep_in.get(), came_in.get()
    for j in range(CHIPS):
        made[j, 0] = dq_ref[j]
        made[j, 1] = (keep_ref[j, 0] + came_ref[j, 0].astype(F32)).astype(BF16)
        made[j, 2] = (keep_ref[j, 1] + came_ref[j, 1].astype(F32)).astype(BF16)
        copies.append(
            pltpu.make_async_copy(made.at[j], outs[0].at[j, pl.ds(0, 3)], next(sems))
        )
        copies[-1].start()
    return copies


def total_kernel(ins, outs, scratch, sems):
    terms_ref = ins[1]
    (made,) = scratch
    total = terms_ref[0].astype(F32)
    for s in range(1, terms_ref.shape[0]):
        total = total + terms_ref[s].astype(F32)
    weight = total.astype(BF16)
    rows = weight.shape[0]
    for t in range(4):
        made[t * rows : (t + 1) * rows] = weight[:, t * HS : (t + 1) * HS]
    copies = []
    for j in range(CHIPS):
        copies.append(pltpu.make_async_copy(made, outs[0].at[j, 3], next(sems)))
        copies[-1].start()
    return copies


def unpack_kernel(ins, outs, scratch, sems):
    mine_ref = ins[0]
    copies = []
    for a in range(HEADS):
        for i in range(3):
            dst = outs[i].at[0, :, pl.ds(a * HS, HS)]
            copies.append(pltpu.make_async_copy(mine_ref.at[a, i], dst, next(sems)))
            copies[-1].start()
    return copies


def widen_kernel(ins, outs, scratch, sems):
    core_ref, mine_ref, other_ref = ins
    out = outs[0]
    core = core_ref[0]
    for y in range(4):
        rows = pl.ds(32 * y, 32)
        for x in range(2):
            a = 4 * x + y
            for t in range(4):
                part = slice(32 * t, 32 * t + 32)
                at = pl.multiple_of(1024 * core + 512 * x + HS * t, HS)
                out.ref[rows, pl.ds(at, HS)] = mine_ref[a, part].astype(F32)
                at = pl.multiple_of(1024 * (1 - core) + 512 * x + HS * t, HS)
                out.ref[rows, pl.ds(at, HS)] = other_ref[a, part].astype(F32)
        out.push(rows)


def exchange(operand):
    return lax.all_to_all(
        operand, "ctx", split_axis=0, concat_axis=0, tiled=True, axis_index_groups=SAME_CORE
    )


def after(value, *others):
    return lax.optimization_barrier((value, *others))[0]


def shards(query_rows, key_rows, value_rows, session, lengths, out_weight, upstream):
    index = lax.axis_index("ctx").astype(jnp.int32)
    core = index & 1
    core_ref = core.reshape(1)
    high_ref = (index >> 3).reshape(1)
    row_ref = lax.axis_index("fsdp").astype(jnp.int32).reshape(1)
    valid_len = lengths[0]
    width = out_weight.shape[1]
    half = width // 2
    quarter = half // 2

    side = ("R", (BLOCK, half), BF16)
    part = ("R", (BLOCK, quarter), BF16)
    packed, own_half, up_mine, up_send, up_pair, up_diag = call(
        pack_kernel,
        [
            ("S", core_ref), ("S", high_ref), ("H", query_rows, 0), ("H", key_rows, 0),
            ("H", value_rows, 0), ("H", out_weight), ("H", upstream, 0),
        ],
        [("R", (HEADS, 3, BLOCK, HS), BF16), ("R", (HS, half), BF16), side, side, part, part],
    )
    own = exchange(packed)

    session_ids = session[0]
    positions = jnp.arange(LEN, dtype=jnp.int32).reshape(CHIPS, 2, BLOCK)
    own_sessions = lax.dynamic_index_in_dim(session_ids.reshape(CHIPS, 2, BLOCK), core, 1, False)
    own_positions = lax.dynamic_index_in_dim(positions, core, 1, False)
    end = jnp.sum(
        (session_ids[:, None] <= own_sessions.reshape(1, -1)).astype(jnp.int32), axis=0
    )
    end = jnp.minimum(end, valid_len).reshape(4, 1, TILE)
    valid = (own_positions < valid_len).astype(F32).reshape(4, 1, TILE)
    rows_here = index * BLOCK + jnp.arange(BLOCK, dtype=jnp.int32)
    valid_here = (rows_here < valid_len).astype(F32)[:, None]

    def step(value, s):
        return lax.ppermute(value, "fsdp", [(i, i ^ s) for i in range(8)])

    over = step(own_half, 4)
    one, three = step(own_half, 1), step(own_half, 3)
    over_one, over_three = step(over, 1), step(over, 3)
    two, over_two = step(one, 3), step(over_three, 1)
    pieces = [own_half, one, two, three, over, over_one, over_two, over_three]
    up_other = lax.ppermute(up_send, "ctx", CORE_SWAP)
    up_pair = lax.ppermute(after(up_pair, over, one), "ctx", PAIR_SWAP)
    up_diag = lax.ppermute(after(up_diag, over, one), "ctx", DIAG_SWAP)

    own = after(
        own, end, valid, valid_here, one, three, over_one, over_three, up_other, up_pair, up_diag
    )
    other = lax.ppermute(own, "ctx", CORE_SWAP)
    pairs = 4 * TILE * SPAN * 5 // 2
    rows = ("H", (LEN, HS), BF16)
    context, lse, query, key, value = call(
        forward_kernel,
        [
            ("S", core_ref), ("A", own, (slice(None), 0)), ("A", own, (slice(None), 1)),
            ("A", own, (slice(None), 2)), ("V", other), ("V", end), ("V", valid),
        ],
        [
            ("H", (CHIPS, 2, BLOCK, HS), BF16),
            ("H", (4, 1, TILE), F32),
            ("H", (CHIPS, BLOCK, HS), BF16),
            rows,
            rows,
        ],
        scratch=(pltpu.VMEM((LEN, TILE), F32),),
        flops=4 * pairs * HS,
    )
    context_mine = exchange(context)
    grads_keep, grads_send = call(
        project_kernel,
        [("S", row_ref), ("A", up_mine), ("A", up_other), *[("V", piece) for piece in pieces]],
        [("V", (HEADS, BLOCK, HS), F32), ("V", (HEADS, BLOCK, HS), BF16)],
        flops=2 * 256 * 1024 * 1024,
    )
    grads_came = lax.ppermute(grads_send, "ctx", CORE_SWAP)
    grads = call(
        add_kernel,
        [("V", valid_here), ("V", grads_keep), ("V", grads_came)],
        [("V", (HEADS, BLOCK, HS), BF16)],
    )
    context_mine = after(context_mine, grads)
    context_other = lax.ppermute(context_mine, "ctx", CORE_SWAP)
    terms = call(
        weight_kernel,
        [
            ("S", high_ref), ("A", up_mine), ("A", up_other), ("A", up_pair), ("A", up_diag),
            ("A", context_mine), ("A", context_other),
        ],
        [("H", (32, 32, quarter), BF16)],
        flops=2 * 512 * 1024 * 512,
    )
    grads = exchange(after(grads, context_mine))
    terms = lax.all_to_all(
        after(terms, grads),
        ("ctx", "fsdp"),
        split_axis=0,
        concat_axis=0,
        tiled=True,
        axis_index_groups=REDUCE,
    )
    dq, keep, send = call(
        backward_kernel,
        [
            ("S", core_ref), ("H", query), ("H", key), ("H", grads), ("H", value),
            ("H", context, (slice(None), 0)), ("A", end), ("H", lse),
        ],
        [
            ("H", (CHIPS, BLOCK, HS), BF16),
            ("H", (CHIPS, 2, BLOCK, HS), F32),
            ("H", (CHIPS, 2, BLOCK, HS), BF16),
        ],
        scratch=(pltpu.VMEM((LEN, HS), F32), pltpu.VMEM((LEN, HS), F32)),
        flops=10 * pairs * HS,
    )
    came = lax.ppermute(send, "ctx", CORE_SWAP)
    joined = call(
        join_kernel,
        [("A", dq), ("A", keep), ("A", came)],
        [("R", (CHIPS, 4, BLOCK, HS), BF16)],
        scratch=(pltpu.VMEM((CHIPS, 3, BLOCK, HS), BF16),),
    )
    joined = call(
        total_kernel,
        [("R", joined), ("V", terms)],
        [("R", (CHIPS, 4, BLOCK, HS), BF16)],
        scratch=(pltpu.VMEM((BLOCK, HS), BF16),),
        aliases={0: 0},
    )
    side = ("H", (BLOCK, half), BF16)
    attended_keep, attended_send = call(
        attend_kernel,
        [
            ("S", row_ref), ("A", after(context_mine, joined), (slice(None), 0)),
            ("A", context_other, (slice(None), 0)), *[("A", piece) for piece in pieces],
        ],
        [side, side],
        flops=2 * 256 * 1024 * 1024,
    )
    attended_came = lax.ppermute(attended_send, "ctx", CORE_SWAP)
    attended = call(
        place_kernel,
        [("S", core_ref), ("A", attended_keep), ("A", attended_came)],
        [("R", (1, BLOCK, width), BF16)],
    )
    result = after(exchange(joined), attended)
    weight_mine = result[:, 3]
    weight_other = lax.ppermute(weight_mine, "ctx", CORE_SWAP)
    grad = ("R", (1, BLOCK, HEADS * HS), BF16)
    query_grad, key_grad, value_grad = call(unpack_kernel, [("V", result)], [grad, grad, grad])
    weight_grad = call(
        widen_kernel,
        [("S", core_ref), ("V", weight_mine), ("V", weight_other)],
        [("H", (HS, width), F32)],
    )
    return (attended, query_grad, key_grad, value_grad, weight_grad)


def solution(mesh):
    rows = P("fsdp", "ctx", None)
    return jax.shard_map(
        shards,
        mesh=mesh,
        in_specs=(rows, rows, rows, P("fsdp", None), P("fsdp"), P("fsdp", None), rows),
        out_specs=(rows, rows, rows, rows, P("fsdp", None)),
        check_vma=False,
    )
```

```python
import functools
import math

import jax
import jax.numpy as jnp
from jax import lax
from jax.experimental import pallas as pl
from jax.experimental.pallas import tpu as pltpu
from jax.sharding import PartitionSpec as P

HEADS = 8
HS = 128
BLOCK = 128
TILE = 256
SPAN = 512
REACH = 128
CHIPS = 8
LEN = 2048
NEG = -1e30
SEMS = 48
SCALE = 1.0 / math.sqrt(HS)
SCALE2 = SCALE * math.log2(math.e)
F32 = jnp.float32
BF16 = jnp.bfloat16

CORE_SWAP = [(i, i ^ 1) for i in range(16)]
PAIR_SWAP = [(i, i ^ 8) for i in range(16)]
DIAG_SWAP = [(i, i ^ 9) for i in range(16)]
SAME_CORE = [[2 * j + c for j in range(CHIPS)] for c in range(2)]
REDUCE = [
    [(8 * h + 2 * y + c) * 8 + f for f in range(8) for y in range(4)]
    for h in range(2)
    for c in range(2)
]


def dot_nt(a, b):
    return lax.dot_general(a, b, (((1,), (1,)), ((), ())), preferred_element_type=F32)


def dot_tn(a, b):
    return lax.dot_general(a, b, (((0,), (0,)), ((), ())), preferred_element_type=F32)


def dot_nn(a, b):
    return lax.dot_general(a, b, (((1,), (0,)), ((), ())), preferred_element_type=F32)


class Load:
    def __init__(self, copy, ref):
        self.copy, self.ref, self.done = copy, ref, False

    def get(self):
        if not self.done:
            self.copy.wait()
            self.done = True
        return self.ref


class Store:
    def __init__(self, hbm, ref, sems):
        self.hbm, self.ref, self.sems, self.copies = hbm, ref, sems, []

    def push(self, *index):
        src = self.ref.at[index] if index else self.ref
        dst = self.hbm.at[index] if index else self.hbm
        copy = pltpu.make_async_copy(src, dst, next(self.sems))
        copy.start()
        self.copies.append(copy)


SPACES = {"S": pltpu.SMEM, "V": pltpu.VMEM, "H": pltpu.HBM, "A": pl.ANY, "R": pltpu.HBM}


def call(kernel, ins, outs, scratch=(), flops=0, mib=14, aliases=None):
    copied = [
        pltpu.VMEM(jax.eval_shape(lambda x: x[i[2]] if len(i) > 2 else x, i[1]).shape, i[1].dtype)
        for i in ins
        if i[0] in "HA"
    ] + [pltpu.VMEM(o[1], o[2]) for o in outs if o[0] == "H"]

    def body(*refs):
        refs = list(refs)
        in_refs = [refs.pop(0) for _ in ins]
        out_refs = [refs.pop(0) for _ in outs]
        sem_ref = refs.pop(0)
        buffers = [refs.pop(0) for _ in copied]
        sems = (sem_ref.at[n] for n in range(SEMS))
        given, made = [], []
        for one, ref in zip(ins, in_refs):
            if one[0] in "HA":
                buffer = buffers.pop(0)
                copy = pltpu.make_async_copy(
                    ref.at[one[2]] if len(one) > 2 else ref, buffer, next(sems)
                )
                copy.start()
                ref = Load(copy, buffer)
            given.append(ref)
        for one, ref in zip(outs, out_refs):
            made.append(Store(ref, buffers.pop(0), sems) if one[0] == "H" else ref)
        more = kernel(given, made, refs, sems) or []
        for one in given:
            if isinstance(one, Load):
                one.get()
        for one in made:
            if isinstance(one, Store):
                for copy in one.copies:
                    copy.wait()
        for copy in more:
            copy.wait()

    result = pl.pallas_call(
        body,
        out_shape=[
            SPACES[o[0]](o[1], o[2]) if o[0] in "HR" else jax.ShapeDtypeStruct(o[1], o[2])
            for o in outs
        ],
        in_specs=[pl.BlockSpec(memory_space=SPACES[i[0]]) for i in ins],
        out_specs=[pl.BlockSpec(memory_space=SPACES[o[0]]) for o in outs],
        scratch_shapes=[pltpu.SemaphoreType.DMA((SEMS,)), *copied, *scratch],
        input_output_aliases=aliases or {},
        compiler_params=pltpu.CompilerParams(vmem_limit_bytes=mib * 1024 * 1024),
        cost_estimate=pl.CostEstimate(flops=flops, bytes_accessed=2_000_000, transcendentals=0),
    )(*[
        pltpu.with_memory_space_constraint(i[1], pltpu.HBM) if i[0] in "HR" else i[1] for i in ins
    ])
    return result[0] if len(outs) == 1 else result


def pack_kernel(ins, outs, scratch, sems):
    core_ref, high_ref, *data = ins
    out_ref, half_ref, up_mine_ref, up_send_ref, pair_ref, diag_ref = outs
    core, high = core_ref[0], high_ref[0]
    half = half_ref.shape[1]
    quarter = half // 2
    copies = []

    def copy(src, dst):
        copies.append(pltpu.make_async_copy(src, dst, next(sems)))
        copies[-1].start()

    mine = pl.ds(pl.multiple_of(core * half, half), half)
    other = pl.ds(pl.multiple_of((1 - core) * half, half), half)
    copy(data[3].get().at[:, mine], half_ref)
    for i in range(3):
        ref = data[i].get()
        for a in range(HEADS):
            copy(ref.at[:, pl.ds(a * HS, HS)], out_ref.at[a, i])
    up_ref = data[4].get()
    copy(up_ref.at[:, mine], up_mine_ref)
    copy(up_ref.at[:, other], up_send_ref)
    for ref, c in ((pair_ref, core), (diag_ref, 1 - core)):
        at = pl.multiple_of(c * half + (1 - high) * quarter, quarter)
        copy(up_ref.at[:, pl.ds(at, quarter)], ref)
    return copies


def in_order(core, own_ref, other_ref, slot, dst_ref):
    for j in range(CHIPS):
        own = pl.multiple_of(2 * BLOCK * j + BLOCK * core, BLOCK)
        other = pl.multiple_of(2 * BLOCK * j + BLOCK * (1 - core), BLOCK)
        dst_ref[pl.ds(own, BLOCK)] = own_ref[j]
        dst_ref[pl.ds(other, BLOCK)] = other_ref[j, slot]


def chunks_of(m):
    stop = min(SPAN * (m + 1) + REACH, LEN)
    return [(start, min(start + SPAN, stop)) for start in range(0, stop, SPAN)]


def masked_scores(k_s, q, end, m, start, stop):
    scores = dot_nt(k_s[start:stop], q)
    if stop > SPAN * m:
        at = lax.broadcasted_iota(jnp.int32, scores.shape, 0) + start
        scores = jnp.where(at < end, scores, NEG)
    return scores


def forward_kernel(ins, outs, scratch, sems):
    core_ref, q_in, k_in, v_in, other_ref, end_ref, valid_ref = ins
    ctx_out, lse_out, q_out, k_out, v_out = outs
    (s_s,) = scratch
    core = core_ref[0]
    k_s, v_s = k_out.ref, v_out.ref
    in_order(core, k_in.get(), other_ref, 1, k_s)
    k_out.push()
    q_ref = q_in.get()
    q_out.ref[...] = q_ref[...]
    q_out.push()
    in_order(core, v_in.get(), other_ref, 2, v_s)
    v_out.push()
    for m in range(4):
        q = q_ref[2 * m : 2 * m + 2].reshape(TILE, HS)
        end = end_ref[m]
        top = jnp.full((1, TILE), NEG, F32)
        for start, stop in chunks_of(m):
            scores = masked_scores(k_s, q, end, m, start, stop)
            s_s[start:stop] = scores
            top = jnp.maximum(top, jnp.max(scores, axis=0, keepdims=True))
        top2 = top * SCALE2
        total = jnp.zeros((1, TILE), F32)
        acc = jnp.zeros((HS, TILE), F32)
        for start, stop in chunks_of(m):
            p = jnp.exp2(s_s[start:stop] * SCALE2 - top2)
            total = total + jnp.sum(p, axis=0, keepdims=True)
            acc = acc + dot_tn(v_s[start:stop], p.astype(BF16))
        lse_out.ref[m] = top2 + jnp.log2(total)
        ctx = (acc * (valid_ref[m] / total)).T.astype(BF16)
        for t in range(2):
            j = 2 * m + t
            block = ctx[t * BLOCK : (t + 1) * BLOCK]
            ctx_out.ref[j, 0] = block
            ctx_out.ref[j ^ 4, 1] = block
            ctx_out.push(j, 0)
            ctx_out.push(j ^ 4, 1)
    lse_out.push()


def backward_kernel(ins, outs, scratch, sems):
    core_ref, q_in, k_in, grad_in, v_in, ctx_in, end_in, lse_in = ins
    dq_out, keep_out, send_out = outs
    dk_s, dv_s = scratch
    core = core_ref[0]
    dk_s[...] = jnp.zeros(dk_s.shape, F32)
    dv_s[...] = jnp.zeros(dv_s.shape, F32)
    end_ref, lse_ref = end_in.get(), lse_in.get()
    q_ref, k_s = q_in.get(), k_in.get()
    grad_ref, v_s, ctx_ref = grad_in.get(), v_in.get(), ctx_in.get()
    for m in range(3, -1, -1):
        rows = slice(2 * m, 2 * m + 2)
        q = q_ref[rows].reshape(TILE, HS)
        do = grad_ref[rows].reshape(TILE, HS)
        ctx = ctx_ref[rows].reshape(TILE, HS)
        delta = jnp.sum((do.astype(F32) * ctx.astype(F32)).T, axis=0, keepdims=True)
        end = end_ref[m]
        lse = lse_ref[m]
        dq = jnp.zeros((HS, TILE), F32)
        for start, stop in chunks_of(m):
            scores = masked_scores(k_s, q, end, m, start, stop)
            p = jnp.exp2(scores * SCALE2 - lse)
            dp = dot_nt(v_s[start:stop], do)
            ds = (p * (dp - delta) * SCALE).astype(BF16)
            dv_s[start:stop] += dot_nn(p.astype(BF16), do)
            dk_s[start:stop] += dot_nn(ds, q)
            dq = dq + dot_tn(k_s[start:stop], ds)
        dq_rows = dq.T.astype(BF16)
        dq_out.ref[2 * m] = dq_rows[:BLOCK]
        dq_out.ref[2 * m + 1] = dq_rows[BLOCK:]
        dq_out.push(pl.ds(2 * m, 2))
        first = 2 * m + 1 if m else 0
        last = 2 * m + 3 if m < 3 else CHIPS
        for j in range(first, last):
            own = pl.multiple_of(2 * BLOCK * j + BLOCK * core, BLOCK)
            other = pl.multiple_of(2 * BLOCK * j + BLOCK * (1 - core), BLOCK)
            send_out.ref[j, 0] = dk_s[pl.ds(other, BLOCK)].astype(BF16)
            send_out.ref[j, 1] = dv_s[pl.ds(other, BLOCK)].astype(BF16)
            send_out.push(j)
            keep_out.ref[j, 0] = dk_s[pl.ds(own, BLOCK)]
            keep_out.ref[j, 1] = dv_s[pl.ds(own, BLOCK)]
            keep_out.push(j)


def project_kernel(ins, outs, scratch, sems):
    row_ref, up_in, up_other_in, *pieces = ins
    keep_ref, send_ref = outs
    row = row_ref[0]
    up = jnp.concatenate([up_in.get()[...], up_other_in.get()[...]], axis=0)
    for s in range(HEADS):
        total = dot_nt(up, pieces[s][...])
        at = jnp.bitwise_xor(row, s)
        keep_ref[at] = total[:BLOCK]
        send_ref[at] = total[BLOCK:].astype(BF16)


def add_kernel(ins, outs, scratch, sems):
    valid_ref, keep_ref, came_ref = ins
    outs[0][...] = ((keep_ref[...] + came_ref[...].astype(F32)) * valid_ref[...]).astype(BF16)


def attend_kernel(ins, outs, scratch, sems):
    row_ref, ctx_in, ctx_other_in, *pieces = ins
    keep, send = outs
    row = row_ref[0]
    order = [jnp.bitwise_xor(row, s) for s in range(HEADS)]
    ctx_ref, ctx_other_ref = ctx_in.get(), ctx_other_in.get()
    ctx = jnp.concatenate(
        [
            jnp.concatenate([ctx_ref[a] for a in order], axis=1),
            jnp.concatenate([ctx_other_ref[a] for a in order], axis=1),
        ],
        axis=0,
    )
    pieces = [piece.get() for piece in pieces]
    for n in range(4):
        cols = slice(n * TILE, (n + 1) * TILE)
        weight = jnp.concatenate([piece[:, cols] for piece in pieces], axis=0)
        total = dot_nn(ctx, weight).astype(BF16)
        keep.ref[:, cols] = total[:BLOCK]
        send.ref[:, cols] = total[BLOCK:]
    send.push()
    keep.push()


def place_kernel(ins, outs, scratch, sems):
    core_ref, keep_in, came_in = ins
    core = core_ref[0]
    half = keep_in.ref.shape[1]
    copies = []
    for one, c in ((keep_in, core), (came_in, 1 - core)):
        at = pl.ds(pl.multiple_of(c * half, half), half)
        copies.append(pltpu.make_async_copy(one.get(), outs[0].at[0, :, at], next(sems)))
        copies[-1].start()
    return copies


def weight_kernel(ins, outs, scratch, sems):
    out = outs[0]
    high_ref = ins[0]
    mine, other, pair, diag, ctx_ref, ctx_other_ref = [one.get() for one in ins[1:]]
    quarter = pair.shape[1]
    at = pl.ds(pl.multiple_of(high_ref[0] * quarter, quarter), quarter)
    up = jnp.concatenate([mine[:, at], pair[...]], axis=0)
    up_other = jnp.concatenate([other[:, at], diag[...]], axis=0)
    for a in range(HEADS):
        total = dot_tn(ctx_ref[a].reshape(TILE, HS), up)
        total = total + dot_tn(ctx_other_ref[a].reshape(TILE, HS), up_other)
        part = pl.ds(4 * a, 4)
        out.ref[part] = total.reshape(4, HS // 4, quarter).astype(BF16)
        out.push(part)


def join_kernel(ins, outs, scratch, sems):
    dq_in, keep_in, came_in = ins
    (made,) = scratch
    copies = []
    dq_ref, keep_ref, came_ref = dq_in.get(), keep_in.get(), came_in.get()
    for j in range(CHIPS):
        made[j, 0] = dq_ref[j]
        made[j, 1] = (keep_ref[j, 0] + came_ref[j, 0].astype(F32)).astype(BF16)
        made[j, 2] = (keep_ref[j, 1] + came_ref[j, 1].astype(F32)).astype(BF16)
        copies.append(
            pltpu.make_async_copy(made.at[j], outs[0].at[j, pl.ds(0, 3)], next(sems))
        )
        copies[-1].start()
    return copies


def total_kernel(ins, outs, scratch, sems):
    terms_ref = ins[1]
    (made,) = scratch
    total = terms_ref[0].astype(F32)
    for s in range(1, terms_ref.shape[0]):
        total = total + terms_ref[s].astype(F32)
    weight = total.astype(BF16)
    rows = weight.shape[0]
    for t in range(4):
        made[t * rows : (t + 1) * rows] = weight[:, t * HS : (t + 1) * HS]
    copies = []
    for j in range(CHIPS):
        copies.append(pltpu.make_async_copy(made, outs[0].at[j, 3], next(sems)))
        copies[-1].start()
    return copies


def unpack_kernel(ins, outs, scratch, sems):
    mine_ref = ins[0]
    copies = []
    for a in range(HEADS):
        for i in range(3):
            dst = outs[i].at[0, :, pl.ds(a * HS, HS)]
            copies.append(pltpu.make_async_copy(mine_ref.at[a, i], dst, next(sems)))
            copies[-1].start()
    return copies


def widen_kernel(ins, outs, scratch, sems):
    core_ref, mine_ref, other_ref = ins
    out = outs[0]
    core = core_ref[0]
    for y in range(4):
        rows = pl.ds(32 * y, 32)
        for x in range(2):
            a = 4 * x + y
            for t in range(4):
                part = slice(32 * t, 32 * t + 32)
                at = pl.multiple_of(1024 * core + 512 * x + HS * t, HS)
                out.ref[rows, pl.ds(at, HS)] = mine_ref[a, part].astype(F32)
                at = pl.multiple_of(1024 * (1 - core) + 512 * x + HS * t, HS)
                out.ref[rows, pl.ds(at, HS)] = other_ref[a, part].astype(F32)
        out.push(rows)


def exchange(operand):
    return lax.all_to_all(
        operand, "ctx", split_axis=0, concat_axis=0, tiled=True, axis_index_groups=SAME_CORE
    )


def after(value, *others):
    return lax.optimization_barrier((value, *others))[0]


def shards(query_rows, key_rows, value_rows, session, lengths, out_weight, upstream):
    index = lax.axis_index("ctx").astype(jnp.int32)
    core = index & 1
    core_ref = core.reshape(1)
    high_ref = (index >> 3).reshape(1)
    row_ref = lax.axis_index("fsdp").astype(jnp.int32).reshape(1)
    valid_len = lengths[0]
    width = out_weight.shape[1]
    half = width // 2
    quarter = half // 2

    side = ("R", (BLOCK, half), BF16)
    part = ("R", (BLOCK, quarter), BF16)
    packed, own_half, up_mine, up_send, up_pair, up_diag = call(
        pack_kernel,
        [
            ("S", core_ref), ("S", high_ref), ("H", query_rows, 0), ("H", key_rows, 0),
            ("H", value_rows, 0), ("H", out_weight), ("H", upstream, 0),
        ],
        [("R", (HEADS, 3, BLOCK, HS), BF16), ("R", (HS, half), BF16), side, side, part, part],
    )
    own = exchange(packed)

    session_ids = session[0]
    positions = jnp.arange(LEN, dtype=jnp.int32).reshape(CHIPS, 2, BLOCK)
    own_sessions = lax.dynamic_index_in_dim(session_ids.reshape(CHIPS, 2, BLOCK), core, 1, False)
    own_positions = lax.dynamic_index_in_dim(positions, core, 1, False)
    end = jnp.sum(
        (session_ids[:, None] <= own_sessions.reshape(1, -1)).astype(jnp.int32), axis=0
    )
    end = jnp.minimum(end, valid_len).reshape(4, 1, TILE)
    valid = (own_positions < valid_len).astype(F32).reshape(4, 1, TILE)
    rows_here = index * BLOCK + jnp.arange(BLOCK, dtype=jnp.int32)
    valid_here = (rows_here < valid_len).astype(F32)[:, None]

    def step(value, s):
        return lax.ppermute(value, "fsdp", [(i, i ^ s) for i in range(8)])

    over = step(own_half, 4)
    own_half = after(own_half, end)
    one, three = step(own_half, 1), step(own_half, 3)
    over_three = step(over, 3)
    up_other = lax.ppermute(up_send, "ctx", CORE_SWAP)
    up_pair = lax.ppermute(after(up_pair, over), "ctx", PAIR_SWAP)

    own = after(own, end, valid, valid_here, one, three, over_three, up_other, up_pair)
    over_one = step(after(over, own), 1)
    two, over_two = step(one, 3), step(over_three, 1)
    pieces = [own_half, one, two, three, over, over_one, over_two, over_three]
    other = lax.ppermute(own, "ctx", CORE_SWAP)
    pairs = 4 * TILE * SPAN * 5 // 2
    rows = ("H", (LEN, HS), BF16)
    context, lse, query, key, value = call(
        forward_kernel,
        [
            ("S", core_ref), ("A", own, (slice(None), 0)), ("A", own, (slice(None), 1)),
            ("A", own, (slice(None), 2)), ("V", other), ("V", end), ("V", valid),
        ],
        [
            ("H", (CHIPS, 2, BLOCK, HS), BF16),
            ("H", (4, 1, TILE), F32),
            ("H", (CHIPS, BLOCK, HS), BF16),
            rows,
            rows,
        ],
        scratch=(pltpu.VMEM((LEN, TILE), F32),),
        flops=4 * pairs * HS,
    )
    context_mine = exchange(context)
    up_diag = lax.ppermute(after(up_diag, context), "ctx", DIAG_SWAP)
    grads_keep, grads_send = call(
        project_kernel,
        [("S", row_ref), ("A", up_mine), ("A", up_other), *[("V", piece) for piece in pieces]],
        [("V", (HEADS, BLOCK, HS), F32), ("V", (HEADS, BLOCK, HS), BF16)],
        flops=2 * 256 * 1024 * 1024,
    )
    grads_came = lax.ppermute(grads_send, "ctx", CORE_SWAP)
    grads = call(
        add_kernel,
        [("V", valid_here), ("V", grads_keep), ("V", grads_came)],
        [("V", (HEADS, BLOCK, HS), BF16)],
    )
    context_mine = after(context_mine, grads, up_diag)
    context_other = lax.ppermute(context_mine, "ctx", CORE_SWAP)
    terms = call(
        weight_kernel,
        [
            ("S", high_ref), ("A", up_mine), ("A", up_other), ("A", up_pair), ("A", up_diag),
            ("A", context_mine), ("A", context_other),
        ],
        [("H", (32, 32, quarter), BF16)],
        flops=2 * 512 * 1024 * 512,
    )
    grads = exchange(after(grads, context_mine))
    terms = lax.all_to_all(
        after(terms, grads),
        ("ctx", "fsdp"),
        split_axis=0,
        concat_axis=0,
        tiled=True,
        axis_index_groups=REDUCE,
    )
    dq, keep, send = call(
        backward_kernel,
        [
            ("S", core_ref), ("H", query), ("H", key), ("H", grads), ("H", value),
            ("H", context, (slice(None), 0)), ("A", end), ("H", lse),
        ],
        [
            ("H", (CHIPS, BLOCK, HS), BF16),
            ("H", (CHIPS, 2, BLOCK, HS), F32),
            ("H", (CHIPS, 2, BLOCK, HS), BF16),
        ],
        scratch=(pltpu.VMEM((LEN, HS), F32), pltpu.VMEM((LEN, HS), F32)),
        flops=10 * pairs * HS,
    )
    came = lax.ppermute(send, "ctx", CORE_SWAP)
    joined = call(
        join_kernel,
        [("A", dq), ("A", keep), ("A", came)],
        [("R", (CHIPS, 4, BLOCK, HS), BF16)],
        scratch=(pltpu.VMEM((CHIPS, 3, BLOCK, HS), BF16),),
    )
    joined = call(
        total_kernel,
        [("R", joined), ("V", terms)],
        [("R", (CHIPS, 4, BLOCK, HS), BF16)],
        scratch=(pltpu.VMEM((BLOCK, HS), BF16),),
        aliases={0: 0},
    )
    side = ("H", (BLOCK, half), BF16)
    attended_keep, attended_send = call(
        attend_kernel,
        [
            ("S", row_ref), ("A", after(context_mine, joined), (slice(None), 0)),
            ("A", context_other, (slice(None), 0)), *[("A", piece) for piece in pieces],
        ],
        [side, side],
        flops=2 * 256 * 1024 * 1024,
    )
    attended_came = lax.ppermute(attended_send, "ctx", CORE_SWAP)
    attended = call(
        place_kernel,
        [("S", core_ref), ("A", attended_keep), ("A", attended_came)],
        [("R", (1, BLOCK, width), BF16)],
    )
    result = after(exchange(joined), attended)
    weight_mine = result[:, 3]
    weight_other = lax.ppermute(weight_mine, "ctx", CORE_SWAP)
    grad = ("R", (1, BLOCK, HEADS * HS), BF16)
    query_grad, key_grad, value_grad = call(unpack_kernel, [("V", result)], [grad, grad, grad])
    weight_grad = call(
        widen_kernel,
        [("S", core_ref), ("V", weight_mine), ("V", weight_other)],
        [("H", (HS, width), F32)],
    )
    return (attended, query_grad, key_grad, value_grad, weight_grad)


def solution(mesh):
    rows = P("fsdp", "ctx", None)
    return jax.shard_map(
        shards,
        mesh=mesh,
        in_specs=(rows, rows, rows, P("fsdp", None), P("fsdp"), P("fsdp", None), rows),
        out_specs=(rows, rows, rows, rows, P("fsdp", None)),
        check_vma=False,
    )
```

```python
import functools
import math

import jax
import jax.numpy as jnp
from jax import lax
from jax.experimental import pallas as pl
from jax.experimental.pallas import tpu as pltpu
from jax.sharding import PartitionSpec as P

HEADS = 8
HS = 128
BLOCK = 128
TILE = 256
SPAN = 512
REACH = 128
CHIPS = 8
LEN = 2048
NEG = -1e30
SEMS = 48
SCALE = 1.0 / math.sqrt(HS)
SCALE2 = SCALE * math.log2(math.e)
F32 = jnp.float32
BF16 = jnp.bfloat16

CORE_SWAP = [(i, i ^ 1) for i in range(16)]
PAIR_SWAP = [(i, i ^ 8) for i in range(16)]
SAME_CORE = [[2 * j + c for j in range(CHIPS)] for c in range(2)]
REDUCE = [
    [(8 * h + 2 * y + c) * 8 + f for f in range(8) for y in range(4)]
    for h in range(2)
    for c in range(2)
]


def dot_nt(a, b):
    return lax.dot_general(a, b, (((1,), (1,)), ((), ())), preferred_element_type=F32)


def dot_tn(a, b):
    return lax.dot_general(a, b, (((0,), (0,)), ((), ())), preferred_element_type=F32)


def dot_nn(a, b):
    return lax.dot_general(a, b, (((1,), (0,)), ((), ())), preferred_element_type=F32)


class Load:
    def __init__(self, copy, ref):
        self.copy, self.ref, self.done = copy, ref, False

    def get(self):
        if not self.done:
            self.copy.wait()
            self.done = True
        return self.ref


class Store:
    def __init__(self, hbm, ref, sems):
        self.hbm, self.ref, self.sems, self.copies = hbm, ref, sems, []

    def push(self, *index):
        src = self.ref.at[index] if index else self.ref
        dst = self.hbm.at[index] if index else self.hbm
        copy = pltpu.make_async_copy(src, dst, next(self.sems))
        copy.start()
        self.copies.append(copy)


SPACES = {"S": pltpu.SMEM, "V": pltpu.VMEM, "H": pltpu.HBM, "A": pl.ANY, "R": pltpu.HBM}


def call(kernel, ins, outs, scratch=(), flops=0, mib=14, aliases=None):
    copied = [
        pltpu.VMEM(jax.eval_shape(lambda x: x[i[2]] if len(i) > 2 else x, i[1]).shape, i[1].dtype)
        for i in ins
        if i[0] in "HA"
    ] + [pltpu.VMEM(o[1], o[2]) for o in outs if o[0] == "H"]

    def body(*refs):
        refs = list(refs)
        in_refs = [refs.pop(0) for _ in ins]
        out_refs = [refs.pop(0) for _ in outs]
        sem_ref = refs.pop(0)
        buffers = [refs.pop(0) for _ in copied]
        sems = (sem_ref.at[n] for n in range(SEMS))
        given, made = [], []
        for one, ref in zip(ins, in_refs):
            if one[0] in "HA":
                buffer = buffers.pop(0)
                copy = pltpu.make_async_copy(
                    ref.at[one[2]] if len(one) > 2 else ref, buffer, next(sems)
                )
                copy.start()
                ref = Load(copy, buffer)
            given.append(ref)
        for one, ref in zip(outs, out_refs):
            made.append(Store(ref, buffers.pop(0), sems) if one[0] == "H" else ref)
        more = kernel(given, made, refs, sems) or []
        for one in given:
            if isinstance(one, Load):
                one.get()
        for one in made:
            if isinstance(one, Store):
                for copy in one.copies:
                    copy.wait()
        for copy in more:
            copy.wait()

    result = pl.pallas_call(
        body,
        out_shape=[
            SPACES[o[0]](o[1], o[2]) if o[0] in "HR" else jax.ShapeDtypeStruct(o[1], o[2])
            for o in outs
        ],
        in_specs=[pl.BlockSpec(memory_space=SPACES[i[0]]) for i in ins],
        out_specs=[pl.BlockSpec(memory_space=SPACES[o[0]]) for o in outs],
        scratch_shapes=[pltpu.SemaphoreType.DMA((SEMS,)), *copied, *scratch],
        input_output_aliases=aliases or {},
        compiler_params=pltpu.CompilerParams(vmem_limit_bytes=mib * 1024 * 1024),
        cost_estimate=pl.CostEstimate(flops=flops, bytes_accessed=2_000_000, transcendentals=0),
    )(*[
        pltpu.with_memory_space_constraint(i[1], pltpu.HBM) if i[0] in "HR" else i[1] for i in ins
    ])
    return result[0] if len(outs) == 1 else result


def pack_kernel(ins, outs, scratch, sems):
    core_ref, *data = ins
    out_ref, half_ref, up_mine_ref, up_send_ref = outs
    core = core_ref[0]
    half = half_ref.shape[1]
    copies = []

    def copy(src, dst):
        copies.append(pltpu.make_async_copy(src, dst, next(sems)))
        copies[-1].start()

    mine = pl.ds(pl.multiple_of(core * half, half), half)
    other = pl.ds(pl.multiple_of((1 - core) * half, half), half)
    copy(data[3].get().at[:, mine], half_ref)
    for i in range(3):
        ref = data[i].get()
        for a in range(HEADS):
            copy(ref.at[:, pl.ds(a * HS, HS)], out_ref.at[a, i])
    up_ref = data[4].get()
    copy(up_ref.at[:, mine], up_mine_ref)
    copy(up_ref.at[:, other], up_send_ref)
    return copies


def quarter_kernel(ins, outs, scratch, sems):
    high_ref, mine_in, other_in = ins
    out = outs[0]
    quarter = out.shape[1]
    at = pl.ds(pl.multiple_of((1 - high_ref[0]) * quarter, quarter), quarter)
    copies = []
    for n, one in enumerate((mine_in, other_in)):
        copies.append(
            pltpu.make_async_copy(one.get().at[:, at], out.at[pl.ds(n * BLOCK, BLOCK)], next(sems))
        )
        copies[-1].start()
    return copies


def in_order(core, own_ref, other_ref, slot, dst_ref):
    for j in range(CHIPS):
        own = pl.multiple_of(2 * BLOCK * j + BLOCK * core, BLOCK)
        other = pl.multiple_of(2 * BLOCK * j + BLOCK * (1 - core), BLOCK)
        dst_ref[pl.ds(own, BLOCK)] = own_ref[j]
        dst_ref[pl.ds(other, BLOCK)] = other_ref[j, slot]


def chunks_of(m):
    stop = min(SPAN * (m + 1) + REACH, LEN)
    return [(start, min(start + SPAN, stop)) for start in range(0, stop, SPAN)]


def masked_scores(k_s, q, end, m, start, stop):
    scores = dot_nt(k_s[start:stop], q)
    if stop > SPAN * m:
        at = lax.broadcasted_iota(jnp.int32, scores.shape, 0) + start
        scores = jnp.where(at < end, scores, NEG)
    return scores


def forward_kernel(ins, outs, scratch, sems):
    core_ref, q_in, k_in, v_in, other_ref, end_ref, valid_ref = ins
    ctx_out, lse_out, q_out, k_out, v_out = outs
    (s_s,) = scratch
    core = core_ref[0]
    k_s, v_s = k_out.ref, v_out.ref
    in_order(core, k_in.get(), other_ref, 1, k_s)
    k_out.push()
    q_ref = q_in.get()
    q_out.ref[...] = q_ref[...]
    q_out.push()
    in_order(core, v_in.get(), other_ref, 2, v_s)
    v_out.push()
    for m in range(4):
        q = q_ref[2 * m : 2 * m + 2].reshape(TILE, HS)
        end = end_ref[m]
        top = jnp.full((1, TILE), NEG, F32)
        for start, stop in chunks_of(m):
            scores = masked_scores(k_s, q, end, m, start, stop)
            s_s[start:stop] = scores
            top = jnp.maximum(top, jnp.max(scores, axis=0, keepdims=True))
        top2 = top * SCALE2
        total = jnp.zeros((1, TILE), F32)
        acc = jnp.zeros((HS, TILE), F32)
        for start, stop in chunks_of(m):
            p = jnp.exp2(s_s[start:stop] * SCALE2 - top2)
            total = total + jnp.sum(p, axis=0, keepdims=True)
            acc = acc + dot_tn(v_s[start:stop], p.astype(BF16))
        lse_out.ref[m] = top2 + jnp.log2(total)
        ctx = (acc * (valid_ref[m] / total)).T.astype(BF16)
        for t in range(2):
            j = 2 * m + t
            block = ctx[t * BLOCK : (t + 1) * BLOCK]
            ctx_out.ref[j, 0] = block
            ctx_out.ref[j ^ 4, 1] = block
            ctx_out.push(j, 0)
            ctx_out.push(j ^ 4, 1)
    lse_out.push()


def backward_kernel(ins, outs, scratch, sems):
    core_ref, q_in, k_in, grad_in, v_in, ctx_in, end_in, lse_in = ins
    dq_out, keep_out, send_out = outs
    dk_s, dv_s = scratch
    core = core_ref[0]
    dk_s[...] = jnp.zeros(dk_s.shape, F32)
    dv_s[...] = jnp.zeros(dv_s.shape, F32)
    end_ref, lse_ref = end_in.get(), lse_in.get()
    q_ref, k_s = q_in.get(), k_in.get()
    grad_ref, v_s, ctx_ref = grad_in.get(), v_in.get(), ctx_in.get()
    for m in range(3, -1, -1):
        rows = slice(2 * m, 2 * m + 2)
        q = q_ref[rows].reshape(TILE, HS)
        do = grad_ref[rows].reshape(TILE, HS)
        ctx = ctx_ref[rows].reshape(TILE, HS)
        delta = jnp.sum((do.astype(F32) * ctx.astype(F32)).T, axis=0, keepdims=True)
        end = end_ref[m]
        lse = lse_ref[m]
        dq = jnp.zeros((HS, TILE), F32)
        for start, stop in chunks_of(m):
            scores = masked_scores(k_s, q, end, m, start, stop)
            p = jnp.exp2(scores * SCALE2 - lse)
            dp = dot_nt(v_s[start:stop], do)
            ds = (p * (dp - delta) * SCALE).astype(BF16)
            dv_s[start:stop] += dot_nn(p.astype(BF16), do)
            dk_s[start:stop] += dot_nn(ds, q)
            dq = dq + dot_tn(k_s[start:stop], ds)
        dq_rows = dq.T.astype(BF16)
        dq_out.ref[2 * m] = dq_rows[:BLOCK]
        dq_out.ref[2 * m + 1] = dq_rows[BLOCK:]
        dq_out.push(pl.ds(2 * m, 2))
        first = 2 * m + 1 if m else 0
        last = 2 * m + 3 if m < 3 else CHIPS
        for j in range(first, last):
            own = pl.multiple_of(2 * BLOCK * j + BLOCK * core, BLOCK)
            other = pl.multiple_of(2 * BLOCK * j + BLOCK * (1 - core), BLOCK)
            send_out.ref[j, 0] = dk_s[pl.ds(other, BLOCK)].astype(BF16)
            send_out.ref[j, 1] = dv_s[pl.ds(other, BLOCK)].astype(BF16)
            send_out.push(j)
            keep_out.ref[j, 0] = dk_s[pl.ds(own, BLOCK)]
            keep_out.ref[j, 1] = dv_s[pl.ds(own, BLOCK)]
            keep_out.push(j)


def project_kernel(ins, outs, scratch, sems):
    row_ref, up_in, up_other_in, *pieces = ins
    keep_ref, send_ref = outs
    row = row_ref[0]
    up = jnp.concatenate([up_in.get()[...], up_other_in.get()[...]], axis=0)
    for s in range(HEADS):
        total = dot_nt(up, pieces[s][...])
        at = jnp.bitwise_xor(row, s)
        keep_ref[at] = total[:BLOCK]
        send_ref[at] = total[BLOCK:].astype(BF16)


def add_kernel(ins, outs, scratch, sems):
    valid_ref, keep_ref, came_ref = ins
    outs[0][...] = ((keep_ref[...] + came_ref[...].astype(F32)) * valid_ref[...]).astype(BF16)


def attend_kernel(ins, outs, scratch, sems):
    row_ref, ctx_in, ctx_other_in, *pieces = ins
    keep, send = outs
    row = row_ref[0]
    order = [jnp.bitwise_xor(row, s) for s in range(HEADS)]
    ctx_ref, ctx_other_ref = ctx_in.get(), ctx_other_in.get()
    ctx = jnp.concatenate(
        [
            jnp.concatenate([ctx_ref[a] for a in order], axis=1),
            jnp.concatenate([ctx_other_ref[a] for a in order], axis=1),
        ],
        axis=0,
    )
    pieces = [piece.get() for piece in pieces]
    for n in range(4):
        cols = slice(n * TILE, (n + 1) * TILE)
        weight = jnp.concatenate([piece[:, cols] for piece in pieces], axis=0)
        total = dot_nn(ctx, weight).astype(BF16)
        keep.ref[:, cols] = total[:BLOCK]
        send.ref[:, cols] = total[BLOCK:]
    send.push()
    keep.push()


def place_kernel(ins, outs, scratch, sems):
    core_ref, keep_in, came_in = ins
    core = core_ref[0]
    half = keep_in.ref.shape[1]
    copies = []
    for one, c in ((keep_in, core), (came_in, 1 - core)):
        at = pl.ds(pl.multiple_of(c * half, half), half)
        copies.append(pltpu.make_async_copy(one.get(), outs[0].at[0, :, at], next(sems)))
        copies[-1].start()
    return copies


def weight_kernel(ins, outs, scratch, sems):
    out = outs[0]
    high_ref = ins[0]
    mine, other, pair, ctx_ref, ctx_other_ref = [one.get() for one in ins[1:]]
    quarter = pair.shape[1]
    at = pl.ds(pl.multiple_of(high_ref[0] * quarter, quarter), quarter)
    up = jnp.concatenate([mine[:, at], pair[:BLOCK]], axis=0)
    up_other = jnp.concatenate([other[:, at], pair[BLOCK:]], axis=0)
    for a in range(HEADS):
        total = dot_tn(ctx_ref[a].reshape(TILE, HS), up)
        total = total + dot_tn(ctx_other_ref[a].reshape(TILE, HS), up_other)
        part = pl.ds(4 * a, 4)
        out.ref[part] = total.reshape(4, HS // 4, quarter).astype(BF16)
        out.push(part)


def join_kernel(ins, outs, scratch, sems):
    dq_in, keep_in, came_in = ins
    (made,) = scratch
    copies = []
    dq_ref, keep_ref, came_ref = dq_in.get(), keep_in.get(), came_in.get()
    for j in range(CHIPS):
        made[j, 0] = dq_ref[j]
        made[j, 1] = (keep_ref[j, 0] + came_ref[j, 0].astype(F32)).astype(BF16)
        made[j, 2] = (keep_ref[j, 1] + came_ref[j, 1].astype(F32)).astype(BF16)
        copies.append(
            pltpu.make_async_copy(made.at[j], outs[0].at[j, pl.ds(0, 3)], next(sems))
        )
        copies[-1].start()
    return copies


def total_kernel(ins, outs, scratch, sems):
    terms_ref = ins[1]
    (made,) = scratch
    total = terms_ref[0].astype(F32)
    for s in range(1, terms_ref.shape[0]):
        total = total + terms_ref[s].astype(F32)
    weight = total.astype(BF16)
    rows = weight.shape[0]
    for t in range(4):
        made[t * rows : (t + 1) * rows] = weight[:, t * HS : (t + 1) * HS]
    copies = []
    for j in range(CHIPS):
        copies.append(pltpu.make_async_copy(made, outs[0].at[j, 3], next(sems)))
        copies[-1].start()
    return copies


def unpack_kernel(ins, outs, scratch, sems):
    mine_ref = ins[0]
    copies = []
    for a in range(HEADS):
        for i in range(3):
            dst = outs[i].at[0, :, pl.ds(a * HS, HS)]
            copies.append(pltpu.make_async_copy(mine_ref.at[a, i], dst, next(sems)))
            copies[-1].start()
    return copies


def widen_kernel(ins, outs, scratch, sems):
    core_ref, mine_ref, other_ref = ins
    out = outs[0]
    core = core_ref[0]
    for y in range(4):
        rows = pl.ds(32 * y, 32)
        for x in range(2):
            a = 4 * x + y
            for t in range(4):
                part = slice(32 * t, 32 * t + 32)
                at = pl.multiple_of(1024 * core + 512 * x + HS * t, HS)
                out.ref[rows, pl.ds(at, HS)] = mine_ref[a, part].astype(F32)
                at = pl.multiple_of(1024 * (1 - core) + 512 * x + HS * t, HS)
                out.ref[rows, pl.ds(at, HS)] = other_ref[a, part].astype(F32)
        out.push(rows)


def exchange(operand):
    return lax.all_to_all(
        operand, "ctx", split_axis=0, concat_axis=0, tiled=True, axis_index_groups=SAME_CORE
    )


def after(value, *others):
    return lax.optimization_barrier((value, *others))[0]


def shards(query_rows, key_rows, value_rows, session, lengths, out_weight, upstream):
    index = lax.axis_index("ctx").astype(jnp.int32)
    core = index & 1
    core_ref = core.reshape(1)
    high_ref = (index >> 3).reshape(1)
    row_ref = lax.axis_index("fsdp").astype(jnp.int32).reshape(1)
    valid_len = lengths[0]
    width = out_weight.shape[1]
    half = width // 2
    quarter = half // 2

    side = ("R", (BLOCK, half), BF16)
    packed, own_half, up_mine, up_send = call(
        pack_kernel,
        [
            ("S", core_ref), ("H", query_rows, 0), ("H", key_rows, 0),
            ("H", value_rows, 0), ("H", out_weight), ("H", upstream, 0),
        ],
        [("R", (HEADS, 3, BLOCK, HS), BF16), side, side, side],
    )
    own = exchange(packed)

    session_ids = session[0]
    positions = jnp.arange(LEN, dtype=jnp.int32).reshape(CHIPS, 2, BLOCK)
    own_sessions = lax.dynamic_index_in_dim(session_ids.reshape(CHIPS, 2, BLOCK), core, 1, False)
    own_positions = lax.dynamic_index_in_dim(positions, core, 1, False)
    end = jnp.sum(
        (session_ids[:, None] <= own_sessions.reshape(1, -1)).astype(jnp.int32), axis=0
    )
    end = jnp.minimum(end, valid_len).reshape(4, 1, TILE)
    valid = (own_positions < valid_len).astype(F32).reshape(4, 1, TILE)
    rows_here = index * BLOCK + jnp.arange(BLOCK, dtype=jnp.int32)
    valid_here = (rows_here < valid_len).astype(F32)[:, None]

    def step(value, s):
        return lax.ppermute(value, "fsdp", [(i, i ^ s) for i in range(8)])

    over = step(own_half, 4)
    one, three = step(own_half, 1), step(own_half, 3)
    over_one, over_three = step(over, 1), step(over, 3)
    two, over_two = step(one, 3), step(over_three, 1)
    pieces = [own_half, one, two, three, over, over_one, over_two, over_three]
    up_other = lax.ppermute(up_send, "ctx", CORE_SWAP)
    up_pair = call(
        quarter_kernel,
        [("S", high_ref), ("A", up_mine), ("A", up_other)],
        [("R", (2 * BLOCK, quarter), BF16)],
    )
    up_pair = lax.ppermute(after(up_pair, over), "ctx", PAIR_SWAP)

    own = after(
        own, end, valid, valid_here, one, three, over_one, over_three, up_other, up_pair
    )
    other = lax.ppermute(own, "ctx", CORE_SWAP)
    pairs = 4 * TILE * SPAN * 5 // 2
    rows = ("H", (LEN, HS), BF16)
    context, lse, query, key, value = call(
        forward_kernel,
        [
            ("S", core_ref), ("A", own, (slice(None), 0)), ("A", own, (slice(None), 1)),
            ("A", own, (slice(None), 2)), ("V", other), ("V", end), ("V", valid),
        ],
        [
            ("H", (CHIPS, 2, BLOCK, HS), BF16),
            ("H", (4, 1, TILE), F32),
            ("H", (CHIPS, BLOCK, HS), BF16),
            rows,
            rows,
        ],
        scratch=(pltpu.VMEM((LEN, TILE), F32),),
        flops=4 * pairs * HS,
    )
    context_mine = exchange(context)
    grads_keep, grads_send = call(
        project_kernel,
        [("S", row_ref), ("A", up_mine), ("A", up_other), *[("V", piece) for piece in pieces]],
        [("V", (HEADS, BLOCK, HS), F32), ("V", (HEADS, BLOCK, HS), BF16)],
        flops=2 * 256 * 1024 * 1024,
    )
    grads_came = lax.ppermute(grads_send, "ctx", CORE_SWAP)
    grads = call(
        add_kernel,
        [("V", valid_here), ("V", grads_keep), ("V", grads_came)],
        [("V", (HEADS, BLOCK, HS), BF16)],
    )
    context_mine = after(context_mine, grads)
    context_other = lax.ppermute(context_mine, "ctx", CORE_SWAP)
    terms = call(
        weight_kernel,
        [
            ("S", high_ref), ("A", up_mine), ("A", up_other), ("A", up_pair),
            ("A", context_mine), ("A", context_other),
        ],
        [("H", (32, 32, quarter), BF16)],
        flops=2 * 512 * 1024 * 512,
    )
    grads = exchange(after(grads, context_mine))
    terms = lax.all_to_all(
        after(terms, grads),
        ("ctx", "fsdp"),
        split_axis=0,
        concat_axis=0,
        tiled=True,
        axis_index_groups=REDUCE,
    )
    dq, keep, send = call(
        backward_kernel,
        [
            ("S", core_ref), ("H", query), ("H", key), ("H", grads), ("H", value),
            ("H", context, (slice(None), 0)), ("A", end), ("H", lse),
        ],
        [
            ("H", (CHIPS, BLOCK, HS), BF16),
            ("H", (CHIPS, 2, BLOCK, HS), F32),
            ("H", (CHIPS, 2, BLOCK, HS), BF16),
        ],
        scratch=(pltpu.VMEM((LEN, HS), F32), pltpu.VMEM((LEN, HS), F32)),
        flops=10 * pairs * HS,
    )
    came = lax.ppermute(send, "ctx", CORE_SWAP)
    joined = call(
        join_kernel,
        [("A", dq), ("A", keep), ("A", came)],
        [("R", (CHIPS, 4, BLOCK, HS), BF16)],
        scratch=(pltpu.VMEM((CHIPS, 3, BLOCK, HS), BF16),),
    )
    joined = call(
        total_kernel,
        [("R", joined), ("V", terms)],
        [("R", (CHIPS, 4, BLOCK, HS), BF16)],
        scratch=(pltpu.VMEM((BLOCK, HS), BF16),),
        aliases={0: 0},
    )
    side = ("H", (BLOCK, half), BF16)
    attended_keep, attended_send = call(
        attend_kernel,
        [
            ("S", row_ref), ("A", after(context_mine, joined), (slice(None), 0)),
            ("A", context_other, (slice(None), 0)), *[("A", piece) for piece in pieces],
        ],
        [side, side],
        flops=2 * 256 * 1024 * 1024,
    )
    attended_came = lax.ppermute(attended_send, "ctx", CORE_SWAP)
    attended = call(
        place_kernel,
        [("S", core_ref), ("A", attended_keep), ("A", attended_came)],
        [("R", (1, BLOCK, width), BF16)],
    )
    result = after(exchange(joined), attended)
    weight_mine = result[:, 3]
    weight_other = lax.ppermute(weight_mine, "ctx", CORE_SWAP)
    grad = ("R", (1, BLOCK, HEADS * HS), BF16)
    query_grad, key_grad, value_grad = call(unpack_kernel, [("V", result)], [grad, grad, grad])
    weight_grad = call(
        widen_kernel,
        [("S", core_ref), ("V", weight_mine), ("V", weight_other)],
        [("H", (HS, width), F32)],
    )
    return (attended, query_grad, key_grad, value_grad, weight_grad)


def solution(mesh):
    rows = P("fsdp", "ctx", None)
    return jax.shard_map(
        shards,
        mesh=mesh,
        in_specs=(rows, rows, rows, P("fsdp", None), P("fsdp"), P("fsdp", None), rows),
        out_specs=(rows, rows, rows, rows, P("fsdp", None)),
        check_vma=False,
    )
```

```python
import functools
import math

import jax
import jax.numpy as jnp
from jax import lax
from jax.experimental import pallas as pl
from jax.experimental.pallas import tpu as pltpu
from jax.sharding import PartitionSpec as P

HEADS = 8
HS = 128
BLOCK = 128
TILE = 256
SPAN = 512
REACH = 128
CHIPS = 8
LEN = 2048
NEG = -1e30
SEMS = 48
SCALE = 1.0 / math.sqrt(HS)
SCALE2 = SCALE * math.log2(math.e)
F32 = jnp.float32
BF16 = jnp.bfloat16

CORE_SWAP = [(i, i ^ 1) for i in range(16)]
PAIR_SWAP = [(i, i ^ 8) for i in range(16)]
SAME_CORE = [[2 * j + c for j in range(CHIPS)] for c in range(2)]
REDUCE = [
    [(8 * h + 2 * y + c) * 8 + f for f in range(8) for y in range(4)]
    for h in range(2)
    for c in range(2)
]


def dot_nt(a, b):
    return lax.dot_general(a, b, (((1,), (1,)), ((), ())), preferred_element_type=F32)


def dot_tn(a, b):
    return lax.dot_general(a, b, (((0,), (0,)), ((), ())), preferred_element_type=F32)


def dot_nn(a, b):
    return lax.dot_general(a, b, (((1,), (0,)), ((), ())), preferred_element_type=F32)


class Load:
    def __init__(self, copy, ref):
        self.copy, self.ref, self.done = copy, ref, False

    def get(self):
        if not self.done:
            self.copy.wait()
            self.done = True
        return self.ref


class Store:
    def __init__(self, hbm, ref, sems):
        self.hbm, self.ref, self.sems, self.copies = hbm, ref, sems, []

    def push(self, *index):
        src = self.ref.at[index] if index else self.ref
        dst = self.hbm.at[index] if index else self.hbm
        copy = pltpu.make_async_copy(src, dst, next(self.sems))
        copy.start()
        self.copies.append(copy)


SPACES = {"S": pltpu.SMEM, "V": pltpu.VMEM, "H": pltpu.HBM, "A": pl.ANY, "R": pltpu.HBM}


def call(kernel, ins, outs, scratch=(), flops=0, mib=14, aliases=None):
    copied = [
        pltpu.VMEM(jax.eval_shape(lambda x: x[i[2]] if len(i) > 2 else x, i[1]).shape, i[1].dtype)
        for i in ins
        if i[0] in "HA"
    ] + [pltpu.VMEM(o[1], o[2]) for o in outs if o[0] == "H"]

    def body(*refs):
        refs = list(refs)
        in_refs = [refs.pop(0) for _ in ins]
        out_refs = [refs.pop(0) for _ in outs]
        sem_ref = refs.pop(0)
        buffers = [refs.pop(0) for _ in copied]
        sems = (sem_ref.at[n] for n in range(SEMS))
        given, made = [], []
        for one, ref in zip(ins, in_refs):
            if one[0] in "HA":
                buffer = buffers.pop(0)
                copy = pltpu.make_async_copy(
                    ref.at[one[2]] if len(one) > 2 else ref, buffer, next(sems)
                )
                copy.start()
                ref = Load(copy, buffer)
            given.append(ref)
        for one, ref in zip(outs, out_refs):
            made.append(Store(ref, buffers.pop(0), sems) if one[0] == "H" else ref)
        more = kernel(given, made, refs, sems) or []
        for one in given:
            if isinstance(one, Load):
                one.get()
        for one in made:
            if isinstance(one, Store):
                for copy in one.copies:
                    copy.wait()
        for copy in more:
            copy.wait()

    result = pl.pallas_call(
        body,
        out_shape=[
            SPACES[o[0]](o[1], o[2]) if o[0] in "HR" else jax.ShapeDtypeStruct(o[1], o[2])
            for o in outs
        ],
        in_specs=[pl.BlockSpec(memory_space=SPACES[i[0]]) for i in ins],
        out_specs=[pl.BlockSpec(memory_space=SPACES[o[0]]) for o in outs],
        scratch_shapes=[pltpu.SemaphoreType.DMA((SEMS,)), *copied, *scratch],
        input_output_aliases=aliases or {},
        compiler_params=pltpu.CompilerParams(vmem_limit_bytes=mib * 1024 * 1024),
        cost_estimate=pl.CostEstimate(flops=flops, bytes_accessed=2_000_000, transcendentals=0),
    )(*[
        pltpu.with_memory_space_constraint(i[1], pltpu.HBM) if i[0] in "HR" else i[1] for i in ins
    ])
    return result[0] if len(outs) == 1 else result


def pack_kernel(ins, outs, scratch, sems):
    core_ref, *data = ins
    out_ref, half_ref, up_mine_ref, up_send_ref = outs
    core = core_ref[0]
    half = half_ref.shape[1]
    copies = []

    def copy(src, dst):
        copies.append(pltpu.make_async_copy(src, dst, next(sems)))
        copies[-1].start()

    mine = pl.ds(pl.multiple_of(core * half, half), half)
    other = pl.ds(pl.multiple_of((1 - core) * half, half), half)
    copy(data[3].get().at[:, mine], half_ref)
    for i in range(3):
        ref = data[i].get()
        for a in range(HEADS):
            copy(ref.at[:, pl.ds(a * HS, HS)], out_ref.at[a, i])
    up_ref = data[4].get()
    copy(up_ref.at[:, mine], up_mine_ref)
    copy(up_ref.at[:, other], up_send_ref)
    return copies


def quarter_kernel(ins, outs, scratch, sems):
    high_ref, mine_in, other_in = ins
    out = outs[0]
    quarter = out.shape[1]
    at = pl.ds(pl.multiple_of((1 - high_ref[0]) * quarter, quarter), quarter)
    copies = []
    for n, one in enumerate((mine_in, other_in)):
        copies.append(
            pltpu.make_async_copy(one.get().at[:, at], out.at[pl.ds(n * BLOCK, BLOCK)], next(sems))
        )
        copies[-1].start()
    return copies


def in_order(core, own_ref, other_ref, slot, dst_ref):
    for j in range(CHIPS):
        own = pl.multiple_of(2 * BLOCK * j + BLOCK * core, BLOCK)
        other = pl.multiple_of(2 * BLOCK * j + BLOCK * (1 - core), BLOCK)
        dst_ref[pl.ds(own, BLOCK)] = own_ref[j]
        dst_ref[pl.ds(other, BLOCK)] = other_ref[j, slot]


def chunks_of(m):
    stop = min(SPAN * (m + 1) + REACH, LEN)
    return [(start, min(start + SPAN, stop)) for start in range(0, stop, SPAN)]


def masked_scores(k_s, q, end, m, start, stop):
    scores = dot_nt(k_s[start:stop], q)
    if stop > SPAN * m:
        at = lax.broadcasted_iota(jnp.int32, scores.shape, 0) + start
        scores = jnp.where(at < end, scores, NEG)
    return scores


def forward_kernel(ins, outs, scratch, sems):
    core_ref, q_in, k_in, v_in, other_ref, end_ref, valid_ref = ins
    ctx_out, lse_out, q_out, k_out, v_out = outs
    (s_s,) = scratch
    core = core_ref[0]
    k_s, v_s = k_out.ref, v_out.ref
    in_order(core, k_in.get(), other_ref, 1, k_s)
    k_out.push()
    q_ref = q_in.get()
    q_out.ref[...] = q_ref[...]
    q_out.push()
    in_order(core, v_in.get(), other_ref, 2, v_s)
    v_out.push()
    for m in range(4):
        q = q_ref[2 * m : 2 * m + 2].reshape(TILE, HS)
        end = end_ref[m]
        top = jnp.full((1, TILE), NEG, F32)
        for start, stop in chunks_of(m):
            scores = masked_scores(k_s, q, end, m, start, stop)
            s_s[start:stop] = scores
            top = jnp.maximum(top, jnp.max(scores, axis=0, keepdims=True))
        top2 = top * SCALE2
        total = jnp.zeros((1, TILE), F32)
        acc = jnp.zeros((HS, TILE), F32)
        for start, stop in chunks_of(m):
            p = jnp.exp2(s_s[start:stop] * SCALE2 - top2)
            total = total + jnp.sum(p, axis=0, keepdims=True)
            acc = acc + dot_tn(v_s[start:stop], p.astype(BF16))
        lse_out.ref[m] = top2 + jnp.log2(total)
        ctx = (acc * (valid_ref[m] / total)).T.astype(BF16)
        for t in range(2):
            j = 2 * m + t
            block = ctx[t * BLOCK : (t + 1) * BLOCK]
            ctx_out.ref[j, 0] = block
            ctx_out.ref[j ^ 4, 1] = block
            ctx_out.push(j, 0)
            ctx_out.push(j ^ 4, 1)
    lse_out.push()


def backward_kernel(ins, outs, scratch, sems):
    core_ref, q_in, k_in, grad_in, v_in, ctx_in, end_in, lse_in = ins
    dq_out, keep_out, send_out = outs
    dk_s, dv_s = scratch
    core = core_ref[0]
    dk_s[...] = jnp.zeros(dk_s.shape, F32)
    dv_s[...] = jnp.zeros(dv_s.shape, F32)
    end_ref, lse_ref = end_in.get(), lse_in.get()
    q_ref, k_s = q_in.get(), k_in.get()
    grad_ref, v_s, ctx_ref = grad_in.get(), v_in.get(), ctx_in.get()
    for m in range(3, -1, -1):
        rows = slice(2 * m, 2 * m + 2)
        q = q_ref[rows].reshape(TILE, HS)
        do = grad_ref[rows].reshape(TILE, HS)
        ctx = ctx_ref[rows].reshape(TILE, HS)
        delta = jnp.sum((do.astype(F32) * ctx.astype(F32)).T, axis=0, keepdims=True)
        end = end_ref[m]
        lse = lse_ref[m]
        dq = jnp.zeros((HS, TILE), F32)
        for start, stop in chunks_of(m):
            scores = masked_scores(k_s, q, end, m, start, stop)
            p = jnp.exp2(scores * SCALE2 - lse)
            dp = dot_nt(v_s[start:stop], do)
            ds = (p * (dp - delta) * SCALE).astype(BF16)
            dv_s[start:stop] += dot_nn(p.astype(BF16), do)
            dk_s[start:stop] += dot_nn(ds, q)
            dq = dq + dot_tn(k_s[start:stop], ds)
        dq_rows = dq.T.astype(BF16)
        dq_out.ref[2 * m] = dq_rows[:BLOCK]
        dq_out.ref[2 * m + 1] = dq_rows[BLOCK:]
        dq_out.push(pl.ds(2 * m, 2))
        first = 2 * m + 1 if m else 0
        last = 2 * m + 3 if m < 3 else CHIPS
        for j in range(first, last):
            own = pl.multiple_of(2 * BLOCK * j + BLOCK * core, BLOCK)
            other = pl.multiple_of(2 * BLOCK * j + BLOCK * (1 - core), BLOCK)
            send_out.ref[j, 0] = dk_s[pl.ds(other, BLOCK)].astype(BF16)
            send_out.ref[j, 1] = dv_s[pl.ds(other, BLOCK)].astype(BF16)
            send_out.push(j)
            keep_out.ref[j, 0] = dk_s[pl.ds(own, BLOCK)]
            keep_out.ref[j, 1] = dv_s[pl.ds(own, BLOCK)]
            keep_out.push(j)


def project_kernel(ins, outs, scratch, sems):
    row_ref, up_in, up_other_in, *pieces = ins
    keep_ref, send_ref = outs
    row = row_ref[0]
    up = jnp.concatenate([up_in.get()[...], up_other_in.get()[...]], axis=0)
    for s in range(HEADS):
        total = dot_nt(up, pieces[s][...])
        at = jnp.bitwise_xor(row, s)
        keep_ref[at] = total[:BLOCK]
        send_ref[at] = total[BLOCK:].astype(BF16)


def add_kernel(ins, outs, scratch, sems):
    valid_ref, keep_ref, came_ref = ins
    outs[0][...] = ((keep_ref[...] + came_ref[...].astype(F32)) * valid_ref[...]).astype(BF16)


def attend_kernel(ins, outs, scratch, sems):
    row_ref, ctx_in, ctx_other_in, *pieces = ins
    keep, send = outs
    row = row_ref[0]
    order = [jnp.bitwise_xor(row, s) for s in range(HEADS)]
    ctx_ref, ctx_other_ref = ctx_in.get(), ctx_other_in.get()
    ctx = jnp.concatenate(
        [
            jnp.concatenate([ctx_ref[a] for a in order], axis=1),
            jnp.concatenate([ctx_other_ref[a] for a in order], axis=1),
        ],
        axis=0,
    )
    pieces = [piece.get() for piece in pieces]
    for n in range(4):
        cols = slice(n * TILE, (n + 1) * TILE)
        weight = jnp.concatenate([piece[:, cols] for piece in pieces], axis=0)
        total = dot_nn(ctx, weight).astype(BF16)
        keep.ref[:, cols] = total[:BLOCK]
        send.ref[:, cols] = total[BLOCK:]
    send.push()
    keep.push()


def place_kernel(ins, outs, scratch, sems):
    core_ref, keep_in, came_in = ins
    core = core_ref[0]
    half = keep_in.ref.shape[1]
    copies = []
    for one, c in ((keep_in, core), (came_in, 1 - core)):
        at = pl.ds(pl.multiple_of(c * half, half), half)
        copies.append(pltpu.make_async_copy(one.get(), outs[0].at[0, :, at], next(sems)))
        copies[-1].start()
    return copies


def weight_kernel(ins, outs, scratch, sems):
    out = outs[0]
    high_ref = ins[0]
    mine, other, pair, ctx_ref, ctx_other_ref = [one.get() for one in ins[1:]]
    quarter = pair.shape[1]
    at = pl.ds(pl.multiple_of(high_ref[0] * quarter, quarter), quarter)
    up = jnp.concatenate([mine[:, at], pair[:BLOCK]], axis=0)
    up_other = jnp.concatenate([other[:, at], pair[BLOCK:]], axis=0)
    for a in range(HEADS):
        total = dot_tn(ctx_ref[a].reshape(TILE, HS), up)
        total = total + dot_tn(ctx_other_ref[a].reshape(TILE, HS), up_other)
        part = pl.ds(4 * a, 4)
        out.ref[part] = total.reshape(4, HS // 4, quarter).astype(BF16)
        out.push(part)


def join_kernel(ins, outs, scratch, sems):
    dq_in, keep_in, came_in = ins
    (made,) = scratch
    copies = []
    dq_ref, keep_ref, came_ref = dq_in.get(), keep_in.get(), came_in.get()
    for j in range(CHIPS):
        made[j, 0] = dq_ref[j]
        made[j, 1] = (keep_ref[j, 0] + came_ref[j, 0].astype(F32)).astype(BF16)
        made[j, 2] = (keep_ref[j, 1] + came_ref[j, 1].astype(F32)).astype(BF16)
        copies.append(
            pltpu.make_async_copy(made.at[j], outs[0].at[j, pl.ds(0, 3)], next(sems))
        )
        copies[-1].start()
    return copies


def total_kernel(ins, outs, scratch, sems):
    terms_ref = ins[1]
    (made,) = scratch
    total = terms_ref[0].astype(F32)
    for s in range(1, terms_ref.shape[0]):
        total = total + terms_ref[s].astype(F32)
    weight = total.astype(BF16)
    rows = weight.shape[0]
    for t in range(4):
        made[t * rows : (t + 1) * rows] = weight[:, t * HS : (t + 1) * HS]
    copies = []
    for j in range(CHIPS):
        copies.append(pltpu.make_async_copy(made, outs[0].at[j, 3], next(sems)))
        copies[-1].start()
    return copies


def unpack_kernel(ins, outs, scratch, sems):
    mine_ref = ins[0]
    copies = []
    for a in range(HEADS):
        for i in range(3):
            dst = outs[i].at[0, :, pl.ds(a * HS, HS)]
            copies.append(pltpu.make_async_copy(mine_ref.at[a, i], dst, next(sems)))
            copies[-1].start()
    return copies


def widen_kernel(ins, outs, scratch, sems):
    core_ref, mine_ref, other_ref = ins
    out = outs[0]
    core = core_ref[0]
    for y in range(4):
        rows = pl.ds(32 * y, 32)
        for x in range(2):
            a = 4 * x + y
            for t in range(4):
                part = slice(32 * t, 32 * t + 32)
                at = pl.multiple_of(1024 * core + 512 * x + HS * t, HS)
                out.ref[rows, pl.ds(at, HS)] = mine_ref[a, part].astype(F32)
                at = pl.multiple_of(1024 * (1 - core) + 512 * x + HS * t, HS)
                out.ref[rows, pl.ds(at, HS)] = other_ref[a, part].astype(F32)
        out.push(rows)


def exchange(operand):
    return lax.all_to_all(
        operand, "ctx", split_axis=0, concat_axis=0, tiled=True, axis_index_groups=SAME_CORE
    )


def after(value, *others):
    return lax.optimization_barrier((value, *others))[0]


def shards(query_rows, key_rows, value_rows, session, lengths, out_weight, upstream):
    index = lax.axis_index("ctx").astype(jnp.int32)
    core = index & 1
    core_ref = core.reshape(1)
    high_ref = (index >> 3).reshape(1)
    row_ref = lax.axis_index("fsdp").astype(jnp.int32).reshape(1)
    valid_len = lengths[0]
    width = out_weight.shape[1]
    half = width // 2
    quarter = half // 2

    side = ("R", (BLOCK, half), BF16)
    packed, own_half, up_mine, up_send = call(
        pack_kernel,
        [
            ("S", core_ref), ("H", query_rows, 0), ("H", key_rows, 0),
            ("H", value_rows, 0), ("H", out_weight), ("H", upstream, 0),
        ],
        [("R", (HEADS, 3, BLOCK, HS), BF16), side, side, side],
    )
    own = exchange(packed)

    session_ids = session[0]
    positions = jnp.arange(LEN, dtype=jnp.int32).reshape(CHIPS, 2, BLOCK)
    own_sessions = lax.dynamic_index_in_dim(session_ids.reshape(CHIPS, 2, BLOCK), core, 1, False)
    own_positions = lax.dynamic_index_in_dim(positions, core, 1, False)
    end = jnp.sum(
        (session_ids[:, None] <= own_sessions.reshape(1, -1)).astype(jnp.int32), axis=0
    )
    end = jnp.minimum(end, valid_len).reshape(4, 1, TILE)
    valid = (own_positions < valid_len).astype(F32).reshape(4, 1, TILE)
    rows_here = index * BLOCK + jnp.arange(BLOCK, dtype=jnp.int32)
    valid_here = (rows_here < valid_len).astype(F32)[:, None]

    def step(value, s):
        return lax.ppermute(value, "fsdp", [(i, i ^ s) for i in range(8)])

    over = step(own_half, 4)
    one, three = step(own_half, 1), step(own_half, 3)
    over_one, over_three = step(over, 1), step(over, 3)
    two, over_two = step(one, 3), step(over_three, 1)
    pieces = [own_half, one, two, three, over, over_one, over_two, over_three]
    up_other = lax.ppermute(up_send, "ctx", CORE_SWAP)
    up_pair = call(
        quarter_kernel,
        [("S", high_ref), ("A", up_mine), ("A", up_other)],
        [("R", (2 * BLOCK, quarter), BF16)],
    )

    own = after(
        own, end, valid, valid_here, one, three, over_one, over_three, up_other, up_pair
    )
    up_pair = lax.ppermute(after(up_pair, own), "ctx", PAIR_SWAP)
    pieces[6] = after(pieces[6], up_pair)
    other = lax.ppermute(own, "ctx", CORE_SWAP)
    pairs = 4 * TILE * SPAN * 5 // 2
    rows = ("H", (LEN, HS), BF16)
    context, lse, query, key, value = call(
        forward_kernel,
        [
            ("S", core_ref), ("A", own, (slice(None), 0)), ("A", own, (slice(None), 1)),
            ("A", own, (slice(None), 2)), ("V", other), ("V", end), ("V", valid),
        ],
        [
            ("H", (CHIPS, 2, BLOCK, HS), BF16),
            ("H", (4, 1, TILE), F32),
            ("H", (CHIPS, BLOCK, HS), BF16),
            rows,
            rows,
        ],
        scratch=(pltpu.VMEM((LEN, TILE), F32),),
        flops=4 * pairs * HS,
    )
    context_mine = exchange(context)
    grads_keep, grads_send = call(
        project_kernel,
        [("S", row_ref), ("A", up_mine), ("A", up_other), *[("V", piece) for piece in pieces]],
        [("V", (HEADS, BLOCK, HS), F32), ("V", (HEADS, BLOCK, HS), BF16)],
        flops=2 * 256 * 1024 * 1024,
    )
    grads_came = lax.ppermute(grads_send, "ctx", CORE_SWAP)
    grads = call(
        add_kernel,
        [("V", valid_here), ("V", grads_keep), ("V", grads_came)],
        [("V", (HEADS, BLOCK, HS), BF16)],
    )
    context_mine = after(context_mine, grads)
    context_other = lax.ppermute(context_mine, "ctx", CORE_SWAP)
    terms = call(
        weight_kernel,
        [
            ("S", high_ref), ("A", up_mine), ("A", up_other), ("A", up_pair),
            ("A", context_mine), ("A", context_other),
        ],
        [("H", (32, 32, quarter), BF16)],
        flops=2 * 512 * 1024 * 512,
    )
    grads = exchange(after(grads, context_mine))
    terms = lax.all_to_all(
        after(terms, grads),
        ("ctx", "fsdp"),
        split_axis=0,
        concat_axis=0,
        tiled=True,
        axis_index_groups=REDUCE,
    )
    dq, keep, send = call(
        backward_kernel,
        [
            ("S", core_ref), ("H", query), ("H", key), ("H", grads), ("H", value),
            ("H", context, (slice(None), 0)), ("A", end), ("H", lse),
        ],
        [
            ("H", (CHIPS, BLOCK, HS), BF16),
            ("H", (CHIPS, 2, BLOCK, HS), F32),
            ("H", (CHIPS, 2, BLOCK, HS), BF16),
        ],
        scratch=(pltpu.VMEM((LEN, HS), F32), pltpu.VMEM((LEN, HS), F32)),
        flops=10 * pairs * HS,
    )
    came = lax.ppermute(send, "ctx", CORE_SWAP)
    joined = call(
        join_kernel,
        [("A", dq), ("A", keep), ("A", came)],
        [("R", (CHIPS, 4, BLOCK, HS), BF16)],
        scratch=(pltpu.VMEM((CHIPS, 3, BLOCK, HS), BF16),),
    )
    joined = call(
        total_kernel,
        [("R", joined), ("V", terms)],
        [("R", (CHIPS, 4, BLOCK, HS), BF16)],
        scratch=(pltpu.VMEM((BLOCK, HS), BF16),),
        aliases={0: 0},
    )
    side = ("H", (BLOCK, half), BF16)
    attended_keep, attended_send = call(
        attend_kernel,
        [
            ("S", row_ref), ("A", after(context_mine, joined), (slice(None), 0)),
            ("A", context_other, (slice(None), 0)), *[("A", piece) for piece in pieces],
        ],
        [side, side],
        flops=2 * 256 * 1024 * 1024,
    )
    attended_came = lax.ppermute(attended_send, "ctx", CORE_SWAP)
    attended = call(
        place_kernel,
        [("S", core_ref), ("A", attended_keep), ("A", attended_came)],
        [("R", (1, BLOCK, width), BF16)],
    )
    result = after(exchange(joined), attended)
    weight_mine = result[:, 3]
    weight_other = lax.ppermute(weight_mine, "ctx", CORE_SWAP)
    grad = ("R", (1, BLOCK, HEADS * HS), BF16)
    query_grad, key_grad, value_grad = call(unpack_kernel, [("V", result)], [grad, grad, grad])
    weight_grad = call(
        widen_kernel,
        [("S", core_ref), ("V", weight_mine), ("V", weight_other)],
        [("H", (HS, width), F32)],
    )
    return (attended, query_grad, key_grad, value_grad, weight_grad)


def solution(mesh):
    rows = P("fsdp", "ctx", None)
    return jax.shard_map(
        shards,
        mesh=mesh,
        in_specs=(rows, rows, rows, P("fsdp", None), P("fsdp"), P("fsdp", None), rows),
        out_specs=(rows, rows, rows, rows, P("fsdp", None)),
        check_vma=False,
    )
```

```python
import functools
import math

import jax
import jax.numpy as jnp
from jax import lax
from jax.experimental import pallas as pl
from jax.experimental.pallas import tpu as pltpu
from jax.sharding import PartitionSpec as P

HEADS = 8
HS = 128
BLOCK = 128
TILE = 256
SPAN = 512
REACH = 128
CHIPS = 8
LEN = 2048
NEG = -1e30
SEMS = 48
SCALE = 1.0 / math.sqrt(HS)
SCALE2 = SCALE * math.log2(math.e)
F32 = jnp.float32
BF16 = jnp.bfloat16

CORE_SWAP = [(i, i ^ 1) for i in range(16)]
PAIR_SWAP = [(i, i ^ 8) for i in range(16)]
SAME_CORE = [[2 * j + c for j in range(CHIPS)] for c in range(2)]
REDUCE = [
    [(8 * h + 2 * y + c) * 8 + f for f in range(8) for y in range(4)]
    for h in range(2)
    for c in range(2)
]


def dot_nt(a, b):
    return lax.dot_general(a, b, (((1,), (1,)), ((), ())), preferred_element_type=F32)


def dot_tn(a, b):
    return lax.dot_general(a, b, (((0,), (0,)), ((), ())), preferred_element_type=F32)


def dot_nn(a, b):
    return lax.dot_general(a, b, (((1,), (0,)), ((), ())), preferred_element_type=F32)


class Load:
    def __init__(self, copy, ref):
        self.copy, self.ref, self.done = copy, ref, False

    def get(self):
        if not self.done:
            self.copy.wait()
            self.done = True
        return self.ref


class Store:
    def __init__(self, hbm, ref, sems):
        self.hbm, self.ref, self.sems, self.copies = hbm, ref, sems, []

    def push(self, *index):
        src = self.ref.at[index] if index else self.ref
        dst = self.hbm.at[index] if index else self.hbm
        copy = pltpu.make_async_copy(src, dst, next(self.sems))
        copy.start()
        self.copies.append(copy)


SPACES = {"S": pltpu.SMEM, "V": pltpu.VMEM, "H": pltpu.HBM, "A": pl.ANY, "R": pltpu.HBM}


def call(kernel, ins, outs, scratch=(), flops=0, mib=14, aliases=None):
    copied = [
        pltpu.VMEM(jax.eval_shape(lambda x: x[i[2]] if len(i) > 2 else x, i[1]).shape, i[1].dtype)
        for i in ins
        if i[0] in "HA"
    ] + [pltpu.VMEM(o[1], o[2]) for o in outs if o[0] == "H"]

    def body(*refs):
        refs = list(refs)
        in_refs = [refs.pop(0) for _ in ins]
        out_refs = [refs.pop(0) for _ in outs]
        sem_ref = refs.pop(0)
        buffers = [refs.pop(0) for _ in copied]
        sems = (sem_ref.at[n] for n in range(SEMS))
        given, made = [], []
        for one, ref in zip(ins, in_refs):
            if one[0] in "HA":
                buffer = buffers.pop(0)
                copy = pltpu.make_async_copy(
                    ref.at[one[2]] if len(one) > 2 else ref, buffer, next(sems)
                )
                copy.start()
                ref = Load(copy, buffer)
            given.append(ref)
        for one, ref in zip(outs, out_refs):
            made.append(Store(ref, buffers.pop(0), sems) if one[0] == "H" else ref)
        more = kernel(given, made, refs, sems) or []
        for one in given:
            if isinstance(one, Load):
                one.get()
        for one in made:
            if isinstance(one, Store):
                for copy in one.copies:
                    copy.wait()
        for copy in more:
            copy.wait()

    result = pl.pallas_call(
        body,
        out_shape=[
            SPACES[o[0]](o[1], o[2]) if o[0] in "HR" else jax.ShapeDtypeStruct(o[1], o[2])
            for o in outs
        ],
        in_specs=[pl.BlockSpec(memory_space=SPACES[i[0]]) for i in ins],
        out_specs=[pl.BlockSpec(memory_space=SPACES[o[0]]) for o in outs],
        scratch_shapes=[pltpu.SemaphoreType.DMA((SEMS,)), *copied, *scratch],
        input_output_aliases=aliases or {},
        compiler_params=pltpu.CompilerParams(vmem_limit_bytes=mib * 1024 * 1024),
        cost_estimate=pl.CostEstimate(flops=flops, bytes_accessed=2_000_000, transcendentals=0),
    )(*[
        pltpu.with_memory_space_constraint(i[1], pltpu.HBM) if i[0] in "HR" else i[1] for i in ins
    ])
    return result[0] if len(outs) == 1 else result


def pack_kernel(ins, outs, scratch, sems):
    core_ref, *data = ins
    out_ref, half_ref, up_mine_ref, up_send_ref = outs
    core = core_ref[0]
    half = half_ref.shape[1]
    copies = []

    def copy(src, dst):
        copies.append(pltpu.make_async_copy(src, dst, next(sems)))
        copies[-1].start()

    mine = pl.ds(pl.multiple_of(core * half, half), half)
    other = pl.ds(pl.multiple_of((1 - core) * half, half), half)
    copy(data[3].get().at[:, mine], half_ref)
    for i in range(3):
        ref = data[i].get()
        for a in range(HEADS):
            copy(ref.at[:, pl.ds(a * HS, HS)], out_ref.at[a, i])
    up_ref = data[4].get()
    copy(up_ref.at[:, mine], up_mine_ref)
    copy(up_ref.at[:, other], up_send_ref)
    return copies


def quarter_kernel(ins, outs, scratch, sems):
    high_ref, mine_in, other_in = ins
    out = outs[0]
    quarter = out.shape[1]
    at = pl.ds(pl.multiple_of((1 - high_ref[0]) * quarter, quarter), quarter)
    copies = []
    for n, one in enumerate((mine_in, other_in)):
        copies.append(
            pltpu.make_async_copy(one.get().at[:, at], out.at[pl.ds(n * BLOCK, BLOCK)], next(sems))
        )
        copies[-1].start()
    return copies


def in_order(core, own_ref, other_ref, slot, dst_ref):
    for j in range(CHIPS):
        own = pl.multiple_of(2 * BLOCK * j + BLOCK * core, BLOCK)
        other = pl.multiple_of(2 * BLOCK * j + BLOCK * (1 - core), BLOCK)
        dst_ref[pl.ds(own, BLOCK)] = own_ref[j]
        dst_ref[pl.ds(other, BLOCK)] = other_ref[j, slot]


def chunks_of(m):
    stop = min(SPAN * (m + 1) + REACH, LEN)
    return [(start, min(start + SPAN, stop)) for start in range(0, stop, SPAN)]


def masked_scores(k_s, q, end, m, start, stop):
    scores = dot_nt(k_s[start:stop], q)
    if stop > SPAN * m:
        at = lax.broadcasted_iota(jnp.int32, scores.shape, 0) + start
        scores = jnp.where(at < end, scores, NEG)
    return scores


def forward_kernel(ins, outs, scratch, sems):
    core_ref, q_in, k_in, v_in, other_ref, end_ref, valid_ref = ins
    ctx_out, lse_out, q_out, k_out, v_out = outs
    (s_s,) = scratch
    core = core_ref[0]
    k_s, v_s = k_out.ref, v_out.ref
    in_order(core, k_in.get(), other_ref, 1, k_s)
    k_out.push()
    q_ref = q_in.get()
    q_out.ref[...] = q_ref[...]
    q_out.push()
    in_order(core, v_in.get(), other_ref, 2, v_s)
    v_out.push()
    for m in range(4):
        q = q_ref[2 * m : 2 * m + 2].reshape(TILE, HS)
        end = end_ref[m]
        top = jnp.full((1, TILE), NEG, F32)
        for start, stop in chunks_of(m):
            scores = masked_scores(k_s, q, end, m, start, stop)
            s_s[start:stop] = scores
            top = jnp.maximum(top, jnp.max(scores, axis=0, keepdims=True))
        top2 = top * SCALE2
        total = jnp.zeros((1, TILE), F32)
        acc = jnp.zeros((HS, TILE), F32)
        for start, stop in chunks_of(m):
            p = jnp.exp2(s_s[start:stop] * SCALE2 - top2)
            total = total + jnp.sum(p, axis=0, keepdims=True)
            acc = acc + dot_tn(v_s[start:stop], p.astype(BF16))
        lse_out.ref[m] = top2 + jnp.log2(total)
        ctx = (acc * (valid_ref[m] / total)).T.astype(BF16)
        for t in range(2):
            j = 2 * m + t
            block = ctx[t * BLOCK : (t + 1) * BLOCK]
            ctx_out.ref[j, 0] = block
            ctx_out.ref[j ^ 4, 1] = block
            ctx_out.push(j, 0)
            ctx_out.push(j ^ 4, 1)
    lse_out.push()


def backward_kernel(ins, outs, scratch, sems):
    core_ref, q_in, k_in, grad_in, v_in, ctx_in, end_in, lse_in = ins
    dq_out, keep_out, send_out = outs
    dk_s, dv_s = scratch
    core = core_ref[0]
    dk_s[...] = jnp.zeros(dk_s.shape, F32)
    dv_s[...] = jnp.zeros(dv_s.shape, F32)
    end_ref, lse_ref = end_in.get(), lse_in.get()
    q_ref, k_s = q_in.get(), k_in.get()
    grad_ref, v_s, ctx_ref = grad_in.get(), v_in.get(), ctx_in.get()
    for m in range(3, -1, -1):
        rows = slice(2 * m, 2 * m + 2)
        q = q_ref[rows].reshape(TILE, HS)
        do = grad_ref[rows].reshape(TILE, HS)
        ctx = ctx_ref[rows].reshape(TILE, HS)
        delta = jnp.sum((do.astype(F32) * ctx.astype(F32)).T, axis=0, keepdims=True)
        end = end_ref[m]
        lse = lse_ref[m]
        dq = jnp.zeros((HS, TILE), F32)
        for start, stop in chunks_of(m):
            scores = masked_scores(k_s, q, end, m, start, stop)
            p = jnp.exp2(scores * SCALE2 - lse)
            dp = dot_nt(v_s[start:stop], do)
            ds = (p * (dp - delta) * SCALE).astype(BF16)
            dv_s[start:stop] += dot_nn(p.astype(BF16), do)
            dk_s[start:stop] += dot_nn(ds, q)
            dq = dq + dot_tn(k_s[start:stop], ds)
        dq_rows = dq.T.astype(BF16)
        dq_out.ref[2 * m] = dq_rows[:BLOCK]
        dq_out.ref[2 * m + 1] = dq_rows[BLOCK:]
        dq_out.push(pl.ds(2 * m, 2))
        first = 2 * m + 1 if m else 0
        last = 2 * m + 3 if m < 3 else CHIPS
        for j in range(first, last):
            own = pl.multiple_of(2 * BLOCK * j + BLOCK * core, BLOCK)
            other = pl.multiple_of(2 * BLOCK * j + BLOCK * (1 - core), BLOCK)
            send_out.ref[j, 0] = dk_s[pl.ds(other, BLOCK)].astype(BF16)
            send_out.ref[j, 1] = dv_s[pl.ds(other, BLOCK)].astype(BF16)
            send_out.push(j)
            keep_out.ref[j, 0] = dk_s[pl.ds(own, BLOCK)]
            keep_out.ref[j, 1] = dv_s[pl.ds(own, BLOCK)]
            keep_out.push(j)


def project_kernel(ins, outs, scratch, sems):
    row_ref, up_in, up_other_in, *pieces = ins
    keep_ref, send_ref = outs
    row = row_ref[0]
    up = jnp.concatenate([up_in.get()[...], up_other_in.get()[...]], axis=0)
    for s in range(HEADS):
        total = dot_nt(up, pieces[s][...])
        at = jnp.bitwise_xor(row, s)
        keep_ref[at] = total[:BLOCK]
        send_ref[at] = total[BLOCK:].astype(BF16)


def add_kernel(ins, outs, scratch, sems):
    valid_ref, keep_ref, came_ref = ins
    outs[0][...] = ((keep_ref[...] + came_ref[...].astype(F32)) * valid_ref[...]).astype(BF16)


def attend_kernel(ins, outs, scratch, sems):
    row_ref, ctx_in, ctx_other_in, *pieces = ins
    keep, send = outs
    row = row_ref[0]
    order = [jnp.bitwise_xor(row, s) for s in range(HEADS)]
    ctx_ref, ctx_other_ref = ctx_in.get(), ctx_other_in.get()
    ctx = jnp.concatenate(
        [
            jnp.concatenate([ctx_ref[a] for a in order], axis=1),
            jnp.concatenate([ctx_other_ref[a] for a in order], axis=1),
        ],
        axis=0,
    )
    pieces = [piece.get() for piece in pieces]
    for n in range(4):
        cols = slice(n * TILE, (n + 1) * TILE)
        weight = jnp.concatenate([piece[:, cols] for piece in pieces], axis=0)
        total = dot_nn(ctx, weight).astype(BF16)
        keep.ref[:, cols] = total[:BLOCK]
        send.ref[:, cols] = total[BLOCK:]
    send.push()
    keep.push()


def place_kernel(ins, outs, scratch, sems):
    core_ref, keep_in, came_in = ins
    core = core_ref[0]
    half = keep_in.ref.shape[1]
    copies = []
    for one, c in ((keep_in, core), (came_in, 1 - core)):
        at = pl.ds(pl.multiple_of(c * half, half), half)
        copies.append(pltpu.make_async_copy(one.get(), outs[0].at[0, :, at], next(sems)))
        copies[-1].start()
    return copies


def weight_kernel(ins, outs, scratch, sems):
    out = outs[0]
    high_ref = ins[0]
    mine, other, pair, ctx_ref, ctx_other_ref = [one.get() for one in ins[1:]]
    quarter = pair.shape[1]
    at = pl.ds(pl.multiple_of(high_ref[0] * quarter, quarter), quarter)
    up = jnp.concatenate([mine[:, at], pair[:BLOCK]], axis=0)
    up_other = jnp.concatenate([other[:, at], pair[BLOCK:]], axis=0)
    for a in range(HEADS):
        total = dot_tn(ctx_ref[a].reshape(TILE, HS), up)
        total = total + dot_tn(ctx_other_ref[a].reshape(TILE, HS), up_other)
        part = pl.ds(4 * a, 4)
        out.ref[part] = total.reshape(4, HS // 4, quarter).astype(BF16)
        out.push(part)


def join_kernel(ins, outs, scratch, sems):
    dq_in, keep_in, came_in = ins
    (made,) = scratch
    copies = []
    dq_ref, keep_ref, came_ref = dq_in.get(), keep_in.get(), came_in.get()
    for j in range(CHIPS):
        made[j, 0] = dq_ref[j]
        made[j, 1] = (keep_ref[j, 0] + came_ref[j, 0].astype(F32)).astype(BF16)
        made[j, 2] = (keep_ref[j, 1] + came_ref[j, 1].astype(F32)).astype(BF16)
        copies.append(
            pltpu.make_async_copy(made.at[j], outs[0].at[j, pl.ds(0, 3)], next(sems))
        )
        copies[-1].start()
    return copies


def total_kernel(ins, outs, scratch, sems):
    terms_ref = ins[1]
    (made,) = scratch
    total = terms_ref[0].astype(F32)
    for s in range(1, terms_ref.shape[0]):
        total = total + terms_ref[s].astype(F32)
    weight = total.astype(BF16)
    rows = weight.shape[0]
    for t in range(4):
        made[t * rows : (t + 1) * rows] = weight[:, t * HS : (t + 1) * HS]
    copies = []
    for j in range(CHIPS):
        copies.append(pltpu.make_async_copy(made, outs[0].at[j, 3], next(sems)))
        copies[-1].start()
    return copies


def unpack_kernel(ins, outs, scratch, sems):
    mine_ref = ins[0]
    copies = []
    for a in range(HEADS):
        for i in range(3):
            dst = outs[i].at[0, :, pl.ds(a * HS, HS)]
            copies.append(pltpu.make_async_copy(mine_ref.at[a, i], dst, next(sems)))
            copies[-1].start()
    return copies


def widen_kernel(ins, outs, scratch, sems):
    core_ref, mine_ref, other_ref = ins
    out = outs[0]
    core = core_ref[0]
    for y in range(4):
        rows = pl.ds(32 * y, 32)
        for x in range(2):
            a = 4 * x + y
            for t in range(4):
                part = slice(32 * t, 32 * t + 32)
                at = pl.multiple_of(1024 * core + 512 * x + HS * t, HS)
                out.ref[rows, pl.ds(at, HS)] = mine_ref[a, part].astype(F32)
                at = pl.multiple_of(1024 * (1 - core) + 512 * x + HS * t, HS)
                out.ref[rows, pl.ds(at, HS)] = other_ref[a, part].astype(F32)
        out.push(rows)


def exchange(operand):
    return lax.all_to_all(
        operand, "ctx", split_axis=0, concat_axis=0, tiled=True, axis_index_groups=SAME_CORE
    )


def after(value, *others):
    return lax.optimization_barrier((value, *others))[0]


def shards(query_rows, key_rows, value_rows, session, lengths, out_weight, upstream):
    index = lax.axis_index("ctx").astype(jnp.int32)
    core = index & 1
    core_ref = core.reshape(1)
    high_ref = (index >> 3).reshape(1)
    row_ref = lax.axis_index("fsdp").astype(jnp.int32).reshape(1)
    valid_len = lengths[0]
    width = out_weight.shape[1]
    half = width // 2
    quarter = half // 2

    side = ("R", (BLOCK, half), BF16)
    packed, own_half, up_mine, up_send = call(
        pack_kernel,
        [
            ("S", core_ref), ("H", query_rows, 0), ("H", key_rows, 0),
            ("H", value_rows, 0), ("H", out_weight), ("H", upstream, 0),
        ],
        [("R", (HEADS, 3, BLOCK, HS), BF16), side, side, side],
    )
    own = exchange(packed)

    def step(value, s):
        return lax.ppermute(value, "fsdp", [(i, i ^ s) for i in range(8)])

    over = step(own_half, 4)

    session_ids = after(session[0], over)
    positions = jnp.arange(LEN, dtype=jnp.int32).reshape(CHIPS, 2, BLOCK)
    own_sessions = lax.dynamic_index_in_dim(session_ids.reshape(CHIPS, 2, BLOCK), core, 1, False)
    own_positions = lax.dynamic_index_in_dim(positions, core, 1, False)
    end = jnp.sum(
        (session_ids[:, None] <= own_sessions.reshape(1, -1)).astype(jnp.int32), axis=0
    )
    end = jnp.minimum(end, valid_len).reshape(4, 1, TILE)
    valid = (own_positions < valid_len).astype(F32).reshape(4, 1, TILE)
    rows_here = index * BLOCK + jnp.arange(BLOCK, dtype=jnp.int32)
    valid_here = (rows_here < valid_len).astype(F32)[:, None]

    one, three = step(own_half, 1), step(own_half, 3)
    over_one, over_three = step(over, 1), step(over, 3)
    two, over_two = step(one, 3), step(over_three, 1)
    pieces = [own_half, one, two, three, over, over_one, over_two, over_three]
    up_other = lax.ppermute(after(up_send, over), "ctx", CORE_SWAP)
    up_pair = call(
        quarter_kernel,
        [("S", high_ref), ("A", up_mine), ("A", up_other)],
        [("R", (2 * BLOCK, quarter), BF16)],
    )

    own = after(
        own, end, valid, valid_here, one, three, over_one, over_three, up_other, up_pair
    )
    up_pair = lax.ppermute(after(up_pair, own), "ctx", PAIR_SWAP)
    pieces[6] = after(pieces[6], up_pair)
    other = lax.ppermute(own, "ctx", CORE_SWAP)
    pairs = 4 * TILE * SPAN * 5 // 2
    rows = ("H", (LEN, HS), BF16)
    context, lse, query, key, value = call(
        forward_kernel,
        [
            ("S", core_ref), ("A", own, (slice(None), 0)), ("A", own, (slice(None), 1)),
            ("A", own, (slice(None), 2)), ("V", other), ("V", end), ("V", valid),
        ],
        [
            ("H", (CHIPS, 2, BLOCK, HS), BF16),
            ("H", (4, 1, TILE), F32),
            ("H", (CHIPS, BLOCK, HS), BF16),
            rows,
            rows,
        ],
        scratch=(pltpu.VMEM((LEN, TILE), F32),),
        flops=4 * pairs * HS,
    )
    context_mine = exchange(context)
    grads_keep, grads_send = call(
        project_kernel,
        [("S", row_ref), ("A", up_mine), ("A", up_other), *[("V", piece) for piece in pieces]],
        [("V", (HEADS, BLOCK, HS), F32), ("V", (HEADS, BLOCK, HS), BF16)],
        flops=2 * 256 * 1024 * 1024,
    )
    grads_came = lax.ppermute(grads_send, "ctx", CORE_SWAP)
    grads = call(
        add_kernel,
        [("V", valid_here), ("V", grads_keep), ("V", grads_came)],
        [("V", (HEADS, BLOCK, HS), BF16)],
    )
    context_mine = after(context_mine, grads)
    context_other = lax.ppermute(context_mine, "ctx", CORE_SWAP)
    terms = call(
        weight_kernel,
        [
            ("S", high_ref), ("A", up_mine), ("A", up_other), ("A", up_pair),
            ("A", context_mine), ("A", context_other),
        ],
        [("H", (32, 32, quarter), BF16)],
        flops=2 * 512 * 1024 * 512,
    )
    grads = exchange(after(grads, context_mine))
    terms = lax.all_to_all(
        after(terms, grads),
        ("ctx", "fsdp"),
        split_axis=0,
        concat_axis=0,
        tiled=True,
        axis_index_groups=REDUCE,
    )
    dq, keep, send = call(
        backward_kernel,
        [
            ("S", core_ref), ("H", query), ("H", key), ("H", grads), ("H", value),
            ("H", context, (slice(None), 0)), ("A", end), ("H", lse),
        ],
        [
            ("H", (CHIPS, BLOCK, HS), BF16),
            ("H", (CHIPS, 2, BLOCK, HS), F32),
            ("H", (CHIPS, 2, BLOCK, HS), BF16),
        ],
        scratch=(pltpu.VMEM((LEN, HS), F32), pltpu.VMEM((LEN, HS), F32)),
        flops=10 * pairs * HS,
    )
    came = lax.ppermute(send, "ctx", CORE_SWAP)
    joined = call(
        join_kernel,
        [("A", dq), ("A", keep), ("A", came)],
        [("R", (CHIPS, 4, BLOCK, HS), BF16)],
        scratch=(pltpu.VMEM((CHIPS, 3, BLOCK, HS), BF16),),
    )
    joined = call(
        total_kernel,
        [("R", joined), ("V", terms)],
        [("R", (CHIPS, 4, BLOCK, HS), BF16)],
        scratch=(pltpu.VMEM((BLOCK, HS), BF16),),
        aliases={0: 0},
    )
    side = ("H", (BLOCK, half), BF16)
    attended_keep, attended_send = call(
        attend_kernel,
        [
            ("S", row_ref), ("A", after(context_mine, joined), (slice(None), 0)),
            ("A", context_other, (slice(None), 0)), *[("A", piece) for piece in pieces],
        ],
        [side, side],
        flops=2 * 256 * 1024 * 1024,
    )
    attended_came = lax.ppermute(attended_send, "ctx", CORE_SWAP)
    attended = call(
        place_kernel,
        [("S", core_ref), ("A", attended_keep), ("A", attended_came)],
        [("R", (1, BLOCK, width), BF16)],
    )
    result = after(exchange(joined), attended)
    weight_mine = result[:, 3]
    weight_other = lax.ppermute(weight_mine, "ctx", CORE_SWAP)
    grad = ("R", (1, BLOCK, HEADS * HS), BF16)
    query_grad, key_grad, value_grad = call(unpack_kernel, [("V", result)], [grad, grad, grad])
    weight_grad = call(
        widen_kernel,
        [("S", core_ref), ("V", weight_mine), ("V", weight_other)],
        [("H", (HS, width), F32)],
    )
    return (attended, query_grad, key_grad, value_grad, weight_grad)


def solution(mesh):
    rows = P("fsdp", "ctx", None)
    return jax.shard_map(
        shards,
        mesh=mesh,
        in_specs=(rows, rows, rows, P("fsdp", None), P("fsdp"), P("fsdp", None), rows),
        out_specs=(rows, rows, rows, rows, P("fsdp", None)),
        check_vma=False,
    )
```

```python
import functools
import math

import jax
import jax.numpy as jnp
from jax import lax
from jax.experimental import pallas as pl
from jax.experimental.pallas import tpu as pltpu
from jax.sharding import PartitionSpec as P

HEADS = 8
HS = 128
BLOCK = 128
TILE = 256
SPAN = 512
REACH = 128
CHIPS = 8
LEN = 2048
NEG = -1e30
SEMS = 48
SCALE = 1.0 / math.sqrt(HS)
SCALE2 = SCALE * math.log2(math.e)
F32 = jnp.float32
BF16 = jnp.bfloat16

CORE_SWAP = [(i, i ^ 1) for i in range(16)]
PAIR_SWAP = [(i, i ^ 8) for i in range(16)]
SAME_CORE = [[2 * j + c for j in range(CHIPS)] for c in range(2)]
REDUCE = [
    [(8 * h + 2 * y + c) * 8 + f for f in range(8) for y in range(4)]
    for h in range(2)
    for c in range(2)
]


def dot_nt(a, b):
    return lax.dot_general(a, b, (((1,), (1,)), ((), ())), preferred_element_type=F32)


def dot_tn(a, b):
    return lax.dot_general(a, b, (((0,), (0,)), ((), ())), preferred_element_type=F32)


def dot_nn(a, b):
    return lax.dot_general(a, b, (((1,), (0,)), ((), ())), preferred_element_type=F32)


class Load:
    def __init__(self, copy, ref):
        self.copy, self.ref, self.done = copy, ref, False

    def get(self):
        if not self.done:
            self.copy.wait()
            self.done = True
        return self.ref


class Store:
    def __init__(self, hbm, ref, sems):
        self.hbm, self.ref, self.sems, self.copies = hbm, ref, sems, []

    def push(self, *index):
        src = self.ref.at[index] if index else self.ref
        dst = self.hbm.at[index] if index else self.hbm
        copy = pltpu.make_async_copy(src, dst, next(self.sems))
        copy.start()
        self.copies.append(copy)


SPACES = {"S": pltpu.SMEM, "V": pltpu.VMEM, "H": pltpu.HBM, "A": pl.ANY, "R": pltpu.HBM}


def call(kernel, ins, outs, scratch=(), flops=0, mib=14, aliases=None):
    copied = [
        pltpu.VMEM(jax.eval_shape(lambda x: x[i[2]] if len(i) > 2 else x, i[1]).shape, i[1].dtype)
        for i in ins
        if i[0] in "HA"
    ] + [pltpu.VMEM(o[1], o[2]) for o in outs if o[0] == "H"]

    def body(*refs):
        refs = list(refs)
        in_refs = [refs.pop(0) for _ in ins]
        out_refs = [refs.pop(0) for _ in outs]
        sem_ref = refs.pop(0)
        buffers = [refs.pop(0) for _ in copied]
        sems = (sem_ref.at[n] for n in range(SEMS))
        given, made = [], []
        for one, ref in zip(ins, in_refs):
            if one[0] in "HA":
                buffer = buffers.pop(0)
                copy = pltpu.make_async_copy(
                    ref.at[one[2]] if len(one) > 2 else ref, buffer, next(sems)
                )
                copy.start()
                ref = Load(copy, buffer)
            given.append(ref)
        for one, ref in zip(outs, out_refs):
            made.append(Store(ref, buffers.pop(0), sems) if one[0] == "H" else ref)
        more = kernel(given, made, refs, sems) or []
        for one in given:
            if isinstance(one, Load):
                one.get()
        for one in made:
            if isinstance(one, Store):
                for copy in one.copies:
                    copy.wait()
        for copy in more:
            copy.wait()

    result = pl.pallas_call(
        body,
        out_shape=[
            SPACES[o[0]](o[1], o[2]) if o[0] in "HR" else jax.ShapeDtypeStruct(o[1], o[2])
            for o in outs
        ],
        in_specs=[pl.BlockSpec(memory_space=SPACES[i[0]]) for i in ins],
        out_specs=[pl.BlockSpec(memory_space=SPACES[o[0]]) for o in outs],
        scratch_shapes=[pltpu.SemaphoreType.DMA((SEMS,)), *copied, *scratch],
        input_output_aliases=aliases or {},
        compiler_params=pltpu.CompilerParams(vmem_limit_bytes=mib * 1024 * 1024),
        cost_estimate=pl.CostEstimate(flops=flops, bytes_accessed=2_000_000, transcendentals=0),
    )(*[
        pltpu.with_memory_space_constraint(i[1], pltpu.HBM) if i[0] in "HR" else i[1] for i in ins
    ])
    return result[0] if len(outs) == 1 else result


def pack_kernel(ins, outs, scratch, sems):
    core_ref, *data = ins
    out_ref, half_ref, again_ref, up_mine_ref, up_send_ref = outs
    core = core_ref[0]
    half = half_ref.shape[1]
    copies = []

    def copy(src, dst):
        copies.append(pltpu.make_async_copy(src, dst, next(sems)))
        copies[-1].start()

    mine = pl.ds(pl.multiple_of(core * half, half), half)
    other = pl.ds(pl.multiple_of((1 - core) * half, half), half)
    copy(data[3].get().at[:, mine], half_ref)
    copy(data[3].get().at[:, mine], again_ref)
    for i in range(3):
        ref = data[i].get()
        for a in range(HEADS):
            copy(ref.at[:, pl.ds(a * HS, HS)], out_ref.at[a, i])
    up_ref = data[4].get()
    copy(up_ref.at[:, mine], up_mine_ref)
    copy(up_ref.at[:, other], up_send_ref)
    return copies


def quarter_kernel(ins, outs, scratch, sems):
    high_ref, mine_in, other_in = ins
    out = outs[0]
    quarter = out.shape[1]
    at = pl.ds(pl.multiple_of((1 - high_ref[0]) * quarter, quarter), quarter)
    copies = []
    for n, one in enumerate((mine_in, other_in)):
        copies.append(
            pltpu.make_async_copy(one.get().at[:, at], out.at[pl.ds(n * BLOCK, BLOCK)], next(sems))
        )
        copies[-1].start()
    return copies


def in_order(core, own_ref, other_ref, slot, dst_ref):
    for j in range(CHIPS):
        own = pl.multiple_of(2 * BLOCK * j + BLOCK * core, BLOCK)
        other = pl.multiple_of(2 * BLOCK * j + BLOCK * (1 - core), BLOCK)
        dst_ref[pl.ds(own, BLOCK)] = own_ref[j]
        dst_ref[pl.ds(other, BLOCK)] = other_ref[j, slot]


def chunks_of(m):
    stop = min(SPAN * (m + 1) + REACH, LEN)
    return [(start, min(start + SPAN, stop)) for start in range(0, stop, SPAN)]


def masked_scores(k_s, q, end, m, start, stop):
    scores = dot_nt(k_s[start:stop], q)
    if stop > SPAN * m:
        at = lax.broadcasted_iota(jnp.int32, scores.shape, 0) + start
        scores = jnp.where(at < end, scores, NEG)
    return scores


def forward_kernel(ins, outs, scratch, sems):
    core_ref, q_in, k_in, v_in, other_ref, end_ref, valid_ref = ins
    ctx_out, lse_out, q_out, k_out, v_out = outs
    (s_s,) = scratch
    core = core_ref[0]
    k_s, v_s = k_out.ref, v_out.ref
    in_order(core, k_in.get(), other_ref, 1, k_s)
    k_out.push()
    q_ref = q_in.get()
    q_out.ref[...] = q_ref[...]
    q_out.push()
    in_order(core, v_in.get(), other_ref, 2, v_s)
    v_out.push()
    for m in range(4):
        q = q_ref[2 * m : 2 * m + 2].reshape(TILE, HS)
        end = end_ref[m]
        top = jnp.full((1, TILE), NEG, F32)
        for start, stop in chunks_of(m):
            scores = masked_scores(k_s, q, end, m, start, stop)
            s_s[start:stop] = scores
            top = jnp.maximum(top, jnp.max(scores, axis=0, keepdims=True))
        top2 = top * SCALE2
        total = jnp.zeros((1, TILE), F32)
        acc = jnp.zeros((HS, TILE), F32)
        for start, stop in chunks_of(m):
            p = jnp.exp2(s_s[start:stop] * SCALE2 - top2)
            total = total + jnp.sum(p, axis=0, keepdims=True)
            acc = acc + dot_tn(v_s[start:stop], p.astype(BF16))
        lse_out.ref[m] = top2 + jnp.log2(total)
        ctx = (acc * (valid_ref[m] / total)).T.astype(BF16)
        for t in range(2):
            j = 2 * m + t
            block = ctx[t * BLOCK : (t + 1) * BLOCK]
            ctx_out.ref[j, 0] = block
            ctx_out.ref[j ^ 4, 1] = block
            ctx_out.push(j, 0)
            ctx_out.push(j ^ 4, 1)
    lse_out.push()


def backward_kernel(ins, outs, scratch, sems):
    core_ref, q_in, k_in, grad_in, v_in, ctx_in, end_in, lse_in = ins
    dq_out, keep_out, send_out = outs
    dk_s, dv_s = scratch
    core = core_ref[0]
    dk_s[...] = jnp.zeros(dk_s.shape, F32)
    dv_s[...] = jnp.zeros(dv_s.shape, F32)
    end_ref, lse_ref = end_in.get(), lse_in.get()
    q_ref, k_s = q_in.get(), k_in.get()
    grad_ref, v_s, ctx_ref = grad_in.get(), v_in.get(), ctx_in.get()
    for m in range(3, -1, -1):
        rows = slice(2 * m, 2 * m + 2)
        q = q_ref[rows].reshape(TILE, HS)
        do = grad_ref[rows].reshape(TILE, HS)
        ctx = ctx_ref[rows].reshape(TILE, HS)
        delta = jnp.sum((do.astype(F32) * ctx.astype(F32)).T, axis=0, keepdims=True)
        end = end_ref[m]
        lse = lse_ref[m]
        dq = jnp.zeros((HS, TILE), F32)
        for start, stop in chunks_of(m):
            scores = masked_scores(k_s, q, end, m, start, stop)
            p = jnp.exp2(scores * SCALE2 - lse)
            dp = dot_nt(v_s[start:stop], do)
            ds = (p * (dp - delta) * SCALE).astype(BF16)
            dv_s[start:stop] += dot_nn(p.astype(BF16), do)
            dk_s[start:stop] += dot_nn(ds, q)
            dq = dq + dot_tn(k_s[start:stop], ds)
        dq_rows = dq.T.astype(BF16)
        dq_out.ref[2 * m] = dq_rows[:BLOCK]
        dq_out.ref[2 * m + 1] = dq_rows[BLOCK:]
        dq_out.push(pl.ds(2 * m, 2))
        first = 2 * m + 1 if m else 0
        last = 2 * m + 3 if m < 3 else CHIPS
        for j in range(first, last):
            own = pl.multiple_of(2 * BLOCK * j + BLOCK * core, BLOCK)
            other = pl.multiple_of(2 * BLOCK * j + BLOCK * (1 - core), BLOCK)
            send_out.ref[j, 0] = dk_s[pl.ds(other, BLOCK)].astype(BF16)
            send_out.ref[j, 1] = dv_s[pl.ds(other, BLOCK)].astype(BF16)
            send_out.push(j)
            keep_out.ref[j, 0] = dk_s[pl.ds(own, BLOCK)]
            keep_out.ref[j, 1] = dv_s[pl.ds(own, BLOCK)]
            keep_out.push(j)


def project_kernel(ins, outs, scratch, sems):
    row_ref, up_in, up_other_in, *pieces = ins
    keep_ref, send_ref = outs
    row = row_ref[0]
    up = jnp.concatenate([up_in.get()[...], up_other_in.get()[...]], axis=0)
    for s in range(HEADS):
        total = dot_nt(up, pieces[s][...])
        at = jnp.bitwise_xor(row, s)
        keep_ref[at] = total[:BLOCK]
        send_ref[at] = total[BLOCK:].astype(BF16)


def add_kernel(ins, outs, scratch, sems):
    valid_ref, keep_ref, came_ref = ins
    outs[0][...] = ((keep_ref[...] + came_ref[...].astype(F32)) * valid_ref[...]).astype(BF16)


def attend_kernel(ins, outs, scratch, sems):
    row_ref, ctx_in, ctx_other_in, *pieces = ins
    keep, send = outs
    row = row_ref[0]
    order = [jnp.bitwise_xor(row, s) for s in range(HEADS)]
    ctx_ref, ctx_other_ref = ctx_in.get(), ctx_other_in.get()
    ctx = jnp.concatenate(
        [
            jnp.concatenate([ctx_ref[a] for a in order], axis=1),
            jnp.concatenate([ctx_other_ref[a] for a in order], axis=1),
        ],
        axis=0,
    )
    pieces = [piece.get() for piece in pieces]
    for n in range(4):
        cols = slice(n * TILE, (n + 1) * TILE)
        weight = jnp.concatenate([piece[:, cols] for piece in pieces], axis=0)
        total = dot_nn(ctx, weight).astype(BF16)
        keep.ref[:, cols] = total[:BLOCK]
        send.ref[:, cols] = total[BLOCK:]
    send.push()
    keep.push()


def place_kernel(ins, outs, scratch, sems):
    core_ref, keep_in, came_in = ins
    core = core_ref[0]
    half = keep_in.ref.shape[1]
    copies = []
    for one, c in ((keep_in, core), (came_in, 1 - core)):
        at = pl.ds(pl.multiple_of(c * half, half), half)
        copies.append(pltpu.make_async_copy(one.get(), outs[0].at[0, :, at], next(sems)))
        copies[-1].start()
    return copies


def weight_kernel(ins, outs, scratch, sems):
    out = outs[0]
    high_ref = ins[0]
    mine, other, pair, ctx_ref, ctx_other_ref = [one.get() for one in ins[1:]]
    quarter = pair.shape[1]
    at = pl.ds(pl.multiple_of(high_ref[0] * quarter, quarter), quarter)
    up = jnp.concatenate([mine[:, at], pair[:BLOCK]], axis=0)
    up_other = jnp.concatenate([other[:, at], pair[BLOCK:]], axis=0)
    for a in range(HEADS):
        total = dot_tn(ctx_ref[a].reshape(TILE, HS), up)
        total = total + dot_tn(ctx_other_ref[a].reshape(TILE, HS), up_other)
        part = pl.ds(4 * a, 4)
        out.ref[part] = total.reshape(4, HS // 4, quarter).astype(BF16)
        out.push(part)


def join_kernel(ins, outs, scratch, sems):
    dq_in, keep_in, came_in = ins
    (made,) = scratch
    copies = []
    dq_ref, keep_ref, came_ref = dq_in.get(), keep_in.get(), came_in.get()
    for j in range(CHIPS):
        made[j, 0] = dq_ref[j]
        made[j, 1] = (keep_ref[j, 0] + came_ref[j, 0].astype(F32)).astype(BF16)
        made[j, 2] = (keep_ref[j, 1] + came_ref[j, 1].astype(F32)).astype(BF16)
        copies.append(
            pltpu.make_async_copy(made.at[j], outs[0].at[j, pl.ds(0, 3)], next(sems))
        )
        copies[-1].start()
    return copies


def total_kernel(ins, outs, scratch, sems):
    terms_ref = ins[1]
    (made,) = scratch
    total = terms_ref[0].astype(F32)
    for s in range(1, terms_ref.shape[0]):
        total = total + terms_ref[s].astype(F32)
    weight = total.astype(BF16)
    rows = weight.shape[0]
    for t in range(4):
        made[t * rows : (t + 1) * rows] = weight[:, t * HS : (t + 1) * HS]
    copies = []
    for j in range(CHIPS):
        copies.append(pltpu.make_async_copy(made, outs[0].at[j, 3], next(sems)))
        copies[-1].start()
    return copies


def unpack_kernel(ins, outs, scratch, sems):
    mine_ref = ins[0]
    copies = []
    for a in range(HEADS):
        for i in range(3):
            dst = outs[i].at[0, :, pl.ds(a * HS, HS)]
            copies.append(pltpu.make_async_copy(mine_ref.at[a, i], dst, next(sems)))
            copies[-1].start()
    return copies


def widen_kernel(ins, outs, scratch, sems):
    core_ref, mine_ref, other_ref = ins
    out = outs[0]
    core = core_ref[0]
    for y in range(4):
        rows = pl.ds(32 * y, 32)
        for x in range(2):
            a = 4 * x + y
            for t in range(4):
                part = slice(32 * t, 32 * t + 32)
                at = pl.multiple_of(1024 * core + 512 * x + HS * t, HS)
                out.ref[rows, pl.ds(at, HS)] = mine_ref[a, part].astype(F32)
                at = pl.multiple_of(1024 * (1 - core) + 512 * x + HS * t, HS)
                out.ref[rows, pl.ds(at, HS)] = other_ref[a, part].astype(F32)
        out.push(rows)


def exchange(operand):
    return lax.all_to_all(
        operand, "ctx", split_axis=0, concat_axis=0, tiled=True, axis_index_groups=SAME_CORE
    )


def after(value, *others):
    return lax.optimization_barrier((value, *others))[0]


def shards(query_rows, key_rows, value_rows, session, lengths, out_weight, upstream):
    index = lax.axis_index("ctx").astype(jnp.int32)
    core = index & 1
    core_ref = core.reshape(1)
    high_ref = (index >> 3).reshape(1)
    row_ref = lax.axis_index("fsdp").astype(jnp.int32).reshape(1)
    valid_len = lengths[0]
    width = out_weight.shape[1]
    half = width // 2
    quarter = half // 2

    side = ("R", (BLOCK, half), BF16)
    packed, own_half, again_half, up_mine, up_send = call(
        pack_kernel,
        [
            ("S", core_ref), ("H", query_rows, 0), ("H", key_rows, 0),
            ("H", value_rows, 0), ("H", out_weight), ("H", upstream, 0),
        ],
        [("R", (HEADS, 3, BLOCK, HS), BF16), side, side, side, side],
    )
    own = exchange(packed)

    def step(value, s):
        return lax.ppermute(value, "fsdp", [(i, i ^ s) for i in range(8)])

    over = step(own_half, 4)

    session_ids = after(session[0], over)
    positions = jnp.arange(LEN, dtype=jnp.int32).reshape(CHIPS, 2, BLOCK)
    own_sessions = lax.dynamic_index_in_dim(session_ids.reshape(CHIPS, 2, BLOCK), core, 1, False)
    own_positions = lax.dynamic_index_in_dim(positions, core, 1, False)
    end = jnp.sum(
        (session_ids[:, None] <= own_sessions.reshape(1, -1)).astype(jnp.int32), axis=0
    )
    end = jnp.minimum(end, valid_len).reshape(4, 1, TILE)
    valid = (own_positions < valid_len).astype(F32).reshape(4, 1, TILE)
    rows_here = index * BLOCK + jnp.arange(BLOCK, dtype=jnp.int32)
    valid_here = (rows_here < valid_len).astype(F32)[:, None]

    again_half = after(again_half, over)
    one, three = step(again_half, 1), step(again_half, 3)
    over_one, over_three = step(over, 1), step(over, 3)
    two, over_two = step(one, 3), step(over_three, 1)
    pieces = [own_half, one, two, three, over, over_one, over_two, over_three]
    up_other = lax.ppermute(after(up_send, over), "ctx", CORE_SWAP)
    up_pair = call(
        quarter_kernel,
        [("S", high_ref), ("A", up_mine), ("A", up_other)],
        [("R", (2 * BLOCK, quarter), BF16)],
    )

    own = after(
        own, end, valid, valid_here, one, three, over_one, over_three, up_other, up_pair
    )
    up_pair = lax.ppermute(after(up_pair, own), "ctx", PAIR_SWAP)
    pieces[6] = after(pieces[6], up_pair)
    other = lax.ppermute(own, "ctx", CORE_SWAP)
    pairs = 4 * TILE * SPAN * 5 // 2
    rows = ("H", (LEN, HS), BF16)
    context, lse, query, key, value = call(
        forward_kernel,
        [
            ("S", core_ref), ("A", own, (slice(None), 0)), ("A", own, (slice(None), 1)),
            ("A", own, (slice(None), 2)), ("V", other), ("V", end), ("V", valid),
        ],
        [
            ("H", (CHIPS, 2, BLOCK, HS), BF16),
            ("H", (4, 1, TILE), F32),
            ("H", (CHIPS, BLOCK, HS), BF16),
            rows,
            rows,
        ],
        scratch=(pltpu.VMEM((LEN, TILE), F32),),
        flops=4 * pairs * HS,
    )
    context_mine = exchange(context)
    grads_keep, grads_send = call(
        project_kernel,
        [("S", row_ref), ("A", up_mine), ("A", up_other), *[("V", piece) for piece in pieces]],
        [("V", (HEADS, BLOCK, HS), F32), ("V", (HEADS, BLOCK, HS), BF16)],
        flops=2 * 256 * 1024 * 1024,
    )
    grads_came = lax.ppermute(grads_send, "ctx", CORE_SWAP)
    grads = call(
        add_kernel,
        [("V", valid_here), ("V", grads_keep), ("V", grads_came)],
        [("V", (HEADS, BLOCK, HS), BF16)],
    )
    context_mine = after(context_mine, grads)
    context_other = lax.ppermute(context_mine, "ctx", CORE_SWAP)
    terms = call(
        weight_kernel,
        [
            ("S", high_ref), ("A", up_mine), ("A", up_other), ("A", up_pair),
            ("A", context_mine), ("A", context_other),
        ],
        [("H", (32, 32, quarter), BF16)],
        flops=2 * 512 * 1024 * 512,
    )
    grads = exchange(after(grads, context_mine))
    terms = lax.all_to_all(
        after(terms, grads),
        ("ctx", "fsdp"),
        split_axis=0,
        concat_axis=0,
        tiled=True,
        axis_index_groups=REDUCE,
    )
    dq, keep, send = call(
        backward_kernel,
        [
            ("S", core_ref), ("H", query), ("H", key), ("H", grads), ("H", value),
            ("H", context, (slice(None), 0)), ("A", end), ("H", lse),
        ],
        [
            ("H", (CHIPS, BLOCK, HS), BF16),
            ("H", (CHIPS, 2, BLOCK, HS), F32),
            ("H", (CHIPS, 2, BLOCK, HS), BF16),
        ],
        scratch=(pltpu.VMEM((LEN, HS), F32), pltpu.VMEM((LEN, HS), F32)),
        flops=10 * pairs * HS,
    )
    came = lax.ppermute(send, "ctx", CORE_SWAP)
    joined = call(
        join_kernel,
        [("A", dq), ("A", keep), ("A", came)],
        [("R", (CHIPS, 4, BLOCK, HS), BF16)],
        scratch=(pltpu.VMEM((CHIPS, 3, BLOCK, HS), BF16),),
    )
    joined = call(
        total_kernel,
        [("R", joined), ("V", terms)],
        [("R", (CHIPS, 4, BLOCK, HS), BF16)],
        scratch=(pltpu.VMEM((BLOCK, HS), BF16),),
        aliases={0: 0},
    )
    side = ("H", (BLOCK, half), BF16)
    attended_keep, attended_send = call(
        attend_kernel,
        [
            ("S", row_ref), ("A", after(context_mine, joined), (slice(None), 0)),
            ("A", context_other, (slice(None), 0)), *[("A", piece) for piece in pieces],
        ],
        [side, side],
        flops=2 * 256 * 1024 * 1024,
    )
    attended_came = lax.ppermute(attended_send, "ctx", CORE_SWAP)
    attended = call(
        place_kernel,
        [("S", core_ref), ("A", attended_keep), ("A", attended_came)],
        [("R", (1, BLOCK, width), BF16)],
    )
    result = after(exchange(joined), attended)
    weight_mine = result[:, 3]
    weight_other = lax.ppermute(weight_mine, "ctx", CORE_SWAP)
    grad = ("R", (1, BLOCK, HEADS * HS), BF16)
    query_grad, key_grad, value_grad = call(unpack_kernel, [("V", result)], [grad, grad, grad])
    weight_grad = call(
        widen_kernel,
        [("S", core_ref), ("V", weight_mine), ("V", weight_other)],
        [("H", (HS, width), F32)],
    )
    return (attended, query_grad, key_grad, value_grad, weight_grad)


def solution(mesh):
    rows = P("fsdp", "ctx", None)
    return jax.shard_map(
        shards,
        mesh=mesh,
        in_specs=(rows, rows, rows, P("fsdp", None), P("fsdp"), P("fsdp", None), rows),
        out_specs=(rows, rows, rows, rows, P("fsdp", None)),
        check_vma=False,
    )
```

```python
import functools
import math

import jax
import jax.numpy as jnp
from jax import lax
from jax.experimental import pallas as pl
from jax.experimental.pallas import tpu as pltpu
from jax.sharding import PartitionSpec as P

HEADS = 8
HS = 128
BLOCK = 128
TILE = 256
SPAN = 512
REACH = 128
CHIPS = 8
LEN = 2048
NEG = -1e30
SEMS = 48
SCALE = 1.0 / math.sqrt(HS)
SCALE2 = SCALE * math.log2(math.e)
F32 = jnp.float32
BF16 = jnp.bfloat16

CORE_SWAP = [(i, i ^ 1) for i in range(16)]
PAIR_SWAP = [(i, i ^ 8) for i in range(16)]
SAME_CORE = [[2 * j + c for j in range(CHIPS)] for c in range(2)]
REDUCE = [
    [(8 * h + 2 * y + c) * 8 + f for f in range(8) for y in range(4)]
    for h in range(2)
    for c in range(2)
]


def dot_nt(a, b):
    return lax.dot_general(a, b, (((1,), (1,)), ((), ())), preferred_element_type=F32)


def dot_tn(a, b):
    return lax.dot_general(a, b, (((0,), (0,)), ((), ())), preferred_element_type=F32)


def dot_nn(a, b):
    return lax.dot_general(a, b, (((1,), (0,)), ((), ())), preferred_element_type=F32)


class Load:
    def __init__(self, copy, ref):
        self.copy, self.ref, self.done = copy, ref, False

    def get(self):
        if not self.done:
            self.copy.wait()
            self.done = True
        return self.ref


class Store:
    def __init__(self, hbm, ref, sems):
        self.hbm, self.ref, self.sems, self.copies = hbm, ref, sems, []

    def push(self, *index):
        src = self.ref.at[index] if index else self.ref
        dst = self.hbm.at[index] if index else self.hbm
        copy = pltpu.make_async_copy(src, dst, next(self.sems))
        copy.start()
        self.copies.append(copy)


SPACES = {"S": pltpu.SMEM, "V": pltpu.VMEM, "H": pltpu.HBM, "A": pl.ANY, "R": pltpu.HBM}


def call(kernel, ins, outs, scratch=(), flops=0, mib=14, aliases=None):
    copied = [
        pltpu.VMEM(jax.eval_shape(lambda x: x[i[2]] if len(i) > 2 else x, i[1]).shape, i[1].dtype)
        for i in ins
        if i[0] in "HA"
    ] + [pltpu.VMEM(o[1], o[2]) for o in outs if o[0] == "H"]

    def body(*refs):
        refs = list(refs)
        in_refs = [refs.pop(0) for _ in ins]
        out_refs = [refs.pop(0) for _ in outs]
        sem_ref = refs.pop(0)
        buffers = [refs.pop(0) for _ in copied]
        sems = (sem_ref.at[n] for n in range(SEMS))
        given, made = [], []
        for one, ref in zip(ins, in_refs):
            if one[0] in "HA":
                buffer = buffers.pop(0)
                copy = pltpu.make_async_copy(
                    ref.at[one[2]] if len(one) > 2 else ref, buffer, next(sems)
                )
                copy.start()
                ref = Load(copy, buffer)
            given.append(ref)
        for one, ref in zip(outs, out_refs):
            made.append(Store(ref, buffers.pop(0), sems) if one[0] == "H" else ref)
        more = kernel(given, made, refs, sems) or []
        for one in given:
            if isinstance(one, Load):
                one.get()
        for one in made:
            if isinstance(one, Store):
                for copy in one.copies:
                    copy.wait()
        for copy in more:
            copy.wait()

    result = pl.pallas_call(
        body,
        out_shape=[
            SPACES[o[0]](o[1], o[2]) if o[0] in "HR" else jax.ShapeDtypeStruct(o[1], o[2])
            for o in outs
        ],
        in_specs=[pl.BlockSpec(memory_space=SPACES[i[0]]) for i in ins],
        out_specs=[pl.BlockSpec(memory_space=SPACES[o[0]]) for o in outs],
        scratch_shapes=[pltpu.SemaphoreType.DMA((SEMS,)), *copied, *scratch],
        input_output_aliases=aliases or {},
        compiler_params=pltpu.CompilerParams(vmem_limit_bytes=mib * 1024 * 1024),
        cost_estimate=pl.CostEstimate(flops=flops, bytes_accessed=2_000_000, transcendentals=0),
    )(*[
        pltpu.with_memory_space_constraint(i[1], pltpu.HBM) if i[0] in "HR" else i[1] for i in ins
    ])
    return result[0] if len(outs) == 1 else result


def pack_kernel(ins, outs, scratch, sems):
    core_ref, *data = ins
    out_ref, half_ref, up_mine_ref, up_send_ref = outs
    core = core_ref[0]
    half = half_ref.shape[1]
    copies = []

    def copy(src, dst):
        copies.append(pltpu.make_async_copy(src, dst, next(sems)))
        copies[-1].start()

    mine = pl.ds(pl.multiple_of(core * half, half), half)
    other = pl.ds(pl.multiple_of((1 - core) * half, half), half)
    copy(data[3].get().at[:, mine], half_ref)
    for i in range(3):
        ref = data[i].get()
        for a in range(HEADS):
            copy(ref.at[:, pl.ds(a * HS, HS)], out_ref.at[a, i])
    up_ref = data[4].get()
    copy(up_ref.at[:, mine], up_mine_ref)
    copy(up_ref.at[:, other], up_send_ref)
    return copies


def quarter_kernel(ins, outs, scratch, sems):
    high_ref, mine_in, other_in = ins
    out = outs[0]
    quarter = out.shape[1]
    at = pl.ds(pl.multiple_of((1 - high_ref[0]) * quarter, quarter), quarter)
    copies = []
    for n, one in enumerate((mine_in, other_in)):
        copies.append(
            pltpu.make_async_copy(one.get().at[:, at], out.at[pl.ds(n * BLOCK, BLOCK)], next(sems))
        )
        copies[-1].start()
    return copies


def in_order(core, own_ref, other_ref, slot, dst_ref):
    for j in range(CHIPS):
        own = pl.multiple_of(2 * BLOCK * j + BLOCK * core, BLOCK)
        other = pl.multiple_of(2 * BLOCK * j + BLOCK * (1 - core), BLOCK)
        dst_ref[pl.ds(own, BLOCK)] = own_ref[j]
        dst_ref[pl.ds(other, BLOCK)] = other_ref[j, slot]


def chunks_of(m):
    stop = min(SPAN * (m + 1) + REACH, LEN)
    return [(start, min(start + SPAN, stop)) for start in range(0, stop, SPAN)]


def masked_scores(k_s, q, end, m, start, stop):
    scores = dot_nt(k_s[start:stop], q)
    if stop > SPAN * m:
        at = lax.broadcasted_iota(jnp.int32, scores.shape, 0) + start
        scores = jnp.where(at < end, scores, NEG)
    return scores


def forward_kernel(ins, outs, scratch, sems):
    core_ref, q_in, k_in, v_in, other_ref, end_ref, valid_ref = ins
    ctx_out, lse_out, q_out, k_out, v_out = outs
    (s_s,) = scratch
    core = core_ref[0]
    k_s, v_s = k_out.ref, v_out.ref
    in_order(core, k_in.get(), other_ref, 1, k_s)
    k_out.push()
    q_ref = q_in.get()
    q_out.ref[...] = q_ref[...]
    q_out.push()
    in_order(core, v_in.get(), other_ref, 2, v_s)
    v_out.push()
    for m in range(4):
        q = q_ref[2 * m : 2 * m + 2].reshape(TILE, HS)
        end = end_ref[m]
        top = jnp.full((1, TILE), NEG, F32)
        for start, stop in chunks_of(m):
            scores = masked_scores(k_s, q, end, m, start, stop)
            s_s[start:stop] = scores
            top = jnp.maximum(top, jnp.max(scores, axis=0, keepdims=True))
        top2 = top * SCALE2
        total = jnp.zeros((1, TILE), F32)
        acc = jnp.zeros((HS, TILE), F32)
        for start, stop in chunks_of(m):
            p = jnp.exp2(s_s[start:stop] * SCALE2 - top2)
            total = total + jnp.sum(p, axis=0, keepdims=True)
            acc = acc + dot_tn(v_s[start:stop], p.astype(BF16))
        lse_out.ref[m] = top2 + jnp.log2(total)
        ctx = (acc * (valid_ref[m] / total)).T.astype(BF16)
        for t in range(2):
            j = 2 * m + t
            block = ctx[t * BLOCK : (t + 1) * BLOCK]
            ctx_out.ref[j, 0] = block
            ctx_out.ref[j ^ 4, 1] = block
            ctx_out.push(j, 0)
            ctx_out.push(j ^ 4, 1)
    lse_out.push()


def backward_kernel(ins, outs, scratch, sems):
    core_ref, q_in, k_in, grad_in, v_in, ctx_in, end_in, lse_in = ins
    dq_out, keep_out, send_out = outs
    dk_s, dv_s = scratch
    core = core_ref[0]
    dk_s[...] = jnp.zeros(dk_s.shape, F32)
    dv_s[...] = jnp.zeros(dv_s.shape, F32)
    end_ref, lse_ref = end_in.get(), lse_in.get()
    q_ref, k_s = q_in.get(), k_in.get()
    grad_ref, v_s, ctx_ref = grad_in.get(), v_in.get(), ctx_in.get()
    for m in range(3, -1, -1):
        rows = slice(2 * m, 2 * m + 2)
        q = q_ref[rows].reshape(TILE, HS)
        do = grad_ref[rows].reshape(TILE, HS)
        ctx = ctx_ref[rows].reshape(TILE, HS)
        delta = jnp.sum((do.astype(F32) * ctx.astype(F32)).T, axis=0, keepdims=True)
        end = end_ref[m]
        lse = lse_ref[m]
        dq = jnp.zeros((HS, TILE), F32)
        for start, stop in chunks_of(m):
            scores = masked_scores(k_s, q, end, m, start, stop)
            p = jnp.exp2(scores * SCALE2 - lse)
            dp = dot_nt(v_s[start:stop], do)
            ds = (p * (dp - delta) * SCALE).astype(BF16)
            dv_s[start:stop] += dot_nn(p.astype(BF16), do)
            dk_s[start:stop] += dot_nn(ds, q)
            dq = dq + dot_tn(k_s[start:stop], ds)
        dq_rows = dq.T.astype(BF16)
        dq_out.ref[2 * m] = dq_rows[:BLOCK]
        dq_out.ref[2 * m + 1] = dq_rows[BLOCK:]
        dq_out.push(pl.ds(2 * m, 2))
        first = 2 * m + 1 if m else 0
        last = 2 * m + 3 if m < 3 else CHIPS
        for j in range(first, last):
            own = pl.multiple_of(2 * BLOCK * j + BLOCK * core, BLOCK)
            other = pl.multiple_of(2 * BLOCK * j + BLOCK * (1 - core), BLOCK)
            send_out.ref[j, 0] = dk_s[pl.ds(other, BLOCK)].astype(BF16)
            send_out.ref[j, 1] = dv_s[pl.ds(other, BLOCK)].astype(BF16)
            send_out.push(j)
            keep_out.ref[j, 0] = dk_s[pl.ds(own, BLOCK)]
            keep_out.ref[j, 1] = dv_s[pl.ds(own, BLOCK)]
            keep_out.push(j)


def project_kernel(ins, outs, scratch, sems):
    row_ref, up_in, up_other_in, *pieces = ins
    keep_ref, send_ref = outs
    row = row_ref[0]
    up = jnp.concatenate([up_in.get()[...], up_other_in.get()[...]], axis=0)
    for s in range(HEADS):
        total = dot_nt(up, pieces[s][...])
        at = jnp.bitwise_xor(row, s)
        keep_ref[at] = total[:BLOCK]
        send_ref[at] = total[BLOCK:].astype(BF16)


def add_kernel(ins, outs, scratch, sems):
    valid_ref, keep_ref, came_ref = ins
    outs[0][...] = ((keep_ref[...] + came_ref[...].astype(F32)) * valid_ref[...]).astype(BF16)


def attend_kernel(ins, outs, scratch, sems):
    row_ref, ctx_in, ctx_other_in, *pieces = ins
    keep, send = outs
    row = row_ref[0]
    order = [jnp.bitwise_xor(row, s) for s in range(HEADS)]
    ctx_ref, ctx_other_ref = ctx_in.get(), ctx_other_in.get()
    ctx = jnp.concatenate(
        [
            jnp.concatenate([ctx_ref[a] for a in order], axis=1),
            jnp.concatenate([ctx_other_ref[a] for a in order], axis=1),
        ],
        axis=0,
    )
    pieces = [piece.get() for piece in pieces]
    for n in range(4):
        cols = slice(n * TILE, (n + 1) * TILE)
        weight = jnp.concatenate([piece[:, cols] for piece in pieces], axis=0)
        total = dot_nn(ctx, weight).astype(BF16)
        keep.ref[:, cols] = total[:BLOCK]
        send.ref[:, cols] = total[BLOCK:]
    send.push()
    keep.push()


def place_kernel(ins, outs, scratch, sems):
    core_ref, keep_in, came_in = ins
    core = core_ref[0]
    half = keep_in.ref.shape[1]
    copies = []
    for one, c in ((keep_in, core), (came_in, 1 - core)):
        at = pl.ds(pl.multiple_of(c * half, half), half)
        copies.append(pltpu.make_async_copy(one.get(), outs[0].at[0, :, at], next(sems)))
        copies[-1].start()
    return copies


def weight_kernel(ins, outs, scratch, sems):
    out = outs[0]
    high_ref = ins[0]
    mine, other, pair, ctx_ref, ctx_other_ref = [one.get() for one in ins[1:]]
    quarter = pair.shape[1]
    at = pl.ds(pl.multiple_of(high_ref[0] * quarter, quarter), quarter)
    up = jnp.concatenate([mine[:, at], pair[:BLOCK]], axis=0)
    up_other = jnp.concatenate([other[:, at], pair[BLOCK:]], axis=0)
    for a in range(HEADS):
        total = dot_tn(ctx_ref[a].reshape(TILE, HS), up)
        total = total + dot_tn(ctx_other_ref[a].reshape(TILE, HS), up_other)
        part = pl.ds(4 * a, 4)
        out.ref[part] = total.reshape(4, HS // 4, quarter).astype(BF16)
        out.push(part)


def join_kernel(ins, outs, scratch, sems):
    dq_in, keep_in, came_in = ins
    (made,) = scratch
    copies = []
    dq_ref, keep_ref, came_ref = dq_in.get(), keep_in.get(), came_in.get()
    for j in range(CHIPS):
        made[j, 0] = dq_ref[j]
        made[j, 1] = (keep_ref[j, 0] + came_ref[j, 0].astype(F32)).astype(BF16)
        made[j, 2] = (keep_ref[j, 1] + came_ref[j, 1].astype(F32)).astype(BF16)
        copies.append(
            pltpu.make_async_copy(made.at[j], outs[0].at[j, pl.ds(0, 3)], next(sems))
        )
        copies[-1].start()
    return copies


def total_kernel(ins, outs, scratch, sems):
    terms_ref = ins[1]
    (made,) = scratch
    total = terms_ref[0].astype(F32)
    for s in range(1, terms_ref.shape[0]):
        total = total + terms_ref[s].astype(F32)
    weight = total.astype(BF16)
    rows = weight.shape[0]
    for t in range(4):
        made[t * rows : (t + 1) * rows] = weight[:, t * HS : (t + 1) * HS]
    copies = []
    for j in range(CHIPS):
        copies.append(pltpu.make_async_copy(made, outs[0].at[j, 3], next(sems)))
        copies[-1].start()
    return copies


def widen(ref, core, wide, out, sems):
    for y in range(4):
        for x in range(2):
            for t in range(4):
                wide[32 * y : 32 * y + 32, 512 * x + HS * t : 512 * x + HS * (t + 1)] = ref[
                    4 * x + y, 32 * t : 32 * t + 32
                ].astype(F32)
    half = wide.shape[1]
    at = pl.ds(pl.multiple_of(core * half, half), half)
    copy = pltpu.make_async_copy(wide, out.at[:, at], next(sems))
    copy.start()
    return copy


def unpack_kernel(ins, outs, scratch, sems):
    core_ref, mine_ref = ins
    copies = []
    for a in range(HEADS):
        for i in range(3):
            dst = outs[i].at[0, :, pl.ds(a * HS, HS)]
            copies.append(pltpu.make_async_copy(mine_ref.at[a, i], dst, next(sems)))
            copies[-1].start()
    copies.append(widen(mine_ref.at[:, 3], core_ref[0], scratch[0], outs[3], sems))
    return copies


def widen_kernel(ins, outs, scratch, sems):
    return [widen(ins[1], 1 - ins[0][0], scratch[0], outs[0], sems)]


def exchange(operand):
    return lax.all_to_all(
        operand, "ctx", split_axis=0, concat_axis=0, tiled=True, axis_index_groups=SAME_CORE
    )


def after(value, *others):
    return lax.optimization_barrier((value, *others))[0]


def shards(query_rows, key_rows, value_rows, session, lengths, out_weight, upstream):
    index = lax.axis_index("ctx").astype(jnp.int32)
    core = index & 1
    core_ref = core.reshape(1)
    high_ref = (index >> 3).reshape(1)
    row_ref = lax.axis_index("fsdp").astype(jnp.int32).reshape(1)
    valid_len = lengths[0]
    width = out_weight.shape[1]
    half = width // 2
    quarter = half // 2

    side = ("R", (BLOCK, half), BF16)
    packed, own_half, up_mine, up_send = call(
        pack_kernel,
        [
            ("S", core_ref), ("H", query_rows, 0), ("H", key_rows, 0),
            ("H", value_rows, 0), ("H", out_weight), ("H", upstream, 0),
        ],
        [("R", (HEADS, 3, BLOCK, HS), BF16), side, side, side],
    )
    own = exchange(packed)

    def step(value, s):
        return lax.ppermute(value, "fsdp", [(i, i ^ s) for i in range(8)])

    over = step(own_half, 4)

    session_ids = after(session[0], over)
    positions = jnp.arange(LEN, dtype=jnp.int32).reshape(CHIPS, 2, BLOCK)
    own_sessions = lax.dynamic_index_in_dim(session_ids.reshape(CHIPS, 2, BLOCK), core, 1, False)
    own_positions = lax.dynamic_index_in_dim(positions, core, 1, False)
    end = jnp.sum(
        (session_ids[:, None] <= own_sessions.reshape(1, -1)).astype(jnp.int32), axis=0
    )
    end = jnp.minimum(end, valid_len).reshape(4, 1, TILE)
    valid = (own_positions < valid_len).astype(F32).reshape(4, 1, TILE)
    rows_here = index * BLOCK + jnp.arange(BLOCK, dtype=jnp.int32)
    valid_here = (rows_here < valid_len).astype(F32)[:, None]

    one, three = step(own_half, 1), step(own_half, 3)
    over_one, over_three = step(over, 1), step(over, 3)
    two, over_two = step(one, 3), step(over_three, 1)
    pieces = [own_half, one, two, three, over, over_one, over_two, over_three]
    up_other = lax.ppermute(after(up_send, over), "ctx", CORE_SWAP)
    up_pair = call(
        quarter_kernel,
        [("S", high_ref), ("A", up_mine), ("A", up_other)],
        [("R", (2 * BLOCK, quarter), BF16)],
    )

    own = after(
        own, end, valid, valid_here, one, three, over_one, over_three, up_other, up_pair
    )
    up_pair = lax.ppermute(after(up_pair, own), "ctx", PAIR_SWAP)
    pieces[6] = after(pieces[6], up_pair)
    other = lax.ppermute(own, "ctx", CORE_SWAP)
    pairs = 4 * TILE * SPAN * 5 // 2
    rows = ("H", (LEN, HS), BF16)
    context, lse, query, key, value = call(
        forward_kernel,
        [
            ("S", core_ref), ("A", own, (slice(None), 0)), ("A", own, (slice(None), 1)),
            ("A", own, (slice(None), 2)), ("V", other), ("V", end), ("V", valid),
        ],
        [
            ("H", (CHIPS, 2, BLOCK, HS), BF16),
            ("H", (4, 1, TILE), F32),
            ("H", (CHIPS, BLOCK, HS), BF16),
            rows,
            rows,
        ],
        scratch=(pltpu.VMEM((LEN, TILE), F32),),
        flops=4 * pairs * HS,
    )
    context_mine = exchange(context)
    grads_keep, grads_send = call(
        project_kernel,
        [("S", row_ref), ("A", up_mine), ("A", up_other), *[("V", piece) for piece in pieces]],
        [("V", (HEADS, BLOCK, HS), F32), ("V", (HEADS, BLOCK, HS), BF16)],
        flops=2 * 256 * 1024 * 1024,
    )
    grads_came = lax.ppermute(grads_send, "ctx", CORE_SWAP)
    grads = call(
        add_kernel,
        [("V", valid_here), ("V", grads_keep), ("V", grads_came)],
        [("V", (HEADS, BLOCK, HS), BF16)],
    )
    context_mine = after(context_mine, grads)
    context_other = lax.ppermute(context_mine, "ctx", CORE_SWAP)
    terms = call(
        weight_kernel,
        [
            ("S", high_ref), ("A", up_mine), ("A", up_other), ("A", up_pair),
            ("A", context_mine), ("A", context_other),
        ],
        [("H", (32, 32, quarter), BF16)],
        flops=2 * 512 * 1024 * 512,
    )
    grads = exchange(after(grads, context_mine))
    terms = lax.all_to_all(
        after(terms, grads),
        ("ctx", "fsdp"),
        split_axis=0,
        concat_axis=0,
        tiled=True,
        axis_index_groups=REDUCE,
    )
    dq, keep, send = call(
        backward_kernel,
        [
            ("S", core_ref), ("H", query), ("H", key), ("H", grads), ("H", value),
            ("H", context, (slice(None), 0)), ("A", end), ("H", lse),
        ],
        [
            ("H", (CHIPS, BLOCK, HS), BF16),
            ("H", (CHIPS, 2, BLOCK, HS), F32),
            ("H", (CHIPS, 2, BLOCK, HS), BF16),
        ],
        scratch=(pltpu.VMEM((LEN, HS), F32), pltpu.VMEM((LEN, HS), F32)),
        flops=10 * pairs * HS,
    )
    came = lax.ppermute(send, "ctx", CORE_SWAP)
    joined = call(
        join_kernel,
        [("A", dq), ("A", keep), ("A", came)],
        [("R", (CHIPS, 4, BLOCK, HS), BF16)],
        scratch=(pltpu.VMEM((CHIPS, 3, BLOCK, HS), BF16),),
    )
    joined = call(
        total_kernel,
        [("R", joined), ("V", terms)],
        [("R", (CHIPS, 4, BLOCK, HS), BF16)],
        scratch=(pltpu.VMEM((BLOCK, HS), BF16),),
        aliases={0: 0},
    )
    side = ("H", (BLOCK, half), BF16)
    attended_keep, attended_send = call(
        attend_kernel,
        [
            ("S", row_ref), ("A", after(context_mine, joined), (slice(None), 0)),
            ("A", context_other, (slice(None), 0)), *[("A", piece) for piece in pieces],
        ],
        [side, side],
        flops=2 * 256 * 1024 * 1024,
    )
    attended_came = lax.ppermute(attended_send, "ctx", CORE_SWAP)
    attended = call(
        place_kernel,
        [("S", core_ref), ("A", attended_keep), ("A", attended_came)],
        [("R", (1, BLOCK, width), BF16)],
    )
    result = after(exchange(joined), attended)
    weight_other = lax.ppermute(result[:, 3], "ctx", CORE_SWAP)
    grad = ("R", (1, BLOCK, HEADS * HS), BF16)
    whole = ("R", (HS, width), F32)
    wide = (pltpu.VMEM((HS, half), F32),)
    query_grad, key_grad, value_grad, weight_grad = call(
        unpack_kernel, [("S", core_ref), ("V", result)], [grad, grad, grad, whole], scratch=wide
    )
    weight_grad = call(
        widen_kernel,
        [("S", core_ref), ("V", weight_other), ("R", weight_grad)],
        [whole],
        scratch=wide,
        aliases={2: 0},
    )
    return (attended, query_grad, key_grad, value_grad, weight_grad)


def solution(mesh):
    rows = P("fsdp", "ctx", None)
    return jax.shard_map(
        shards,
        mesh=mesh,
        in_specs=(rows, rows, rows, P("fsdp", None), P("fsdp"), P("fsdp", None), rows),
        out_specs=(rows, rows, rows, rows, P("fsdp", None)),
        check_vma=False,
    )
```

```python
import functools
import math

import jax
import jax.numpy as jnp
from jax import lax
from jax.experimental import pallas as pl
from jax.experimental.pallas import tpu as pltpu
from jax.sharding import PartitionSpec as P

HEADS = 8
HS = 128
BLOCK = 128
TILE = 256
SPAN = 512
REACH = 128
CHIPS = 8
LEN = 2048
NEG = -1e30
SEMS = 48
SCALE = 1.0 / math.sqrt(HS)
SCALE2 = SCALE * math.log2(math.e)
F32 = jnp.float32
BF16 = jnp.bfloat16

CORE_SWAP = [(i, i ^ 1) for i in range(16)]
PAIR_SWAP = [(i, i ^ 8) for i in range(16)]
SAME_CORE = [[2 * j + c for j in range(CHIPS)] for c in range(2)]
REDUCE = [
    [(8 * h + 2 * y + c) * 8 + f for f in range(8) for y in range(4)]
    for h in range(2)
    for c in range(2)
]


def dot_nt(a, b):
    return lax.dot_general(a, b, (((1,), (1,)), ((), ())), preferred_element_type=F32)


def dot_tn(a, b):
    return lax.dot_general(a, b, (((0,), (0,)), ((), ())), preferred_element_type=F32)


def dot_nn(a, b):
    return lax.dot_general(a, b, (((1,), (0,)), ((), ())), preferred_element_type=F32)


class Load:
    def __init__(self, copy, ref):
        self.copy, self.ref, self.done = copy, ref, False

    def get(self):
        if not self.done:
            self.copy.wait()
            self.done = True
        return self.ref


class Store:
    def __init__(self, hbm, ref, sems):
        self.hbm, self.ref, self.sems, self.copies = hbm, ref, sems, []

    def push(self, *index):
        src = self.ref.at[index] if index else self.ref
        dst = self.hbm.at[index] if index else self.hbm
        copy = pltpu.make_async_copy(src, dst, next(self.sems))
        copy.start()
        self.copies.append(copy)


SPACES = {"S": pltpu.SMEM, "V": pltpu.VMEM, "H": pltpu.HBM, "A": pl.ANY, "R": pltpu.HBM}


def call(kernel, ins, outs, scratch=(), flops=0, mib=14, aliases=None):
    copied = [
        pltpu.VMEM(jax.eval_shape(lambda x: x[i[2]] if len(i) > 2 else x, i[1]).shape, i[1].dtype)
        for i in ins
        if i[0] in "HA"
    ] + [pltpu.VMEM(o[1], o[2]) for o in outs if o[0] == "H"]

    def body(*refs):
        refs = list(refs)
        in_refs = [refs.pop(0) for _ in ins]
        out_refs = [refs.pop(0) for _ in outs]
        sem_ref = refs.pop(0)
        buffers = [refs.pop(0) for _ in copied]
        sems = (sem_ref.at[n] for n in range(SEMS))
        given, made = [], []
        for one, ref in zip(ins, in_refs):
            if one[0] in "HA":
                buffer = buffers.pop(0)
                copy = pltpu.make_async_copy(
                    ref.at[one[2]] if len(one) > 2 else ref, buffer, next(sems)
                )
                copy.start()
                ref = Load(copy, buffer)
            given.append(ref)
        for one, ref in zip(outs, out_refs):
            made.append(Store(ref, buffers.pop(0), sems) if one[0] == "H" else ref)
        more = kernel(given, made, refs, sems) or []
        for one in given:
            if isinstance(one, Load):
                one.get()
        for one in made:
            if isinstance(one, Store):
                for copy in one.copies:
                    copy.wait()
        for copy in more:
            copy.wait()

    result = pl.pallas_call(
        body,
        out_shape=[
            SPACES[o[0]](o[1], o[2]) if o[0] in "HR" else jax.ShapeDtypeStruct(o[1], o[2])
            for o in outs
        ],
        in_specs=[pl.BlockSpec(memory_space=SPACES[i[0]]) for i in ins],
        out_specs=[pl.BlockSpec(memory_space=SPACES[o[0]]) for o in outs],
        scratch_shapes=[pltpu.SemaphoreType.DMA((SEMS,)), *copied, *scratch],
        input_output_aliases=aliases or {},
        compiler_params=pltpu.CompilerParams(vmem_limit_bytes=mib * 1024 * 1024),
        cost_estimate=pl.CostEstimate(flops=flops, bytes_accessed=2_000_000, transcendentals=0),
    )(*[
        pltpu.with_memory_space_constraint(i[1], pltpu.HBM) if i[0] in "HR" else i[1] for i in ins
    ])
    return result[0] if len(outs) == 1 else result


def pack_kernel(ins, outs, scratch, sems):
    core_ref, *data = ins
    out_ref, half_ref, up_mine_ref, up_send_ref = outs
    core = core_ref[0]
    half = half_ref.shape[1]
    copies = []

    def copy(src, dst):
        copies.append(pltpu.make_async_copy(src, dst, next(sems)))
        copies[-1].start()

    mine = pl.ds(pl.multiple_of(core * half, half), half)
    other = pl.ds(pl.multiple_of((1 - core) * half, half), half)
    load = pltpu.make_async_copy(data[3].at[:, mine], scratch[0], next(sems))
    load.start()
    for i in range(3):
        ref = data[i].get()
        for a in range(HEADS):
            copy(ref.at[:, pl.ds(a * HS, HS)], out_ref.at[a, i])
    load.wait()
    copy(scratch[0], half_ref)
    up_ref = data[4].get()
    copy(up_ref.at[:, mine], up_mine_ref)
    copy(up_ref.at[:, other], up_send_ref)
    return copies


def quarter_kernel(ins, outs, scratch, sems):
    high_ref, mine_in, other_in = ins
    out = outs[0]
    quarter = out.shape[1]
    at = pl.ds(pl.multiple_of((1 - high_ref[0]) * quarter, quarter), quarter)
    copies = []
    for n, one in enumerate((mine_in, other_in)):
        copies.append(
            pltpu.make_async_copy(one.get().at[:, at], out.at[pl.ds(n * BLOCK, BLOCK)], next(sems))
        )
        copies[-1].start()
    return copies


def in_order(core, own_ref, other_ref, slot, dst_ref):
    for j in range(CHIPS):
        own = pl.multiple_of(2 * BLOCK * j + BLOCK * core, BLOCK)
        other = pl.multiple_of(2 * BLOCK * j + BLOCK * (1 - core), BLOCK)
        dst_ref[pl.ds(own, BLOCK)] = own_ref[j]
        dst_ref[pl.ds(other, BLOCK)] = other_ref[j, slot]


def chunks_of(m):
    stop = min(SPAN * (m + 1) + REACH, LEN)
    return [(start, min(start + SPAN, stop)) for start in range(0, stop, SPAN)]


def masked_scores(k_s, q, end, m, start, stop):
    scores = dot_nt(k_s[start:stop], q)
    if stop > SPAN * m:
        at = lax.broadcasted_iota(jnp.int32, scores.shape, 0) + start
        scores = jnp.where(at < end, scores, NEG)
    return scores


def forward_kernel(ins, outs, scratch, sems):
    core_ref, q_in, k_in, v_in, other_ref, end_ref, valid_ref = ins
    ctx_out, lse_out, q_out, k_out, v_out = outs
    (s_s,) = scratch
    core = core_ref[0]
    k_s, v_s = k_out.ref, v_out.ref
    in_order(core, k_in.get(), other_ref, 1, k_s)
    k_out.push()
    q_ref = q_in.get()
    q_out.ref[...] = q_ref[...]
    q_out.push()
    in_order(core, v_in.get(), other_ref, 2, v_s)
    v_out.push()
    for m in range(4):
        q = q_ref[2 * m : 2 * m + 2].reshape(TILE, HS)
        end = end_ref[m]
        top = jnp.full((1, TILE), NEG, F32)
        for start, stop in chunks_of(m):
            scores = masked_scores(k_s, q, end, m, start, stop)
            s_s[start:stop] = scores
            top = jnp.maximum(top, jnp.max(scores, axis=0, keepdims=True))
        top2 = top * SCALE2
        total = jnp.zeros((1, TILE), F32)
        acc = jnp.zeros((HS, TILE), F32)
        for start, stop in chunks_of(m):
            p = jnp.exp2(s_s[start:stop] * SCALE2 - top2)
            total = total + jnp.sum(p, axis=0, keepdims=True)
            acc = acc + dot_tn(v_s[start:stop], p.astype(BF16))
        lse_out.ref[m] = top2 + jnp.log2(total)
        ctx = (acc * (valid_ref[m] / total)).T.astype(BF16)
        for t in range(2):
            j = 2 * m + t
            block = ctx[t * BLOCK : (t + 1) * BLOCK]
            ctx_out.ref[j, 0] = block
            ctx_out.ref[j ^ 4, 1] = block
            ctx_out.push(j, 0)
            ctx_out.push(j ^ 4, 1)
    lse_out.push()


def backward_kernel(ins, outs, scratch, sems):
    core_ref, q_in, k_in, grad_in, v_in, ctx_in, end_in, lse_in = ins
    dq_out, keep_out, send_out = outs
    dk_s, dv_s = scratch
    core = core_ref[0]
    dk_s[...] = jnp.zeros(dk_s.shape, F32)
    dv_s[...] = jnp.zeros(dv_s.shape, F32)
    end_ref, lse_ref = end_in.get(), lse_in.get()
    q_ref, k_s = q_in.get(), k_in.get()
    grad_ref, v_s, ctx_ref = grad_in.get(), v_in.get(), ctx_in.get()
    for m in range(3, -1, -1):
        rows = slice(2 * m, 2 * m + 2)
        q = q_ref[rows].reshape(TILE, HS)
        do = grad_ref[rows].reshape(TILE, HS)
        ctx = ctx_ref[rows].reshape(TILE, HS)
        delta = jnp.sum((do.astype(F32) * ctx.astype(F32)).T, axis=0, keepdims=True)
        end = end_ref[m]
        lse = lse_ref[m]
        dq = jnp.zeros((HS, TILE), F32)
        for start, stop in chunks_of(m):
            scores = masked_scores(k_s, q, end, m, start, stop)
            p = jnp.exp2(scores * SCALE2 - lse)
            dp = dot_nt(v_s[start:stop], do)
            ds = (p * (dp - delta) * SCALE).astype(BF16)
            dv_s[start:stop] += dot_nn(p.astype(BF16), do)
            dk_s[start:stop] += dot_nn(ds, q)
            dq = dq + dot_tn(k_s[start:stop], ds)
        dq_rows = dq.T.astype(BF16)
        dq_out.ref[2 * m] = dq_rows[:BLOCK]
        dq_out.ref[2 * m + 1] = dq_rows[BLOCK:]
        dq_out.push(pl.ds(2 * m, 2))
        first = 2 * m + 1 if m else 0
        last = 2 * m + 3 if m < 3 else CHIPS
        for j in range(first, last):
            own = pl.multiple_of(2 * BLOCK * j + BLOCK * core, BLOCK)
            other = pl.multiple_of(2 * BLOCK * j + BLOCK * (1 - core), BLOCK)
            send_out.ref[j, 0] = dk_s[pl.ds(other, BLOCK)].astype(BF16)
            send_out.ref[j, 1] = dv_s[pl.ds(other, BLOCK)].astype(BF16)
            send_out.push(j)
            keep_out.ref[j, 0] = dk_s[pl.ds(own, BLOCK)]
            keep_out.ref[j, 1] = dv_s[pl.ds(own, BLOCK)]
            keep_out.push(j)


def project_kernel(ins, outs, scratch, sems):
    row_ref, up_in, up_other_in, *pieces = ins
    keep_ref, send_ref = outs
    row = row_ref[0]
    up = jnp.concatenate([up_in.get()[...], up_other_in.get()[...]], axis=0)
    for s in range(HEADS):
        total = dot_nt(up, pieces[s][...])
        at = jnp.bitwise_xor(row, s)
        keep_ref[at] = total[:BLOCK]
        send_ref[at] = total[BLOCK:].astype(BF16)


def add_kernel(ins, outs, scratch, sems):
    valid_ref, keep_ref, came_ref = ins
    outs[0][...] = ((keep_ref[...] + came_ref[...].astype(F32)) * valid_ref[...]).astype(BF16)


def attend_kernel(ins, outs, scratch, sems):
    row_ref, ctx_in, ctx_other_in, *pieces = ins
    keep, send = outs
    row = row_ref[0]
    order = [jnp.bitwise_xor(row, s) for s in range(HEADS)]
    ctx_ref, ctx_other_ref = ctx_in.get(), ctx_other_in.get()
    ctx = jnp.concatenate(
        [
            jnp.concatenate([ctx_ref[a] for a in order], axis=1),
            jnp.concatenate([ctx_other_ref[a] for a in order], axis=1),
        ],
        axis=0,
    )
    pieces = [piece.get() for piece in pieces]
    for n in range(4):
        cols = slice(n * TILE, (n + 1) * TILE)
        weight = jnp.concatenate([piece[:, cols] for piece in pieces], axis=0)
        total = dot_nn(ctx, weight).astype(BF16)
        keep.ref[:, cols] = total[:BLOCK]
        send.ref[:, cols] = total[BLOCK:]
    send.push()
    keep.push()


def place_kernel(ins, outs, scratch, sems):
    core_ref, keep_in, came_in = ins
    core = core_ref[0]
    half = keep_in.ref.shape[1]
    copies = []
    for one, c in ((keep_in, core), (came_in, 1 - core)):
        at = pl.ds(pl.multiple_of(c * half, half), half)
        copies.append(pltpu.make_async_copy(one.get(), outs[0].at[0, :, at], next(sems)))
        copies[-1].start()
    return copies


def weight_kernel(ins, outs, scratch, sems):
    out = outs[0]
    high_ref = ins[0]
    mine, other, pair, ctx_ref, ctx_other_ref = [one.get() for one in ins[1:]]
    quarter = pair.shape[1]
    at = pl.ds(pl.multiple_of(high_ref[0] * quarter, quarter), quarter)
    up = jnp.concatenate([mine[:, at], pair[:BLOCK]], axis=0)
    up_other = jnp.concatenate([other[:, at], pair[BLOCK:]], axis=0)
    for a in range(HEADS):
        total = dot_tn(ctx_ref[a].reshape(TILE, HS), up)
        total = total + dot_tn(ctx_other_ref[a].reshape(TILE, HS), up_other)
        part = pl.ds(4 * a, 4)
        out.ref[part] = total.reshape(4, HS // 4, quarter).astype(BF16)
        out.push(part)


def join_kernel(ins, outs, scratch, sems):
    dq_in, keep_in, came_in = ins
    (made,) = scratch
    copies = []
    dq_ref, keep_ref, came_ref = dq_in.get(), keep_in.get(), came_in.get()
    for j in range(CHIPS):
        made[j, 0] = dq_ref[j]
        made[j, 1] = (keep_ref[j, 0] + came_ref[j, 0].astype(F32)).astype(BF16)
        made[j, 2] = (keep_ref[j, 1] + came_ref[j, 1].astype(F32)).astype(BF16)
        copies.append(
            pltpu.make_async_copy(made.at[j], outs[0].at[j, pl.ds(0, 3)], next(sems))
        )
        copies[-1].start()
    return copies


def total_kernel(ins, outs, scratch, sems):
    terms_ref = ins[1]
    (made,) = scratch
    total = terms_ref[0].astype(F32)
    for s in range(1, terms_ref.shape[0]):
        total = total + terms_ref[s].astype(F32)
    weight = total.astype(BF16)
    rows = weight.shape[0]
    for t in range(4):
        made[t * rows : (t + 1) * rows] = weight[:, t * HS : (t + 1) * HS]
    copies = []
    for j in range(CHIPS):
        copies.append(pltpu.make_async_copy(made, outs[0].at[j, 3], next(sems)))
        copies[-1].start()
    return copies


def unpack_kernel(ins, outs, scratch, sems):
    mine_ref = ins[0]
    copies = []
    for a in range(HEADS):
        for i in range(3):
            dst = outs[i].at[0, :, pl.ds(a * HS, HS)]
            copies.append(pltpu.make_async_copy(mine_ref.at[a, i], dst, next(sems)))
            copies[-1].start()
    return copies


def widen_kernel(ins, outs, scratch, sems):
    core_ref, mine_ref, other_ref = ins
    out = outs[0]
    core = core_ref[0]
    for y in range(4):
        rows = pl.ds(32 * y, 32)
        for x in range(2):
            a = 4 * x + y
            for t in range(4):
                part = slice(32 * t, 32 * t + 32)
                at = pl.multiple_of(1024 * core + 512 * x + HS * t, HS)
                out.ref[rows, pl.ds(at, HS)] = mine_ref[a, part].astype(F32)
                at = pl.multiple_of(1024 * (1 - core) + 512 * x + HS * t, HS)
                out.ref[rows, pl.ds(at, HS)] = other_ref[a, part].astype(F32)
        out.push(rows)


def exchange(operand):
    return lax.all_to_all(
        operand, "ctx", split_axis=0, concat_axis=0, tiled=True, axis_index_groups=SAME_CORE
    )


def after(value, *others):
    return lax.optimization_barrier((value, *others))[0]


def shards(query_rows, key_rows, value_rows, session, lengths, out_weight, upstream):
    index = lax.axis_index("ctx").astype(jnp.int32)
    core = index & 1
    core_ref = core.reshape(1)
    high_ref = (index >> 3).reshape(1)
    row_ref = lax.axis_index("fsdp").astype(jnp.int32).reshape(1)
    valid_len = lengths[0]
    width = out_weight.shape[1]
    half = width // 2
    quarter = half // 2

    side = ("R", (BLOCK, half), BF16)
    packed, own_half, up_mine, up_send = call(
        pack_kernel,
        [
            ("S", core_ref), ("H", query_rows, 0), ("H", key_rows, 0),
            ("H", value_rows, 0), ("R", out_weight), ("H", upstream, 0),
        ],
        [("R", (HEADS, 3, BLOCK, HS), BF16), side, side, side],
        scratch=(pltpu.VMEM((HS, half), BF16),),
    )
    own = exchange(packed)

    def step(value, s):
        return lax.ppermute(value, "fsdp", [(i, i ^ s) for i in range(8)])

    over = step(own_half, 4)

    session_ids = after(session[0], over)
    positions = jnp.arange(LEN, dtype=jnp.int32).reshape(CHIPS, 2, BLOCK)
    own_sessions = lax.dynamic_index_in_dim(session_ids.reshape(CHIPS, 2, BLOCK), core, 1, False)
    own_positions = lax.dynamic_index_in_dim(positions, core, 1, False)
    end = jnp.sum(
        (session_ids[:, None] <= own_sessions.reshape(1, -1)).astype(jnp.int32), axis=0
    )
    end = jnp.minimum(end, valid_len).reshape(4, 1, TILE)
    valid = (own_positions < valid_len).astype(F32).reshape(4, 1, TILE)
    rows_here = index * BLOCK + jnp.arange(BLOCK, dtype=jnp.int32)
    valid_here = (rows_here < valid_len).astype(F32)[:, None]

    one, three = step(own_half, 1), step(own_half, 3)
    over_one, over_three = step(over, 1), step(over, 3)
    two, over_two = step(one, 3), step(over_three, 1)
    pieces = [own_half, one, two, three, over, over_one, over_two, over_three]
    up_other = lax.ppermute(after(up_send, over), "ctx", CORE_SWAP)
    up_pair = call(
        quarter_kernel,
        [("S", high_ref), ("A", up_mine), ("A", up_other)],
        [("R", (2 * BLOCK, quarter), BF16)],
    )

    own = after(
        own, end, valid, valid_here, one, three, over_one, over_three, up_other, up_pair
    )
    up_pair = lax.ppermute(after(up_pair, own), "ctx", PAIR_SWAP)
    pieces[6] = after(pieces[6], up_pair)
    other = lax.ppermute(own, "ctx", CORE_SWAP)
    pairs = 4 * TILE * SPAN * 5 // 2
    rows = ("H", (LEN, HS), BF16)
    context, lse, query, key, value = call(
        forward_kernel,
        [
            ("S", core_ref), ("A", own, (slice(None), 0)), ("A", own, (slice(None), 1)),
            ("A", own, (slice(None), 2)), ("V", other), ("V", end), ("V", valid),
        ],
        [
            ("H", (CHIPS, 2, BLOCK, HS), BF16),
            ("H", (4, 1, TILE), F32),
            ("H", (CHIPS, BLOCK, HS), BF16),
            rows,
            rows,
        ],
        scratch=(pltpu.VMEM((LEN, TILE), F32),),
        flops=4 * pairs * HS,
    )
    context_mine = exchange(context)
    grads_keep, grads_send = call(
        project_kernel,
        [("S", row_ref), ("A", up_mine), ("A", up_other), *[("V", piece) for piece in pieces]],
        [("V", (HEADS, BLOCK, HS), F32), ("V", (HEADS, BLOCK, HS), BF16)],
        flops=2 * 256 * 1024 * 1024,
    )
    grads_came = lax.ppermute(grads_send, "ctx", CORE_SWAP)
    grads = call(
        add_kernel,
        [("V", valid_here), ("V", grads_keep), ("V", grads_came)],
        [("V", (HEADS, BLOCK, HS), BF16)],
    )
    context_mine = after(context_mine, grads)
    context_other = lax.ppermute(context_mine, "ctx", CORE_SWAP)
    terms = call(
        weight_kernel,
        [
            ("S", high_ref), ("A", up_mine), ("A", up_other), ("A", up_pair),
            ("A", context_mine), ("A", context_other),
        ],
        [("H", (32, 32, quarter), BF16)],
        flops=2 * 512 * 1024 * 512,
    )
    grads = exchange(after(grads, context_mine))
    terms = lax.all_to_all(
        after(terms, grads),
        ("ctx", "fsdp"),
        split_axis=0,
        concat_axis=0,
        tiled=True,
        axis_index_groups=REDUCE,
    )
    dq, keep, send = call(
        backward_kernel,
        [
            ("S", core_ref), ("H", query), ("H", key), ("H", grads), ("H", value),
            ("H", context, (slice(None), 0)), ("A", end), ("H", lse),
        ],
        [
            ("H", (CHIPS, BLOCK, HS), BF16),
            ("H", (CHIPS, 2, BLOCK, HS), F32),
            ("H", (CHIPS, 2, BLOCK, HS), BF16),
        ],
        scratch=(pltpu.VMEM((LEN, HS), F32), pltpu.VMEM((LEN, HS), F32)),
        flops=10 * pairs * HS,
    )
    came = lax.ppermute(send, "ctx", CORE_SWAP)
    joined = call(
        join_kernel,
        [("A", dq), ("A", keep), ("A", came)],
        [("R", (CHIPS, 4, BLOCK, HS), BF16)],
        scratch=(pltpu.VMEM((CHIPS, 3, BLOCK, HS), BF16),),
    )
    joined = call(
        total_kernel,
        [("R", joined), ("V", terms)],
        [("R", (CHIPS, 4, BLOCK, HS), BF16)],
        scratch=(pltpu.VMEM((BLOCK, HS), BF16),),
        aliases={0: 0},
    )
    side = ("H", (BLOCK, half), BF16)
    attended_keep, attended_send = call(
        attend_kernel,
        [
            ("S", row_ref), ("A", after(context_mine, joined), (slice(None), 0)),
            ("A", context_other, (slice(None), 0)), *[("A", piece) for piece in pieces],
        ],
        [side, side],
        flops=2 * 256 * 1024 * 1024,
    )
    attended_came = lax.ppermute(attended_send, "ctx", CORE_SWAP)
    attended = call(
        place_kernel,
        [("S", core_ref), ("A", attended_keep), ("A", attended_came)],
        [("R", (1, BLOCK, width), BF16)],
    )
    result = after(exchange(joined), attended)
    weight_mine = result[:, 3]
    weight_other = lax.ppermute(weight_mine, "ctx", CORE_SWAP)
    grad = ("R", (1, BLOCK, HEADS * HS), BF16)
    query_grad, key_grad, value_grad = call(unpack_kernel, [("V", result)], [grad, grad, grad])
    weight_grad = call(
        widen_kernel,
        [("S", core_ref), ("V", weight_mine), ("V", weight_other)],
        [("H", (HS, width), F32)],
    )
    return (attended, query_grad, key_grad, value_grad, weight_grad)


def solution(mesh):
    rows = P("fsdp", "ctx", None)
    return jax.shard_map(
        shards,
        mesh=mesh,
        in_specs=(rows, rows, rows, P("fsdp", None), P("fsdp"), P("fsdp", None), rows),
        out_specs=(rows, rows, rows, rows, P("fsdp", None)),
        check_vma=False,
    )
```
